32 devices in a mesh: fsdp: 2 (over core), ctx: 4 (over y, x), tp: 4 (over z).
Axes of the slice: x: 2, y: 2, z: 4, core: 2. Of those that a mesh axis runs over, the one named last changes fastest.
Arguments:
- tokens: bfloat16 [4, 1536, 2048], P(None, ('fsdp', 'ctx')), may hold values from -6 to 6
- cotangent: bfloat16 [4, 1536, 2048], P(None, ('fsdp', 'ctx')), may hold values from -6 to 6
- lengths: int32 [4, 2, 8], replicated, may hold values from 1 to 761, as said below
- order: int32 [4, 1536], replicated, may hold values from 0 to 1535, as said below
- gain_in: bfloat16 [2048], P(('fsdp', 'ctx')), may hold values from 0.5 to 1.5
- query_proj: bfloat16 [2048, 2048], P(('fsdp', 'ctx'), 'tp'), may hold values from -0.125 to 0.125
- key_proj: bfloat16 [2048, 2048], P(('fsdp', 'ctx'), 'tp'), may hold values from -0.125 to 0.125
- value_proj: bfloat16 [2048, 4096], P(('fsdp', 'ctx'), 'tp'), may hold values from -0.125 to 0.125
- gate_proj: bfloat16 [2048, 4096], P(('fsdp', 'ctx'), 'tp'), may hold values from -0.125 to 0.125
- alpha_proj: bfloat16 [2048, 16], P(('fsdp', 'ctx'), 'tp'), may hold values from -0.25 to 0.25
- beta_proj: bfloat16 [2048, 16], P(('fsdp', 'ctx'), 'tp'), may hold values from -0.125 to 0.125
- query_conv: bfloat16 [4, 16, 128], P(None, 'tp', ('fsdp', 'ctx')), may hold values from -3 to 3
- key_conv: bfloat16 [4, 16, 128], P(None, 'tp', ('fsdp', 'ctx')), may hold values from -3 to 3
- value_conv: bfloat16 [4, 16, 256], P(None, 'tp', ('fsdp', 'ctx')), may hold values from -3 to 3
- decay_log: float32 [16], P('tp'), may hold values from -0.9 to 2.5
- step_bias: float32 [16], P('tp'), may hold values from -7 to -5
- gain_head: bfloat16 [256], P(('fsdp', 'ctx')), may hold values from 0.5 to 1.5
- out_proj: bfloat16 [4096, 2048], P('tp', ('fsdp', 'ctx')), may hold values from -0.125 to 0.125
- gain_mid: bfloat16 [2048], P(('fsdp', 'ctx')), may hold values from 0.5 to 1.5
- ffn_gate: bfloat16 [2048, 5632], P(('fsdp', 'ctx'), 'tp'), may hold values from -0.125 to 0.125
- ffn_up: bfloat16 [2048, 5632], P(('fsdp', 'ctx'), 'tp'), may hold values from -0.125 to 0.125
- ffn_down: bfloat16 [5632, 2048], P('tp', ('fsdp', 'ctx')), may hold values from -0.078125 to 0.078125
Outputs:
- mixed: bfloat16 [4, 1536, 2048], P(None, ('fsdp', 'ctx'))
- grad_tokens: bfloat16 [4, 1536, 2048], P(None, ('fsdp', 'ctx'))
- grad_gain_in: float32 [2048], P(('fsdp', 'ctx'))
- grad_query_proj: float32 [2048, 2048], P(('fsdp', 'ctx'), 'tp')
- grad_key_proj: float32 [2048, 2048], P(('fsdp', 'ctx'), 'tp')
- grad_value_proj: float32 [2048, 4096], P(('fsdp', 'ctx'), 'tp')
- grad_gate_proj: float32 [2048, 4096], P(('fsdp', 'ctx'), 'tp')
- grad_alpha_proj: float32 [2048, 16], P(('fsdp', 'ctx'), 'tp')
- grad_beta_proj: float32 [2048, 16], P(('fsdp', 'ctx'), 'tp')
- grad_query_conv: float32 [4, 16, 128], P(None, 'tp', ('fsdp', 'ctx'))
- grad_key_conv: float32 [4, 16, 128], P(None, 'tp', ('fsdp', 'ctx'))
- value_convolved_gradient: float32 [4, 16, 256], P(None, 'tp', ('fsdp', 'ctx'))
- grad_decay_log: float32 [16], P('tp')
- grad_step_bias: float32 [16], P('tp')
- head_gain_gradient: float32 [256], P(('fsdp', 'ctx'))
- grad_out_proj: float32 [4096, 2048], P('tp', ('fsdp', 'ctx'))
- grad_gain_mid: float32 [2048], P(('fsdp', 'ctx'))
- grad_ffn_gate: float32 [2048, 5632], P(('fsdp', 'ctx'), 'tp')
- grad_ffn_up: float32 [2048, 5632], P(('fsdp', 'ctx'), 'tp')
- grad_ffn_down: float32 [5632, 2048], P('tp', ('fsdp', 'ctx'))
The draws below stay inside these ranges and needn't reach their ends.
Inputs may be any that keep to these rules, and one draw needn't show every extreme that they name: Each pack's lengths sum to at most 768; every sequence has at least one place; every pack has exactly one sequence of 761 places, never its first. `order`: each micro-batch's row is a permutation; the tokens of given indices g * 192 to (g + 1) * 192 - 1 fill exactly 24 places in each range h * 192 to (h + 1) * 192 - 1 of packed places.
All inputs are finite; a program needn't handle non-finite values.
Results may differ from the reference program's by a relative error of at most 0.018.
Values may be sent and summed in bfloat16 or wider, within the bound.
No kernel may reach another device: no remote copies, remote signals or barrier semaphores. Data moves between devices by JAX's collectives and lax.ppermute only.
A program may use at most 448 MiB of HBM per device.

```python
import jax
import jax.numpy as jnp
from jax import lax

D = 2048
HEADS = 16
HEAD_K = 128
HEAD_V = 256
FF = 5632
KCONV = 4
BLOCK = 64
SEQS = 8
MICRO = 4
TOK_DEV = 192
GROUPS = 8
PACKS = 2
PACK = 768
LONGEST = 761
TOK_MB = 1536
SHARE = 24


def draw_lengths(key, part):
    lead_places = max(0, PACK - TOK_DEV - LONGEST + 1)
    short_most = max(1, min((PACK - LONGEST - lead_places) // (SEQS - 1), (TOK_DEV - 1 - lead_places) // (SEQS - 2)))
    others = jax.random.randint(jax.random.fold_in(key, 11), (MICRO, PACKS, SEQS), 1, short_most + 1)
    chosen = jax.random.randint(jax.random.fold_in(key, 13), (MICRO, PACKS, 1), 1, SEQS)
    seq_index = jnp.arange(SEQS, dtype=jnp.int32)[None, None, :]
    others = others + jnp.where(seq_index == 0, lead_places, 0)
    return jnp.where(seq_index == chosen, LONGEST, others).astype(jnp.int32)


def shuffled(sub_key):
    return jax.random.permutation(sub_key, TOK_DEV).astype(jnp.int32)


def one_micro(micro_key):
    first_key = jax.random.fold_in(micro_key, 21)
    second_key = jax.random.fold_in(micro_key, 22)
    sending = jax.vmap(shuffled)(jax.random.split(first_key, GROUPS))
    sources = jnp.arange(GROUPS, dtype=jnp.int32)[:, None, None]
    given = sources * TOK_DEV + sending.reshape(GROUPS, GROUPS, SHARE)
    buffers = jnp.transpose(given, (1, 0, 2)).reshape(GROUPS, TOK_DEV)
    placing = jax.vmap(shuffled)(jax.random.split(second_key, GROUPS))
    targets = jnp.arange(GROUPS, dtype=jnp.int32)[:, None] * TOK_DEV + placing
    return jnp.zeros((TOK_MB,), jnp.int32).at[targets.reshape(-1)].set(buffers.reshape(-1))


def draw_order(key, part):
    return jax.vmap(one_micro)(jax.random.split(jax.random.fold_in(key, 20), MICRO)).astype(jnp.int32)


def strengthened(array, key, source, target, parts, factor):
    owner, partner = [(jnp.arange(array.shape[dim]) // (array.shape[dim] // parts)).reshape([-1 if axis == dim else 1 for axis in range(array.ndim)]) for dim in (source, target)]
    chosen = jax.random.permutation(key, parts)[partner]
    strong = (owner == chosen) | (owner == (partner + parts // 2) % parts)
    return jnp.where(strong, factor * array, array)


def levels(own_key, extent, shards, smallest, top_value):
    gain, own = 1.0, jax.random.fold_in(own_key, 6)
    for dim, parts in shards:
        draws = jnp.exp(jax.random.uniform(jax.random.fold_in(own, dim), (parts,), jnp.float32, smallest / len(shards), top_value / len(shards)))
        gain = gain * jnp.repeat(draws, extent[dim] // parts).reshape([-1 if axis == dim else 1 for axis in range(len(extent))])
    return gain


def noise(key, shape, scale, most, cuts=(), held_as=jnp.bfloat16):
    result = jax.random.normal(key, shape, jnp.float32) * scale
    if len(cuts) > 0:
        result = levels(key, shape, cuts, -0.22, 0.18) * result
    return jnp.clip(result, min=-most, max=most).astype(held_as)


def heavy_noise(key, extent, deviation, reach, cuts, heavy, kind=jnp.bfloat16):
    values = deviation * jax.random.normal(key, extent, jnp.float32)
    if cuts:
        values = values * levels(key, extent, cuts, -0.22, 0.18)
    return jnp.clip(strengthened(values, jax.random.fold_in(key, 3), *heavy), -reach, reach).astype(kind)


def setup_inputs(seed: int = 0) -> dict:
    keys = jax.random.split(jax.random.key(seed), 23)
    return {
        "tokens": heavy_noise(keys[0], (MICRO, TOK_MB, D), 1.0, 6.0, ((1, 8),), (1, 2, 8, 2.0)),
        "cotangent": heavy_noise(keys[1], (MICRO, TOK_MB, D), 1.0, 6.0, ((1, 8),), (1, 2, 8, 2.0)),
        "lengths": draw_lengths(jax.random.fold_in(keys[22], 71), 0),
        "order": draw_order(jax.random.fold_in(keys[22], 71), 0),
        "gain_in": jnp.clip(1.0 + 0.1 * jax.random.normal(keys[4], (D,), jnp.float32), 0.5, 1.5).astype(jnp.bfloat16),
        "query_proj": noise(keys[5], (D, HEADS * HEAD_K), D ** -0.5, 0.125, ((0, 8), (1, 4))),
        "key_proj": noise(keys[6], (D, HEADS * HEAD_K), D ** -0.5, 0.125, ((0, 8), (1, 4))),
        "value_proj": noise(keys[7], (D, HEADS * HEAD_V), D ** -0.5, 0.125, ((0, 8), (1, 4))),
        "gate_proj": noise(keys[8], (D, HEADS * HEAD_V), D ** -0.5, 0.125, ((0, 8), (1, 4))),
        "alpha_proj": noise(keys[9], (D, HEADS), (D // 4) ** -0.5, 0.25, ((0, 8), (1, 4))),
        "beta_proj": noise(keys[10], (D, HEADS), D ** -0.5, 0.125, ((0, 8), (1, 4))),
        "query_conv": noise(keys[11], (KCONV, HEADS, HEAD_K), KCONV ** -0.5, 3.0, ((1, 4), (2, 8))),
        "key_conv": noise(keys[12], (KCONV, HEADS, HEAD_K), KCONV ** -0.5, 3.0, ((1, 4), (2, 8))),
        "value_conv": noise(keys[13], (KCONV, HEADS, HEAD_V), KCONV ** -0.5, 3.0, ((1, 4), (2, 8))),
        "decay_log": jnp.clip(-0.9 + 3.4 * jax.random.uniform(keys[14], (HEADS,), jnp.float32) ** levels(keys[14], (HEADS,), ((0, 4),), -0.2, 0.2), -0.9, 2.5),
        "step_bias": jnp.clip(-7.0 + 2.0 * jax.random.uniform(keys[15], (HEADS,), jnp.float32) ** levels(keys[15], (HEADS,), ((0, 4),), -0.2, 0.2), -7.0, -5.0),
        "gain_head": jnp.clip(1.0 + 0.1 * jax.random.normal(keys[16], (HEAD_V,), jnp.float32), 0.5, 1.5).astype(jnp.bfloat16),
        "out_proj": noise(keys[17], (HEADS * HEAD_V, D), (HEADS * HEAD_V // 2) ** -0.5, 0.125, ((0, 4), (1, 8))),
        "gain_mid": jnp.clip(1.0 + 0.1 * jax.random.normal(keys[18], (D,), jnp.float32), 0.5, 1.5).astype(jnp.bfloat16),
        "ffn_gate": noise(keys[19], (D, FF), D ** -0.5, 0.125, ((0, 8), (1, 4))),
        "ffn_up": noise(keys[20], (D, FF), D ** -0.5, 0.125, ((0, 8), (1, 4))),
        "ffn_down": noise(keys[21], (FF, D), FF ** -0.5, 0.078125, ((0, 4), (1, 8))),
    }


@jax.custom_vjp
def low(v):
    return lax.optimization_barrier(v.astype(jnp.bfloat16)).astype(jnp.float32)

@jax.custom_vjp
def low_back(v):
    return v

def low_keep(v):
    return (low(v), None)

def low_pass(kept, grad):
    return (grad,)

def back_keep(v):
    return (v, None)

def back_low(kept, grad):
    return (low(grad),)
low.defvjp(low_keep, low_pass)
low_back.defvjp(back_keep, back_low)
square_eps = 1e-05
unit_eps = 1e-06

def product(left, right):
    return jnp.dot(left, right, precision=lax.Precision.HIGHEST, preferred_element_type=jnp.float32)

def scale_rows(values, gain_vec):
    return values * lax.rsqrt(lax.optimization_barrier(jnp.mean(values * values, axis=-1, keepdims=True)) + square_eps) * gain_vec

def unit_rows(values):
    return values * lax.rsqrt(lax.optimization_barrier(jnp.sum(values * values, axis=-1, keepdims=True)) + unit_eps)

def place_info(length_row, places):
    end_places = jnp.cumsum(length_row)
    starts = end_places - length_row
    segment = lax.optimization_barrier(jnp.sum((places[:, None] >= starts[None, :]).astype(jnp.int32), axis=1)) - 1
    inside = jnp.logical_and(places >= 0, places < end_places[-1]).astype(jnp.float32)
    return (segment.astype(jnp.int32), inside)

def convolve(extended, segment_ext, weight):
    span_size = weight.shape[0]
    row_count = extended.shape[0] - span_size + 1
    segment = segment_ext[span_size - 1:]
    running = jnp.zeros((row_count, extended.shape[1]), jnp.float32)
    for offset in range(span_size):
        same_seq = (segment_ext[offset:offset + row_count] == segment).astype(jnp.float32)
        running = running + weight[offset][None, :] * extended[offset:offset + row_count] * same_seq[:, None]
    return jax.nn.silu(running)

def delta_rule(queries, keys_unit, values, betas, log_decays, resets):
    length_all = queries.shape[0]
    head_count = keys_unit.shape[1]
    key_size = keys_unit.shape[2]
    value_size = values.shape[2]

    def one_place(memory_state, inputs):
        query_vector_row, key_vector_row, value_row, beta_row, decay_row, reset_row = inputs
        keep_rate = jnp.exp(decay_row) * (1.0 - reset_row)
        decayed_state = memory_state * keep_rate[:, None, None]
        predicted_value = jnp.einsum('diw,di->dw', decayed_state, key_vector_row, precision=lax.Precision.HIGHEST)
        pseudo = value_row - predicted_value
        memory_state = decayed_state + beta_row[:, None, None] * key_vector_row[:, :, None] * pseudo[:, None, :]
        output_rows = jnp.einsum('diw,di->dw', memory_state, query_vector_row, precision=lax.Precision.HIGHEST)
        return (memory_state, output_rows)

    def one_block(memory_state, inputs):
        return lax.scan(one_place, memory_state, inputs)
    blocks = length_all // BLOCK
    inputs = tuple((item.reshape((blocks, BLOCK) + item.shape[1:]) for item in (queries, keys_unit, values, betas, log_decays, resets)))
    initial = jnp.zeros((head_count, key_size, value_size), jnp.float32)
    final_state, outputs = lax.scan(jax.checkpoint(one_block), initial, inputs)
    return outputs.reshape(length_all, head_count, value_size)

def pack_forward(tokens_pack, segment, inside, resets, weight_set):
    gain_in, query_proj, key_proj, value_proj, gate_proj, alpha_proj, beta_proj, query_conv, key_conv, value_conv, decay_log, step_bias, gain_head, out_proj, gain_mid, ffn_gate, ffn_up, ffn_down = weight_set
    row_count = tokens_pack.shape[0]
    head_count = decay_log.shape[0]
    key_size = query_conv.shape[2]
    value_size = value_conv.shape[2]
    span_size = query_conv.shape[0]
    segment_ext = jnp.concatenate([jnp.full((span_size - 1,), -1, jnp.int32), segment])
    normed_in = low(scale_rows(tokens_pack, gain_in))
    proj_query = low_back(product(normed_in, query_proj))
    proj_key = low_back(product(normed_in, key_proj))
    proj_value = low_back(product(normed_in, value_proj))
    proj_gate = low_back(product(normed_in, gate_proj))
    proj_alpha = low_back(product(normed_in, alpha_proj))
    proj_beta = low_back(product(normed_in, beta_proj))

    def conv_part(projected, conv_weight):
        extended = jnp.concatenate([jnp.zeros((span_size - 1, projected.shape[1]), jnp.float32), projected], axis=0)
        return convolve(extended, segment_ext, conv_weight.reshape(span_size, -1))
    queries = unit_rows(conv_part(proj_query, query_conv).reshape(row_count, head_count, key_size)) * key_size ** (-0.5)
    keys_unit = unit_rows(conv_part(proj_key, key_conv).reshape(row_count, head_count, key_size))
    values = conv_part(proj_value, value_conv).reshape(row_count, head_count, value_size)
    betas = jax.nn.sigmoid(proj_beta) * inside[:, None]
    log_decays = -jnp.exp(decay_log) * jax.nn.softplus(proj_alpha + step_bias)
    outputs = delta_rule(queries, keys_unit, values, betas, log_decays, resets)
    gated = scale_rows(outputs, gain_head) * jax.nn.silu(proj_gate.reshape(row_count, head_count, value_size)) * inside[:, None, None]
    mixer = low_back(product(low(gated.reshape(row_count, head_count * value_size)), out_proj))
    hidden_in = tokens_pack + mixer
    mid_low = low(scale_rows(hidden_in, gain_mid))
    gate_value = low_back(product(mid_low, ffn_gate))
    up_value = low_back(product(mid_low, ffn_up))
    hidden_low = low(jax.nn.silu(gate_value) * up_value)
    return hidden_in + low_back(product(hidden_low, ffn_down))

def pick_rows(source, picked):
    return source[picked]

def put_rows(source, picked):
    return jnp.zeros_like(source).at[picked].set(source)

def reference(tokens, cotangent, lengths, order, gain_in, query_proj, key_proj, value_proj, gate_proj, alpha_proj, beta_proj, query_conv, key_conv, value_conv, decay_log, step_bias, gain_head, out_proj, gain_mid, ffn_gate, ffn_up, ffn_down):
    weights = tuple((item.astype(jnp.float32) for item in (gain_in, query_proj, key_proj, value_proj, gate_proj, alpha_proj, beta_proj, query_conv, key_conv, value_conv, decay_log, step_bias, gain_head, out_proj, gain_mid, ffn_gate, ffn_up, ffn_down)))
    packed_tokens = jax.vmap(pick_rows)(tokens.astype(jnp.float32), order).reshape(MICRO * PACKS, PACK, D)
    packed_grads = jax.vmap(pick_rows)(cotangent.astype(jnp.float32), order).reshape(MICRO * PACKS, PACK, D)
    places = jnp.arange(PACK, dtype=jnp.int32)

    def info_row(length_row):
        return place_info(length_row, places)
    segments, insides = jax.vmap(info_row)(lengths.reshape(MICRO * PACKS, SEQS))
    previous = jnp.concatenate([jnp.full((MICRO * PACKS, 1), -1, jnp.int32), segments[:, :-1]], axis=1)
    resets = (segments != previous).astype(jnp.float32)

    def forward(packed, weight_set):

        def one_pack(carried, inputs):
            tokens_pack, segment, inside, reset_row = inputs
            return (carried, pack_forward(tokens_pack, segment, inside, reset_row, weight_set))
        unused, outputs = lax.scan(jax.checkpoint(one_pack), jnp.zeros((), jnp.float32), (packed, segments, insides, resets))
        return outputs
    outputs, pullback = jax.vjp(forward, packed_tokens, weights)
    grad_packed, grad_weights = pullback(packed_grads)
    mixed = jax.vmap(put_rows)(outputs.reshape(MICRO, TOK_MB, D), order).astype(jnp.bfloat16)
    grad_tokens = jax.vmap(put_rows)(grad_packed.reshape(MICRO, TOK_MB, D), order).astype(jnp.bfloat16)
    return (mixed, grad_tokens, grad_weights[0], grad_weights[1], grad_weights[2], grad_weights[3], grad_weights[4], grad_weights[5], grad_weights[6], grad_weights[7], grad_weights[8], grad_weights[9], grad_weights[10], grad_weights[11], grad_weights[12], grad_weights[13], grad_weights[14], grad_weights[15], grad_weights[16], grad_weights[17])
```

```python
import functools
import jax
import jax.numpy as jnp
from jax import lax
from jax.sharding import PartitionSpec as P
from jax.experimental import pallas as pl
from jax.experimental.pallas import tpu as pltpu

CHUNK = 128
LANES = 128
PAD = 8
square_eps = 1e-05
unit_eps = 1e-06
F32 = jnp.float32
BF16 = jnp.bfloat16


def dot_nn(left, right):
    return lax.dot_general(left, right, (((1,), (0,)), ((), ())), preferred_element_type=F32)


def dot_nt(left, right):
    return lax.dot_general(left, right, (((1,), (1,)), ((), ())), preferred_element_type=F32)


def dot_tn(left, right):
    return lax.dot_general(left, right, (((0,), (0,)), ((), ())), preferred_element_type=F32)


def halves(value):
    high = value.astype(BF16)
    return high, (value - high.astype(F32)).astype(BF16)


def dot_fine(left, right):
    left_high, left_low = halves(left)
    right_high, right_low = halves(right)
    return (
        dot_nn(left_high, right_high)
        + dot_nn(left_high, right_low)
        + dot_nn(left_low, right_high)
    )


def sum_by(mask, value):
    high, rest = halves(value)
    middle, low = halves(value - high.astype(F32))
    return dot_nn(mask, high) + dot_nn(mask, middle) + dot_nn(mask, low)


def sigmoid(value):
    return 1.0 / (1.0 + jnp.exp(-value))


def softplus(value):
    return jnp.maximum(value, 0.0) + jnp.log1p(jnp.exp(-jnp.abs(value)))


def inverse_lower(lower_mat, row_id, col_id):
    size = lower_mat.shape[0]

    def level(width):
        same = row_id // (2 * width) == col_id // (2 * width)
        return same & ((row_id // width) % 2 == 1) & ((col_id // width) % 2 == 0)

    unit = jnp.where(row_id == col_id, 1.0, 0.0)
    result = unit - jnp.where(level(1), lower_mat, 0.0)
    width = 2
    while width < size:
        part = jnp.where(level(width), lower_mat, 0.0)
        result = result - dot_fine(dot_fine(result, part), result)
        width *= 2
    return result


def chunk_basics(gates, par, info, seg_row, row_id, col_id, lane_id, head_count):
    step = gates + par[1:2, :]
    log_decay = jnp.where(lane_id < head_count, par[0:1, :] * softplus(step), 0.0)
    beta_raw = sigmoid(gates)
    valid = info[:, 1:2]
    lower = row_id >= col_id
    cumulative = sum_by(jnp.where(lower, 1.0, 0.0).astype(BF16), log_decay)
    both = jnp.where(lane_id < head_count, cumulative, beta_raw * valid)
    turned = jnp.transpose(both)
    inner = lower & (info[:, 0:1] == seg_row)
    return step, log_decay, beta_raw, both, turned, inner


def activations(ext, taps, masks, start, stop, rows):
    value = taps[3:4, start:stop] * ext[PAD : PAD + rows, start:stop]
    for distance in (1, 2, 3):
        shifted = ext[PAD - distance : PAD - distance + rows, start:stop]
        value = value + masks[distance - 1] * (taps[3 - distance : 4 - distance, start:stop] * shifted)
    return value


def forward_kernel(
    head_count, key_size, value_size,
    proj, info_ref, segr, par_ref, taps, gain_ref,
    normed_out, state_out, inverse_out, pseudo_out, output_out,
    state, ext,
):
    rows = proj.shape[0]
    width = head_count * (2 * key_size + value_size)
    gate_at = width
    tail_at = width + head_count * value_size

    @pl.when(pl.program_id(0) == 0)
    def start():
        state[...] = jnp.zeros_like(state)
        ext[0:PAD, :] = jnp.zeros((PAD, width), F32)

    ext[PAD : PAD + rows, :] = proj[:, 0:width]
    info = info_ref[...]
    row_id = lax.broadcasted_iota(jnp.int32, (rows, rows), 0)
    col_id = lax.broadcasted_iota(jnp.int32, (rows, rows), 1)
    lane_id = lax.broadcasted_iota(jnp.int32, (rows, LANES), 1)
    masks = tuple(info[:, 1 + d : 2 + d] for d in (1, 2, 3))
    valid = info[:, 1:2]
    unused, log_decay, beta_raw, both, turned, inner = chunk_basics(
        proj[:, tail_at : tail_at + LANES], par_ref[...], info, segr[0:1, :],
        row_id, col_id, lane_id, head_count,
    )
    carried_mask = info[:, 8:9]
    tail_mask = info[:, 9:10]
    strict = row_id > col_id
    key_at = head_count * key_size
    value_at = 2 * key_at
    for head in range(head_count):
        ks = key_size
        vs = value_size
        act_q = activations(ext, taps, masks, head * ks, (head + 1) * ks, rows)
        act_k = activations(ext, taps, masks, key_at + head * ks, key_at + (head + 1) * ks, rows)
        act_v = activations(ext, taps, masks, value_at + head * vs, value_at + (head + 1) * vs, rows)
        cq = act_q * sigmoid(act_q)
        ck = act_k * sigmoid(act_k)
        values = act_v * sigmoid(act_v)
        query = cq * (lax.rsqrt(jnp.sum(cq * cq, axis=1, keepdims=True) + unit_eps) * ks ** -0.5)
        key = ck * lax.rsqrt(jnp.sum(ck * ck, axis=1, keepdims=True) + unit_eps)
        qb = query.astype(BF16)
        kb = key.astype(BF16)
        cum = both[:, head : head + 1]
        beta = both[:, head_count + head : head_count + head + 1]
        cum_row = turned[head : head + 1, :]
        beta_row = turned[head_count + head : head_count + head + 1, :]
        decays = jnp.where(inner, jnp.exp(jnp.minimum(cum - cum_row, 0.0)), 0.0)
        lower_mat = jnp.where(strict, decays * dot_nt(kb, kb) * beta_row, 0.0)
        inverse = inverse_lower(lower_mat, row_id, col_id)
        carried = jnp.exp(cum) * carried_mask
        last = cum[rows - 1 : rows, :]
        tail = jnp.exp(last - cum) * tail_mask
        keep = carried[rows - 1 : rows, :]
        before = state[head]
        state_out[0, head] = before
        sb = before.astype(BF16)
        target = values - carried * dot_nn(kb, sb)
        ib = inverse.astype(BF16)
        pseudo = dot_nn(ib, target.astype(BF16))
        inverse_out[0, head] = ib
        pseudo_out[:, head * vs : (head + 1) * vs] = pseudo
        weighted = beta * pseudo
        mix = decays * dot_nt(qb, kb)
        output = carried * dot_nn(qb, sb) + dot_nn(mix.astype(BF16), weighted.astype(BF16))
        output_out[:, head * vs : (head + 1) * vs] = output
        state[head] = keep * before + dot_tn(kb, (tail * weighted).astype(BF16))
        gate = proj[:, gate_at + head * vs : gate_at + (head + 1) * vs]
        scale = lax.rsqrt(jnp.mean(output * output, axis=1, keepdims=True) + square_eps)
        normed = output * scale * gain_ref[0:1, :] * (gate * sigmoid(gate)) * valid
        normed_out[:, head * vs : (head + 1) * vs] = normed.astype(BF16)
    ext[0:PAD, :] = ext[rows : rows + PAD, :]


def backward_kernel(
    head_count, key_size, value_size,
    proj, prior, info_ref, segr, par_ref, taps, gain_ref,
    state_in, inverse_in, pseudo_in, output_in, dnormed,
    grad_out, conv_out, gain_out, small_out,
    dstate, ext, dext,
):
    rows = proj.shape[0]
    width = head_count * (2 * key_size + value_size)
    gate_at = width
    tail_at = width + head_count * value_size
    place = pl.program_id(0)
    count = pl.num_programs(0)

    @pl.when(place == 0)
    def start():
        dstate[...] = jnp.zeros_like(dstate)
        dext[rows : rows + PAD, :] = jnp.zeros((PAD, width), F32)
        conv_out[...] = jnp.zeros_like(conv_out)
        gain_out[...] = jnp.zeros_like(gain_out)
        small_out[...] = jnp.zeros_like(small_out)

    first = place == count - 1
    ext[0:PAD, :] = jnp.where(first, 0.0, prior[:, 0:width])
    ext[PAD : PAD + rows, :] = proj[:, 0:width]
    info = info_ref[...]
    row_id = lax.broadcasted_iota(jnp.int32, (rows, rows), 0)
    col_id = lax.broadcasted_iota(jnp.int32, (rows, rows), 1)
    lane_id = lax.broadcasted_iota(jnp.int32, (rows, LANES), 1)
    masks = tuple(info[:, 1 + d : 2 + d] for d in (1, 2, 3))
    later = tuple(info[:, 4 + d : 5 + d] for d in (1, 2, 3))
    valid = info[:, 1:2]
    step, log_decay, beta_raw, both, turned, inner = chunk_basics(
        proj[:, tail_at : tail_at + LANES], par_ref[...], info, segr[0:1, :],
        row_id, col_id, lane_id, head_count,
    )
    carried_mask = info[:, 8:9]
    tail_mask = info[:, 9:10]
    strict = row_id > col_id
    last_row = lax.broadcasted_iota(jnp.int32, (rows, 1), 0) == rows - 1
    row_of = lax.broadcasted_iota(jnp.int32, (LANES, rows), 0)
    ks = key_size
    vs = value_size
    key_at = head_count * ks
    value_at = 2 * key_at
    dcum = jnp.zeros((rows, LANES), F32)
    dturned = jnp.zeros((LANES, rows), F32)

    def fold(value):
        return jnp.sum(value.reshape(rows // PAD, PAD, value.shape[1]), axis=0)

    def conv_back(da, start, stop):
        dext[0:rows, start:stop] = da
        back = taps[3:4, start:stop] * da
        conv_out[3 * PAD : 4 * PAD, start:stop] += fold(da * ext[PAD : PAD + rows, start:stop])
        for d in (1, 2, 3):
            back = back + later[d - 1] * (taps[3 - d : 4 - d, start:stop] * dext[d : d + rows, start:stop])
            shifted = ext[PAD - d : PAD - d + rows, start:stop]
            conv_out[(3 - d) * PAD : (4 - d) * PAD, start:stop] += fold(masks[d - 1] * da * shifted)
        grad_out[:, start:stop] = back.astype(BF16)

    for head in range(head_count):
        act_q = activations(ext, taps, masks, head * ks, (head + 1) * ks, rows)
        act_k = activations(ext, taps, masks, key_at + head * ks, key_at + (head + 1) * ks, rows)
        act_v = activations(ext, taps, masks, value_at + head * vs, value_at + (head + 1) * vs, rows)
        sig_q, sig_k, sig_v = sigmoid(act_q), sigmoid(act_k), sigmoid(act_v)
        cq, ck, values = act_q * sig_q, act_k * sig_k, act_v * sig_v
        rate_q = lax.rsqrt(jnp.sum(cq * cq, axis=1, keepdims=True) + unit_eps)
        rate_k = lax.rsqrt(jnp.sum(ck * ck, axis=1, keepdims=True) + unit_eps)
        unit_q = cq * rate_q
        query = unit_q * ks ** -0.5
        key = ck * rate_k
        qb = query.astype(BF16)
        kb = key.astype(BF16)
        cum = both[:, head : head + 1]
        beta = both[:, head_count + head : head_count + head + 1]
        cum_row = turned[head : head + 1, :]
        beta_row = turned[head_count + head : head_count + head + 1, :]
        decays = jnp.where(inner, jnp.exp(jnp.minimum(cum - cum_row, 0.0)), 0.0)
        carried = jnp.exp(cum) * carried_mask
        tail = jnp.exp(cum[rows - 1 : rows, :] - cum) * tail_mask
        keep = carried[rows - 1 : rows, :]
        before = state_in[0, head]
        sb = before.astype(BF16)
        ib = inverse_in[0, head]
        pseudo = pseudo_in[:, head * vs : (head + 1) * vs]
        output = output_in[:, head * vs : (head + 1) * vs]
        gate = proj[:, gate_at + head * vs : gate_at + (head + 1) * vs]
        given = dnormed[:, head * vs : (head + 1) * vs] * valid
        gain = gain_ref[0:1, :]
        scale = lax.rsqrt(jnp.mean(output * output, axis=1, keepdims=True) + square_eps)
        unit_o = output * scale
        sig_g = sigmoid(gate)
        silu_g = gate * sig_g
        dunit = given * gain * silu_g
        doutput = scale * (dunit - unit_o * jnp.mean(unit_o * dunit, axis=1, keepdims=True))
        dgate = given * unit_o * gain * (sig_g * (1.0 + gate * (1.0 - sig_g)))
        gain_out[:, head * vs : (head + 1) * vs] += fold(given * unit_o * silu_g)
        grad_out[:, gate_at + head * vs : gate_at + (head + 1) * vs] = dgate.astype(BF16)
        dob = doutput.astype(BF16)
        weighted = beta * pseudo
        wb = weighted.astype(BF16)
        gram = dot_nt(kb, kb)
        cross = dot_nt(qb, kb)
        mix = decays * cross
        after = dstate[head]
        ab = after.astype(BF16)
        from_state = dot_nn(kb, ab)
        dweighted = dot_tn(mix.astype(BF16), dob) + tail * from_state
        dbeta = jnp.sum(dweighted * pseudo, axis=1, keepdims=True)
        dtarget = dot_tn(ib, (beta * dweighted).astype(BF16))
        dtb = dtarget.astype(BF16)
        read = dot_nn(kb, sb)
        dcarried = jnp.sum(doutput * dot_nn(qb, sb), axis=1, keepdims=True) - jnp.sum(
            dtarget * read, axis=1, keepdims=True
        )
        dtail = jnp.sum(weighted * from_state, axis=1, keepdims=True)
        dkeep = jnp.sum(jnp.sum(after * before, axis=1, keepdims=True), axis=0, keepdims=True)
        cdo = (carried * doutput).astype(BF16)
        cdt = (carried * dtarget).astype(BF16)
        dstate[head] = keep * after + dot_tn(qb, cdo) - dot_tn(kb, cdt)
        dmix = dot_nt(dob, wb)
        dcross = (dmix * decays).astype(BF16)
        dlower = jnp.where(strict, -dot_nt(dtb, pseudo.astype(BF16)), 0.0) * decays
        dgram = (dlower * beta_row).astype(BF16)
        plain = dlower * gram
        inner_grad = dmix * mix + plain * beta_row
        dquery = dot_nt(cdo, sb) + dot_nn(dcross, kb)
        dkey = (
            dot_tn(dcross, qb)
            + dot_nn(dgram, kb)
            + dot_tn(dgram, kb)
            + dot_nt((tail * weighted).astype(BF16), ab)
            - dot_nt(cdt, sb)
        )
        dlast = jnp.sum(dtail * tail, axis=0, keepdims=True) + dkeep * keep
        dcum_col = (
            jnp.sum(inner_grad, axis=1, keepdims=True)
            + dcarried * carried
            - dtail * tail
            + jnp.where(last_row, dlast, 0.0)
        )
        dcum = jnp.where(lane_id == head, dcum_col, dcum)
        dcum = jnp.where(lane_id == head_count + head, dbeta, dcum)
        dturned = jnp.where(row_of == head, -jnp.sum(inner_grad, axis=0, keepdims=True), dturned)
        dturned = jnp.where(
            row_of == head_count + head, jnp.sum(plain, axis=0, keepdims=True), dturned
        )
        dq_scaled = dquery * ks ** -0.5
        dcq = (dq_scaled - unit_q * jnp.sum(unit_q * dq_scaled, axis=1, keepdims=True)) * rate_q
        dck = (dkey - key * jnp.sum(key * dkey, axis=1, keepdims=True)) * rate_k
        conv_back(dcq * (sig_q * (1.0 + act_q * (1.0 - sig_q))), head * ks, (head + 1) * ks)
        conv_back(
            dck * (sig_k * (1.0 + act_k * (1.0 - sig_k))), key_at + head * ks, key_at + (head + 1) * ks
        )
        conv_back(
            dtarget * (sig_v * (1.0 + act_v * (1.0 - sig_v))),
            value_at + head * vs,
            value_at + (head + 1) * vs,
        )
    dboth = dcum + jnp.transpose(dturned)
    upper = jnp.where(row_id <= col_id, 1.0, 0.0).astype(BF16)
    dlog = sum_by(upper, jnp.where(lane_id < head_count, dboth, 0.0))
    dalpha = dlog * par_ref[0:1, :] * sigmoid(step)
    dbeta_raw = dboth * valid * beta_raw * (1.0 - beta_raw)
    tail_grad = jnp.where(
        lane_id < head_count, dalpha, jnp.where(lane_id < 2 * head_count, dbeta_raw, 0.0)
    )
    grad_out[:, tail_at : tail_at + LANES] = tail_grad.astype(BF16)
    small_out[0:PAD, :] += fold(dlog * log_decay)
    small_out[PAD : 2 * PAD, :] += fold(jnp.where(lane_id < head_count, dalpha, 0.0))
    dext[rows : rows + PAD, :] = dext[0:PAD, :]


def delta_forward(proj, info, seg_rows, par, taps, gain, sizes):
    head_count, key_size, value_size = sizes
    total, columns = proj.shape
    steps = total // CHUNK
    width = head_count * (2 * key_size + value_size)
    span = head_count * value_size
    whole = lambda a: pl.BlockSpec(a.shape, lambda i: (0, 0))
    by_rows = lambda n: pl.BlockSpec((CHUNK, n), lambda i: (i, 0))
    return pl.pallas_call(
        functools.partial(forward_kernel, head_count, key_size, value_size),
        grid=(steps,),
        in_specs=[
            by_rows(columns),
            by_rows(LANES),
            pl.BlockSpec((PAD, CHUNK), lambda i: (0, i)),
            whole(par),
            whole(taps),
            whole(gain),
        ],
        out_specs=[
            by_rows(span),
            pl.BlockSpec((1, head_count, key_size, value_size), lambda i: (i, 0, 0, 0)),
            pl.BlockSpec((1, head_count, CHUNK, CHUNK), lambda i: (i, 0, 0, 0)),
            by_rows(span),
            by_rows(span),
        ],
        out_shape=[
            jax.ShapeDtypeStruct((total, span), BF16),
            jax.ShapeDtypeStruct((steps, head_count, key_size, value_size), F32),
            jax.ShapeDtypeStruct((steps, head_count, CHUNK, CHUNK), BF16),
            jax.ShapeDtypeStruct((total, span), F32),
            jax.ShapeDtypeStruct((total, span), F32),
        ],
        scratch_shapes=[
            pltpu.VMEM((head_count, key_size, value_size), F32),
            pltpu.VMEM((CHUNK + PAD, width), F32),
        ],
        compiler_params=pltpu.CompilerParams(vmem_limit_bytes=48 * 1024 * 1024),
        name="delta_forward",
    )(proj, info, seg_rows, par, taps, gain)


def delta_backward(proj, info, seg_rows, par, taps, gain, saved, dnormed, sizes):
    head_count, key_size, value_size = sizes
    total, columns = proj.shape
    steps = total // CHUNK
    width = head_count * (2 * key_size + value_size)
    span = head_count * value_size
    states, inverses, pseudos, outputs = saved
    blocks = CHUNK // PAD
    turn = lambda i: steps - 1 - i
    whole = lambda a: pl.BlockSpec(a.shape, lambda i: (0, 0))
    by_rows = lambda n: pl.BlockSpec((CHUNK, n), lambda i: (turn(i), 0))
    return pl.pallas_call(
        functools.partial(backward_kernel, head_count, key_size, value_size),
        grid=(steps,),
        in_specs=[
            by_rows(columns),
            pl.BlockSpec((PAD, columns), lambda i: (jnp.maximum(turn(i) * blocks - 1, 0), 0)),
            by_rows(LANES),
            pl.BlockSpec((PAD, CHUNK), lambda i: (0, turn(i))),
            whole(par),
            whole(taps),
            whole(gain),
            pl.BlockSpec((1, head_count, key_size, value_size), lambda i: (turn(i), 0, 0, 0)),
            pl.BlockSpec((1, head_count, CHUNK, CHUNK), lambda i: (turn(i), 0, 0, 0)),
            by_rows(span),
            by_rows(span),
            by_rows(span),
        ],
        out_specs=[
            by_rows(columns),
            pl.BlockSpec((4 * PAD, width), lambda i: (0, 0)),
            pl.BlockSpec((PAD, span), lambda i: (0, 0)),
            pl.BlockSpec((2 * PAD, LANES), lambda i: (0, 0)),
        ],
        out_shape=[
            jax.ShapeDtypeStruct((total, columns), BF16),
            jax.ShapeDtypeStruct((4 * PAD, width), F32),
            jax.ShapeDtypeStruct((PAD, span), F32),
            jax.ShapeDtypeStruct((2 * PAD, LANES), F32),
        ],
        scratch_shapes=[
            pltpu.VMEM((head_count, key_size, value_size), F32),
            pltpu.VMEM((CHUNK + PAD, width), F32),
            pltpu.VMEM((CHUNK + PAD, width), F32),
        ],
        compiler_params=pltpu.CompilerParams(vmem_limit_bytes=48 * 1024 * 1024),
        name="delta_backward",
    )(proj, proj, info, seg_rows, par, taps, gain, states, inverses, pseudos, outputs, dnormed)


def place_arrays(length_row, total):
    places = jnp.arange(total, dtype=jnp.int32)
    ids = jnp.arange(length_row.shape[0])
    ends = jnp.sum(jnp.where(ids[None, :] <= ids[:, None], length_row[None, :], 0), axis=1)
    starts = ends - length_row

    def seg_at(at):
        return jnp.sum((at[:, None] >= starts[None, :]).astype(jnp.int32), axis=1) - 1

    segment = seg_at(places)
    valid = (places < ends[-1]).astype(F32)
    lanes = [segment.astype(F32), valid]
    for d in (1, 2, 3):
        lanes.append((seg_at(places - d) == segment).astype(F32))
    for d in (1, 2, 3):
        lanes.append(((seg_at(places + d) == segment) & (places + d < total)).astype(F32))
    head_place = places - places % CHUNK
    lanes.append(((seg_at(head_place - 1) == segment) & (head_place > 0)).astype(F32))
    lanes.append((seg_at(head_place + CHUNK - 1) == segment).astype(F32))
    info = jnp.stack(lanes, axis=1)
    info = jnp.pad(info, ((0, 0), (0, LANES - len(lanes))))
    rows = jnp.broadcast_to(segment.astype(F32)[None, :], (PAD, total))
    return info, rows


GROUP = ("fsdp", "ctx")


def pair_rows(values):
    high, low = halves(values)
    return jnp.stack([high, low], axis=-2)


def share_sum(part):
    count = lax.axis_size("tp")
    moved = lax.all_to_all(part, "tp", split_axis=0, concat_axis=0, tiled=True)
    return jnp.sum(moved.reshape(count, -1, part.shape[1]).astype(F32), axis=0)


def per_device(
    tokens, cotangent, lengths, order, gain_in, query_proj, key_proj, value_proj, gate_proj,
    alpha_proj, beta_proj, query_conv, key_conv, value_conv, decay_log, step_bias, gain_head,
    out_proj, gain_mid, ffn_gate, ffn_up, ffn_down,
):
    groups = lax.axis_size(GROUP)
    tp_count = lax.axis_size("tp")
    tp_place = lax.axis_index("tp")
    group = lax.axis_index(GROUP)
    micros, rows, width = tokens.shape
    packs = lengths.shape[1]
    all_rows = order.shape[1]
    pack_rows = all_rows // packs
    assert micros * packs == groups and pack_rows == tp_count * rows
    share = rows // groups
    heads = decay_log.shape[0]
    spans = query_conv.shape[0]
    key_size = query_conv.shape[2] * groups
    value_size = value_conv.shape[2] * groups
    sizes = (heads, key_size, value_size)
    key_cols = heads * key_size
    value_cols = heads * value_size
    own = width // groups
    my_micro = group // packs
    my_pack = group % packs

    strict_up = jnp.triu(jnp.ones((rows, rows), BF16), 1)
    mine = (order // rows == group).reshape(micros * packs * tp_count, rows)
    rank = jnp.dot(mine.astype(BF16), strict_up, preferred_element_type=F32).astype(jnp.int32)
    rank = rank.reshape(micros, packs, tp_count, rows)
    ids = jnp.arange(packs * tp_count, dtype=jnp.int32).reshape(packs, tp_count, 1)
    send_slot = (ids * share + rank).reshape(micros, 1, all_rows)
    held = rows + PAD
    pack_id = jnp.arange(groups, dtype=jnp.int32).reshape(micros, packs, 1, 1)
    tp_id = jnp.arange(tp_count, dtype=jnp.int32).reshape(tp_count, 1)
    back_slot = (tp_id * held + pack_id * share + rank).reshape(micros, 1, all_rows)
    local = group * rows + jnp.arange(rows, dtype=jnp.int32)
    hit = order[:, None, :] == local[None, :, None]
    send_at = jnp.sum(jnp.where(hit, send_slot, 0), axis=2)
    back_at = jnp.sum(jnp.where(hit, back_slot, 0), axis=2).reshape(micros * rows)
    row_ids = jnp.arange(rows, dtype=jnp.int32)
    send_pick = (row_ids[None, :, None] == send_at[:, None, :]).astype(BF16)
    back_ids = jnp.arange(tp_count * held, dtype=jnp.int32)
    back_pick = (back_at[:, None] == back_ids[None, :]).astype(BF16)

    pack_order = lax.dynamic_slice(order, (my_micro, my_pack * pack_rows), (1, pack_rows))
    source = (pack_order // rows).reshape(tp_count, rows)
    from_each = (source[:, :, None] == jnp.arange(groups, dtype=jnp.int32)).astype(BF16)
    before = jnp.einsum(
        "qp,tqg->tpg", strict_up, from_each, preferred_element_type=F32
    )
    source_rank = jnp.sum(before * from_each.astype(F32), axis=2).astype(jnp.int32)
    arrive_at = source * (tp_count * share) + tp_id * share + source_rank
    pack_ids = jnp.arange(pack_rows, dtype=jnp.int32)
    arrive_pick = (arrive_at.reshape(pack_rows, 1) == pack_ids[None, :]).astype(BF16)
    return_at = lax.dynamic_slice(source * share + source_rank, (tp_place, 0), (1, rows))
    return_pick = (row_ids[:, None] == return_at).astype(BF16)

    def to_pack(values):
        sent = jnp.einsum("msi,mid->msd", send_pick, values, preferred_element_type=F32)
        sent = sent.astype(BF16).reshape(micros * rows, width)
        moved = lax.all_to_all(sent, GROUP, split_axis=0, concat_axis=0, tiled=True)
        return jnp.dot(arrive_pick, moved, preferred_element_type=F32).astype(BF16)

    def to_given(values, extra):
        sent = jnp.dot(return_pick, values.astype(BF16), preferred_element_type=F32).astype(BF16)
        sent = sent.reshape(groups, share, width)
        if extra is not None:
            sent = jnp.concatenate([sent, extra], axis=1)
        return lax.all_to_all(sent, GROUP, split_axis=0, concat_axis=0, tiled=True)

    def spread(values):
        full = lax.all_gather(values, "tp", axis=0, tiled=True)
        picked = jnp.dot(back_pick, full, preferred_element_type=F32).astype(BF16)
        return picked.reshape(micros, rows, width), full

    small = jnp.concatenate(
        [
            gain_in[None],
            gain_mid[None],
            query_conv.reshape(-1, own),
            key_conv.reshape(-1, own),
            value_conv.reshape(-1, own),
            jnp.pad(gain_head, (0, own - gain_head.shape[0]))[None],
        ],
        axis=0,
    )
    small = jnp.pad(small, ((0, LANES - 2 * heads - small.shape[0]), (0, 0)))
    mixer_weight = lax.all_gather(
        jnp.concatenate(
            [query_proj, key_proj, value_proj, gate_proj, alpha_proj, beta_proj, small.T], axis=1
        ),
        GROUP, axis=0, tiled=True,
    )
    x_low = to_pack(tokens)
    out_weight = lax.all_gather(out_proj.T, GROUP, axis=0, tiled=True)
    pair_weight = lax.all_gather(
        jnp.concatenate([ffn_gate, ffn_up], axis=1), GROUP, axis=0, tiled=True
    )
    down_weight = lax.all_gather(ffn_down.T, GROUP, axis=0, tiled=True)
    dy_low = to_pack(cotangent)

    tail_at = 2 * key_cols + 2 * value_cols
    extras = mixer_weight[:, tail_at:].T[2 * heads :].astype(F32)
    gain_in_full = extras[0:1]
    gain_mid_full = extras[1:2]

    def taps_of(start, weight):
        count = weight.size // own
        flat = extras[start : start + count].reshape(count, groups, own)
        flat = jnp.transpose(flat, (1, 0, 2)).reshape(groups, spans, heads, weight.shape[2])
        return jnp.transpose(flat, (1, 2, 0, 3)).reshape(spans, -1), start + count

    query_taps, at = taps_of(2, query_conv)
    key_taps, at = taps_of(at, key_conv)
    value_taps, at = taps_of(at, value_conv)
    taps = jnp.pad(
        jnp.concatenate([query_taps, key_taps, value_taps], axis=1), ((0, PAD - spans), (0, 0))
    )
    head_gain = extras[at].reshape(groups, own)[:, : gain_head.shape[0]].reshape(1, value_size)
    head_gain = jnp.broadcast_to(head_gain, (PAD, value_size))
    par = jnp.zeros((PAD, LANES), F32)
    par = par.at[0, :heads].set(-jnp.exp(decay_log)).at[1, :heads].set(step_bias)
    length_row = lax.dynamic_slice(
        lengths, (my_micro, my_pack, 0), (1, 1, lengths.shape[2])
    ).reshape(-1)
    info, seg_rows = place_arrays(length_row, pack_rows)

    x_float = x_low.astype(F32)
    rate_in = lax.rsqrt(jnp.mean(x_float * x_float, axis=1, keepdims=True) + square_eps)
    normed_in = (x_float * rate_in * gain_in_full).astype(BF16)
    proj = dot_nn(normed_in, mixer_weight)
    normed_low, *saved = delta_forward(proj, info, seg_rows, par, taps, head_gain, sizes)

    def my_rows(values):
        return lax.dynamic_slice(values, (tp_place * rows, 0), (rows, values.shape[1])).astype(F32)

    hidden_in = my_rows(x_low) + share_sum(dot_nt(normed_low, out_weight).astype(BF16))
    rate_mid = lax.rsqrt(jnp.mean(hidden_in * hidden_in, axis=1, keepdims=True) + square_eps)
    mid_low = lax.all_gather(
        (hidden_in * rate_mid * gain_mid_full).astype(BF16), "tp", axis=0, tiled=True
    )
    units = ffn_gate.shape[1]
    both = dot_nn(mid_low, pair_weight)
    gate_value, up_value = both[:, :units], both[:, units:]
    gate_sig = sigmoid(gate_value)
    gate_act = gate_value * gate_sig
    hidden_low = (gate_act * up_value).astype(BF16)
    grad_hidden = dot_nn(dy_low, down_weight)
    pair_grad = jnp.concatenate(
        [
            (grad_hidden * up_value * (gate_sig * (1.0 + gate_value * (1.0 - gate_sig)))).astype(BF16),
            (grad_hidden * gate_act).astype(BF16),
        ],
        axis=1,
    )
    mid_grad = share_sum(dot_nt(pair_grad, pair_weight).astype(BF16))
    ffn_part = dot_nt(hidden_low, down_weight).astype(BF16)

    scaled = mid_grad * gain_mid_full
    hidden_grad = (
        my_rows(dy_low)
        + rate_mid * scaled
        - rate_mid**3 * hidden_in * jnp.mean(hidden_in * scaled, axis=1, keepdims=True)
    )
    grad_mid_gain = jnp.sum(mid_grad * hidden_in * rate_mid, axis=0)
    mix_low = lax.all_gather(hidden_grad.astype(BF16), "tp", axis=0, tiled=True)
    mix_low, ffn_part = lax.optimization_barrier((mix_low, ffn_part))
    dnormed = dot_nn(mix_low, out_weight)
    grad_proj, conv_grad, head_gain_grad, decay_grads = delta_backward(
        proj, info, seg_rows, par, taps, head_gain, saved, dnormed, sizes
    )
    first_grad = share_sum(dot_nt(grad_proj, mixer_weight).astype(BF16))

    result = hidden_in + share_sum(ffn_part)
    result_back = to_given(result, None).reshape(rows, width)
    mixed, unused = spread(jnp.pad(result_back, ((0, PAD), (0, 0))))

    def owners(value, axis):
        return lax.psum_scatter(
            value.astype(BF16), GROUP, scatter_dimension=axis, tiled=True
        ).astype(F32)

    grad_pair = owners(dot_tn(mid_low, pair_grad), 0)
    grad_down = owners(dot_tn(dy_low, hidden_low), 0).T
    grad_out = owners(dot_tn(mix_low, normed_low), 0).T
    grad_mixer = owners(dot_tn(normed_in, grad_proj), 0)

    x_own = my_rows(x_low)
    rate_own = lax.rsqrt(jnp.mean(x_own * x_own, axis=1, keepdims=True) + square_eps)
    scaled_in = first_grad * gain_in_full
    token_grad = (
        hidden_grad
        + rate_own * scaled_in
        - rate_own**3 * x_own * jnp.mean(x_own * scaled_in, axis=1, keepdims=True)
    )
    grad_in_gain = jnp.sum(first_grad * x_own * rate_own, axis=0)

    conv_sum = jnp.sum(conv_grad.reshape(spans, PAD, -1), axis=1)

    def taps_to(value, size):
        parted = value.reshape(spans, heads, groups, size // groups)
        return jnp.transpose(parted, (2, 0, 1, 3)).reshape(groups, -1)

    gain_sum = jnp.sum(head_gain_grad.reshape(PAD * heads, value_size), axis=0)
    decay_sums = jnp.sum(decay_grads.reshape(2, PAD, LANES), axis=1)[:, :heads].reshape(1, -1)
    parts = [
        grad_in_gain.reshape(groups, own),
        grad_mid_gain.reshape(groups, own),
        gain_sum.reshape(groups, -1),
        taps_to(conv_sum[:, :key_cols], key_size),
        taps_to(conv_sum[:, key_cols : 2 * key_cols], key_size),
        taps_to(conv_sum[:, 2 * key_cols :], value_size),
        jnp.broadcast_to(decay_sums, (groups, decay_sums.shape[1])),
    ]
    lens = [part.shape[1] for part in parts]
    packed = jnp.concatenate(parts, axis=1)
    packed = jnp.pad(packed, ((0, 0), (0, width - packed.shape[1])))
    extra = jnp.pad(pair_rows(packed), ((0, 0), (0, PAD - 2), (0, 0)))
    came = to_given(token_grad, extra)
    summed = jnp.sum(came[:, share : share + 2].astype(F32), axis=(0, 1))
    block = jnp.concatenate(
        [
            came[:, :share].reshape(rows, width),
            jnp.pad(pair_rows(summed), ((0, PAD - 2), (0, 0))),
        ],
        axis=0,
    )
    grad_tokens, full = spread(block)
    tp_summed = jnp.sum(
        full.reshape(tp_count, held, width)[:, rows : rows + 2].astype(F32), axis=(0, 1)
    )
    pieces = []
    offset = 0
    for index, length in enumerate(lens):
        origin = tp_summed if index < 3 else summed
        pieces.append(origin[offset : offset + length])
        offset += length
    decay_pair = pieces[6].reshape(2, heads)
    edges = [0, key_cols, 2 * key_cols, 2 * key_cols + value_cols, tail_at]
    return (
        mixed,
        grad_tokens,
        pieces[0],
        grad_mixer[:, edges[0] : edges[1]],
        grad_mixer[:, edges[1] : edges[2]],
        grad_mixer[:, edges[2] : edges[3]],
        grad_mixer[:, edges[3] : edges[4]],
        grad_mixer[:, tail_at : tail_at + heads],
        grad_mixer[:, tail_at + heads : tail_at + 2 * heads],
        pieces[3].reshape(query_conv.shape),
        pieces[4].reshape(key_conv.shape),
        pieces[5].reshape(value_conv.shape),
        decay_pair[0],
        decay_pair[1],
        pieces[2],
        grad_out,
        pieces[1],
        grad_pair[:, :units],
        grad_pair[:, units:],
        grad_down,
    )


def solution(mesh):
    in_specs = (
        P(None, ("fsdp", "ctx"), None),
        P(None, ("fsdp", "ctx"), None),
        P(),
        P(),
        P(("fsdp", "ctx")),
        P(("fsdp", "ctx"), "tp"),
        P(("fsdp", "ctx"), "tp"),
        P(("fsdp", "ctx"), "tp"),
        P(("fsdp", "ctx"), "tp"),
        P(("fsdp", "ctx"), "tp"),
        P(("fsdp", "ctx"), "tp"),
        P(None, "tp", ("fsdp", "ctx")),
        P(None, "tp", ("fsdp", "ctx")),
        P(None, "tp", ("fsdp", "ctx")),
        P("tp"),
        P("tp"),
        P(("fsdp", "ctx")),
        P("tp", ("fsdp", "ctx")),
        P(("fsdp", "ctx")),
        P(("fsdp", "ctx"), "tp"),
        P(("fsdp", "ctx"), "tp"),
        P("tp", ("fsdp", "ctx")),
    )
    out_specs = (
        P(None, ("fsdp", "ctx"), None),
        P(None, ("fsdp", "ctx"), None),
        P(("fsdp", "ctx")),
        P(("fsdp", "ctx"), "tp"),
        P(("fsdp", "ctx"), "tp"),
        P(("fsdp", "ctx"), "tp"),
        P(("fsdp", "ctx"), "tp"),
        P(("fsdp", "ctx"), "tp"),
        P(("fsdp", "ctx"), "tp"),
        P(None, "tp", ("fsdp", "ctx")),
        P(None, "tp", ("fsdp", "ctx")),
        P(None, "tp", ("fsdp", "ctx")),
        P("tp"),
        P("tp"),
        P(("fsdp", "ctx")),
        P("tp", ("fsdp", "ctx")),
        P(("fsdp", "ctx")),
        P(("fsdp", "ctx"), "tp"),
        P(("fsdp", "ctx"), "tp"),
        P("tp", ("fsdp", "ctx")),
    )
    return jax.shard_map(
        per_device, mesh=mesh, in_specs=in_specs, out_specs=out_specs, check_vma=False
    )
```

```python
import functools
import jax
import jax.numpy as jnp
from jax import lax
from jax.sharding import PartitionSpec as P
from jax.experimental import pallas as pl
from jax.experimental.pallas import tpu as pltpu

CHUNK = 128
LANES = 128
PAD = 8
square_eps = 1e-05
unit_eps = 1e-06
F32 = jnp.float32
BF16 = jnp.bfloat16


def dot_nn(left, right):
    return lax.dot_general(left, right, (((1,), (0,)), ((), ())), preferred_element_type=F32)


def dot_nt(left, right):
    return lax.dot_general(left, right, (((1,), (1,)), ((), ())), preferred_element_type=F32)


def dot_tn(left, right):
    return lax.dot_general(left, right, (((0,), (0,)), ((), ())), preferred_element_type=F32)


def halves(value):
    high = value.astype(BF16)
    return high, (value - high.astype(F32)).astype(BF16)


def dot_fine(left, right):
    left_high, left_low = halves(left)
    right_high, right_low = halves(right)
    return (
        dot_nn(left_high, right_high)
        + dot_nn(left_high, right_low)
        + dot_nn(left_low, right_high)
    )


def sum_by(mask, value):
    high, rest = halves(value)
    middle, low = halves(value - high.astype(F32))
    return dot_nn(mask, high) + dot_nn(mask, middle) + dot_nn(mask, low)


def sigmoid(value):
    return 1.0 / (1.0 + jnp.exp(-value))


def softplus(value):
    return jnp.maximum(value, 0.0) + jnp.log1p(jnp.exp(-jnp.abs(value)))


def low_dot(left, right):
    return dot_nn(left.astype(BF16), right.astype(BF16))


def inverses_lower(lower_mats, row_id, col_id):
    size = row_id.shape[0]

    def level(width):
        same = row_id // (2 * width) == col_id // (2 * width)
        return same & ((row_id // width) % 2 == 1) & ((col_id // width) % 2 == 0)

    unit = jnp.where(row_id == col_id, 1.0, 0.0)
    mask = level(1)
    results = [unit - jnp.where(mask, mat, 0.0) for mat in lower_mats]
    width = 2
    while width < size:
        mask = level(width)
        parts = [low_dot(r, jnp.where(mask, mat, 0.0)) for r, mat in zip(results, lower_mats)]
        results = [r - low_dot(p, r) for p, r in zip(parts, results)]
        width *= 2
    rests = [unit - r - dot_fine(mat, r) for r, mat in zip(results, lower_mats)]
    return [r + low_dot(r, rest) for r, rest in zip(results, rests)]


def in_turn(bodies):
    asked = [next(body) for body in bodies]
    while asked:
        made = asked[0][0]([item[1] for item in asked]) if asked[0] else [None] * len(asked)
        following = []
        for body, value in zip(bodies, made):
            try:
                following.append(body.send(value))
            except StopIteration:
                pass
        asked = following


def chunk_basics(gates, par, info, seg_row, row_id, col_id, lane_id, head_count):
    step = gates + par[1:2, :]
    log_decay = jnp.where(lane_id < head_count, par[0:1, :] * softplus(step), 0.0)
    beta_raw = sigmoid(gates)
    valid = info[:, 1:2]
    lower = row_id >= col_id
    cumulative = sum_by(jnp.where(lower, 1.0, 0.0).astype(BF16), log_decay)
    both = jnp.where(lane_id < head_count, cumulative, beta_raw * valid)
    turned = jnp.transpose(both)
    inner = lower & (info[:, 0:1] == seg_row)
    return step, log_decay, beta_raw, both, turned, inner


def activations(ext, taps, masks, start, stop, rows):
    value = taps[3:4, start:stop] * ext[PAD : PAD + rows, start:stop]
    for distance in (1, 2, 3):
        shifted = ext[PAD - distance : PAD - distance + rows, start:stop]
        value = value + masks[distance - 1] * (taps[3 - distance : 4 - distance, start:stop] * shifted)
    return value


def forward_kernel(
    head_count, key_size, value_size,
    proj, info_ref, segr, par_ref, taps, gain_ref,
    normed_out, state_out, inverse_out, pseudo_out, output_out,
    state, ext,
):
    rows = proj.shape[0]
    width = head_count * (2 * key_size + value_size)
    gate_at = width
    tail_at = width + head_count * value_size

    @pl.when(pl.program_id(0) == 0)
    def start():
        state[...] = jnp.zeros_like(state)
        ext[0:PAD, :] = jnp.zeros((PAD, width), F32)

    ext[PAD : PAD + rows, :] = proj[:, 0:width]
    info = info_ref[...]
    row_id = lax.broadcasted_iota(jnp.int32, (rows, rows), 0)
    col_id = lax.broadcasted_iota(jnp.int32, (rows, rows), 1)
    lane_id = lax.broadcasted_iota(jnp.int32, (rows, LANES), 1)
    masks = tuple(info[:, 1 + d : 2 + d] for d in (1, 2, 3))
    valid = info[:, 1:2]
    unused, log_decay, beta_raw, both, turned, inner = chunk_basics(
        proj[:, tail_at : tail_at + LANES], par_ref[...], info, segr[0:1, :],
        row_id, col_id, lane_id, head_count,
    )
    carried_mask = info[:, 8:9]
    tail_mask = info[:, 9:10]
    strict = row_id > col_id
    key_at = head_count * key_size
    value_at = 2 * key_at
    def one_head(head):
        ks = key_size
        vs = value_size
        act_q = activations(ext, taps, masks, head * ks, (head + 1) * ks, rows)
        act_k = activations(ext, taps, masks, key_at + head * ks, key_at + (head + 1) * ks, rows)
        act_v = activations(ext, taps, masks, value_at + head * vs, value_at + (head + 1) * vs, rows)
        cq = act_q * sigmoid(act_q)
        ck = act_k * sigmoid(act_k)
        values = act_v * sigmoid(act_v)
        query = cq * (lax.rsqrt(jnp.sum(cq * cq, axis=1, keepdims=True) + unit_eps) * ks ** -0.5)
        key = ck * lax.rsqrt(jnp.sum(ck * ck, axis=1, keepdims=True) + unit_eps)
        yield
        qb = query.astype(BF16)
        kb = key.astype(BF16)
        cum = both[:, head : head + 1]
        beta = both[:, head_count + head : head_count + head + 1]
        cum_row = turned[head : head + 1, :]
        beta_row = turned[head_count + head : head_count + head + 1, :]
        decays = jnp.where(inner, jnp.exp(jnp.minimum(cum - cum_row, 0.0)), 0.0)
        lower_mat = jnp.where(strict, decays * dot_nt(kb, kb) * beta_row, 0.0)
        inverse = yield (lambda mats: inverses_lower(mats, row_id, col_id)), lower_mat
        yield
        carried = jnp.exp(cum) * carried_mask
        last = cum[rows - 1 : rows, :]
        tail = jnp.exp(last - cum) * tail_mask
        keep = carried[rows - 1 : rows, :]
        before = state[head]
        state_out[0, head] = before
        sb = before.astype(BF16)
        target = values - carried * dot_nn(kb, sb)
        ib = inverse.astype(BF16)
        pseudo = dot_nn(ib, target.astype(BF16))
        inverse_out[0, head] = ib
        pseudo_out[:, head * vs : (head + 1) * vs] = pseudo
        yield
        weighted = beta * pseudo
        mix = decays * dot_nt(qb, kb)
        output = carried * dot_nn(qb, sb) + dot_nn(mix.astype(BF16), weighted.astype(BF16))
        output_out[:, head * vs : (head + 1) * vs] = output
        state[head] = keep * before + dot_tn(kb, (tail * weighted).astype(BF16))
        yield
        gate = proj[:, gate_at + head * vs : gate_at + (head + 1) * vs]
        scale = lax.rsqrt(jnp.mean(output * output, axis=1, keepdims=True) + square_eps)
        normed = output * scale * gain_ref[0:1, :] * (gate * sigmoid(gate)) * valid
        normed_out[:, head * vs : (head + 1) * vs] = normed.astype(BF16)

    in_turn([one_head(head) for head in range(head_count)])
    ext[0:PAD, :] = ext[rows : rows + PAD, :]


def backward_kernel(
    head_count, key_size, value_size,
    proj, prior, info_ref, segr, par_ref, taps, gain_ref,
    state_in, inverse_in, pseudo_in, output_in, dnormed,
    grad_out, conv_out, gain_out, small_out,
    dstate, ext, dext,
):
    rows = proj.shape[0]
    width = head_count * (2 * key_size + value_size)
    gate_at = width
    tail_at = width + head_count * value_size
    place = pl.program_id(0)
    count = pl.num_programs(0)

    @pl.when(place == 0)
    def start():
        dstate[...] = jnp.zeros_like(dstate)
        dext[rows : rows + PAD, :] = jnp.zeros((PAD, width), F32)
        conv_out[...] = jnp.zeros_like(conv_out)
        gain_out[...] = jnp.zeros_like(gain_out)
        small_out[...] = jnp.zeros_like(small_out)

    first = place == count - 1
    ext[0:PAD, :] = jnp.where(first, 0.0, prior[:, 0:width])
    ext[PAD : PAD + rows, :] = proj[:, 0:width]
    info = info_ref[...]
    row_id = lax.broadcasted_iota(jnp.int32, (rows, rows), 0)
    col_id = lax.broadcasted_iota(jnp.int32, (rows, rows), 1)
    lane_id = lax.broadcasted_iota(jnp.int32, (rows, LANES), 1)
    masks = tuple(info[:, 1 + d : 2 + d] for d in (1, 2, 3))
    later = tuple(info[:, 4 + d : 5 + d] for d in (1, 2, 3))
    valid = info[:, 1:2]
    step, log_decay, beta_raw, both, turned, inner = chunk_basics(
        proj[:, tail_at : tail_at + LANES], par_ref[...], info, segr[0:1, :],
        row_id, col_id, lane_id, head_count,
    )
    carried_mask = info[:, 8:9]
    tail_mask = info[:, 9:10]
    strict = row_id > col_id
    last_row = lax.broadcasted_iota(jnp.int32, (rows, 1), 0) == rows - 1
    row_of = lax.broadcasted_iota(jnp.int32, (LANES, rows), 0)
    ks = key_size
    vs = value_size
    key_at = head_count * ks
    value_at = 2 * key_at
    sums = {}

    def fold(value):
        return jnp.sum(value.reshape(rows // PAD, PAD, value.shape[1]), axis=0)

    def conv_back(da, start, stop):
        dext[0:rows, start:stop] = da
        back = taps[3:4, start:stop] * da
        conv_out[3 * PAD : 4 * PAD, start:stop] += fold(da * ext[PAD : PAD + rows, start:stop])
        for d in (1, 2, 3):
            back = back + later[d - 1] * (taps[3 - d : 4 - d, start:stop] * dext[d : d + rows, start:stop])
            shifted = ext[PAD - d : PAD - d + rows, start:stop]
            conv_out[(3 - d) * PAD : (4 - d) * PAD, start:stop] += fold(masks[d - 1] * da * shifted)
        grad_out[:, start:stop] = back.astype(BF16)

    def one_head(head):
        act_q = activations(ext, taps, masks, head * ks, (head + 1) * ks, rows)
        act_k = activations(ext, taps, masks, key_at + head * ks, key_at + (head + 1) * ks, rows)
        act_v = activations(ext, taps, masks, value_at + head * vs, value_at + (head + 1) * vs, rows)
        sig_q, sig_k, sig_v = sigmoid(act_q), sigmoid(act_k), sigmoid(act_v)
        cq, ck, values = act_q * sig_q, act_k * sig_k, act_v * sig_v
        rate_q = lax.rsqrt(jnp.sum(cq * cq, axis=1, keepdims=True) + unit_eps)
        rate_k = lax.rsqrt(jnp.sum(ck * ck, axis=1, keepdims=True) + unit_eps)
        unit_q = cq * rate_q
        query = unit_q * ks ** -0.5
        key = ck * rate_k
        yield
        qb = query.astype(BF16)
        kb = key.astype(BF16)
        cum = both[:, head : head + 1]
        beta = both[:, head_count + head : head_count + head + 1]
        cum_row = turned[head : head + 1, :]
        beta_row = turned[head_count + head : head_count + head + 1, :]
        decays = jnp.where(inner, jnp.exp(jnp.minimum(cum - cum_row, 0.0)), 0.0)
        carried = jnp.exp(cum) * carried_mask
        tail = jnp.exp(cum[rows - 1 : rows, :] - cum) * tail_mask
        keep = carried[rows - 1 : rows, :]
        yield
        before = state_in[0, head]
        sb = before.astype(BF16)
        ib = inverse_in[0, head]
        pseudo = pseudo_in[:, head * vs : (head + 1) * vs]
        output = output_in[:, head * vs : (head + 1) * vs]
        gate = proj[:, gate_at + head * vs : gate_at + (head + 1) * vs]
        given = dnormed[:, head * vs : (head + 1) * vs] * valid
        gain = gain_ref[0:1, :]
        scale = lax.rsqrt(jnp.mean(output * output, axis=1, keepdims=True) + square_eps)
        unit_o = output * scale
        sig_g = sigmoid(gate)
        silu_g = gate * sig_g
        dunit = given * gain * silu_g
        doutput = scale * (dunit - unit_o * jnp.mean(unit_o * dunit, axis=1, keepdims=True))
        dgate = given * unit_o * gain * (sig_g * (1.0 + gate * (1.0 - sig_g)))
        gain_out[:, head * vs : (head + 1) * vs] += fold(given * unit_o * silu_g)
        grad_out[:, gate_at + head * vs : gate_at + (head + 1) * vs] = dgate.astype(BF16)
        yield
        dob = doutput.astype(BF16)
        weighted = beta * pseudo
        wb = weighted.astype(BF16)
        gram = dot_nt(kb, kb)
        cross = dot_nt(qb, kb)
        mix = decays * cross
        yield
        after = dstate[head]
        ab = after.astype(BF16)
        from_state = dot_nn(kb, ab)
        dweighted = dot_tn(mix.astype(BF16), dob) + tail * from_state
        dbeta = jnp.sum(dweighted * pseudo, axis=1, keepdims=True)
        yield
        dtarget = dot_tn(ib, (beta * dweighted).astype(BF16))
        dtb = dtarget.astype(BF16)
        read = dot_nn(kb, sb)
        yield
        dcarried = jnp.sum(doutput * dot_nn(qb, sb), axis=1, keepdims=True) - jnp.sum(
            dtarget * read, axis=1, keepdims=True
        )
        dtail = jnp.sum(weighted * from_state, axis=1, keepdims=True)
        dkeep = jnp.sum(jnp.sum(after * before, axis=1, keepdims=True), axis=0, keepdims=True)
        cdo = (carried * doutput).astype(BF16)
        cdt = (carried * dtarget).astype(BF16)
        dstate[head] = keep * after + dot_tn(qb, cdo) - dot_tn(kb, cdt)
        yield
        dmix = dot_nt(dob, wb)
        dcross = (dmix * decays).astype(BF16)
        dlower = jnp.where(strict, -dot_nt(dtb, pseudo.astype(BF16)), 0.0) * decays
        dgram = (dlower * beta_row).astype(BF16)
        plain = dlower * gram
        inner_grad = dmix * mix + plain * beta_row
        yield
        dquery = dot_nt(cdo, sb) + dot_nn(dcross, kb)
        dkey = (
            dot_tn(dcross, qb)
            + dot_nn(dgram, kb)
            + dot_tn(dgram, kb)
            + dot_nt((tail * weighted).astype(BF16), ab)
            - dot_nt(cdt, sb)
        )
        yield
        dlast = jnp.sum(dtail * tail, axis=0, keepdims=True) + dkeep * keep
        dcum_col = (
            jnp.sum(inner_grad, axis=1, keepdims=True)
            + dcarried * carried
            - dtail * tail
            + jnp.where(last_row, dlast, 0.0)
        )
        sums[head] = (
            dcum_col,
            dbeta,
            -jnp.sum(inner_grad, axis=0, keepdims=True),
            jnp.sum(plain, axis=0, keepdims=True),
        )
        yield
        dq_scaled = dquery * ks ** -0.5
        dcq = (dq_scaled - unit_q * jnp.sum(unit_q * dq_scaled, axis=1, keepdims=True)) * rate_q
        dck = (dkey - key * jnp.sum(key * dkey, axis=1, keepdims=True)) * rate_k
        conv_back(dcq * (sig_q * (1.0 + act_q * (1.0 - sig_q))), head * ks, (head + 1) * ks)
        yield
        conv_back(
            dck * (sig_k * (1.0 + act_k * (1.0 - sig_k))), key_at + head * ks, key_at + (head + 1) * ks
        )
        conv_back(
            dtarget * (sig_v * (1.0 + act_v * (1.0 - sig_v))),
            value_at + head * vs,
            value_at + (head + 1) * vs,
        )

    for head in range(head_count):
        in_turn([one_head(head)])
    dcum = jnp.zeros((rows, LANES), F32)
    dturned = jnp.zeros((LANES, rows), F32)
    for head, (dcum_col, dbeta, dcum_row, dbeta_row) in sums.items():
        dcum = jnp.where(lane_id == head, dcum_col, dcum)
        dcum = jnp.where(lane_id == head_count + head, dbeta, dcum)
        dturned = jnp.where(row_of == head, dcum_row, dturned)
        dturned = jnp.where(row_of == head_count + head, dbeta_row, dturned)
    dboth = dcum + jnp.transpose(dturned)
    upper = jnp.where(row_id <= col_id, 1.0, 0.0).astype(BF16)
    dlog = sum_by(upper, jnp.where(lane_id < head_count, dboth, 0.0))
    dalpha = dlog * par_ref[0:1, :] * sigmoid(step)
    dbeta_raw = dboth * valid * beta_raw * (1.0 - beta_raw)
    tail_grad = jnp.where(
        lane_id < head_count, dalpha, jnp.where(lane_id < 2 * head_count, dbeta_raw, 0.0)
    )
    grad_out[:, tail_at : tail_at + LANES] = tail_grad.astype(BF16)
    small_out[0:PAD, :] += fold(dlog * log_decay)
    small_out[PAD : 2 * PAD, :] += fold(jnp.where(lane_id < head_count, dalpha, 0.0))
    dext[rows : rows + PAD, :] = dext[0:PAD, :]


def delta_forward(proj, info, seg_rows, par, taps, gain, sizes):
    head_count, key_size, value_size = sizes
    total, columns = proj.shape
    steps = total // CHUNK
    width = head_count * (2 * key_size + value_size)
    span = head_count * value_size
    whole = lambda a: pl.BlockSpec(a.shape, lambda i: (0, 0))
    by_rows = lambda n: pl.BlockSpec((CHUNK, n), lambda i: (i, 0))
    return pl.pallas_call(
        functools.partial(forward_kernel, head_count, key_size, value_size),
        grid=(steps,),
        in_specs=[
            by_rows(columns),
            by_rows(LANES),
            pl.BlockSpec((PAD, CHUNK), lambda i: (0, i)),
            whole(par),
            whole(taps),
            whole(gain),
        ],
        out_specs=[
            by_rows(span),
            pl.BlockSpec((1, head_count, key_size, value_size), lambda i: (i, 0, 0, 0)),
            pl.BlockSpec((1, head_count, CHUNK, CHUNK), lambda i: (i, 0, 0, 0)),
            by_rows(span),
            by_rows(span),
        ],
        out_shape=[
            jax.ShapeDtypeStruct((total, span), BF16),
            jax.ShapeDtypeStruct((steps, head_count, key_size, value_size), F32),
            jax.ShapeDtypeStruct((steps, head_count, CHUNK, CHUNK), BF16),
            jax.ShapeDtypeStruct((total, span), F32),
            jax.ShapeDtypeStruct((total, span), F32),
        ],
        scratch_shapes=[
            pltpu.VMEM((head_count, key_size, value_size), F32),
            pltpu.VMEM((CHUNK + PAD, width), F32),
        ],
        compiler_params=pltpu.CompilerParams(vmem_limit_bytes=48 * 1024 * 1024),
        name="delta_forward",
    )(proj, info, seg_rows, par, taps, gain)


def delta_backward(proj, info, seg_rows, par, taps, gain, saved, dnormed, sizes):
    head_count, key_size, value_size = sizes
    total, columns = proj.shape
    steps = total // CHUNK
    width = head_count * (2 * key_size + value_size)
    span = head_count * value_size
    states, inverses, pseudos, outputs = saved
    blocks = CHUNK // PAD
    turn = lambda i: steps - 1 - i
    whole = lambda a: pl.BlockSpec(a.shape, lambda i: (0, 0))
    by_rows = lambda n: pl.BlockSpec((CHUNK, n), lambda i: (turn(i), 0))
    return pl.pallas_call(
        functools.partial(backward_kernel, head_count, key_size, value_size),
        grid=(steps,),
        in_specs=[
            by_rows(columns),
            pl.BlockSpec((PAD, columns), lambda i: (jnp.maximum(turn(i) * blocks - 1, 0), 0)),
            by_rows(LANES),
            pl.BlockSpec((PAD, CHUNK), lambda i: (0, turn(i))),
            whole(par),
            whole(taps),
            whole(gain),
            pl.BlockSpec((1, head_count, key_size, value_size), lambda i: (turn(i), 0, 0, 0)),
            pl.BlockSpec((1, head_count, CHUNK, CHUNK), lambda i: (turn(i), 0, 0, 0)),
            by_rows(span),
            by_rows(span),
            by_rows(span),
        ],
        out_specs=[
            by_rows(columns),
            pl.BlockSpec((4 * PAD, width), lambda i: (0, 0)),
            pl.BlockSpec((PAD, span), lambda i: (0, 0)),
            pl.BlockSpec((2 * PAD, LANES), lambda i: (0, 0)),
        ],
        out_shape=[
            jax.ShapeDtypeStruct((total, columns), BF16),
            jax.ShapeDtypeStruct((4 * PAD, width), F32),
            jax.ShapeDtypeStruct((PAD, span), F32),
            jax.ShapeDtypeStruct((2 * PAD, LANES), F32),
        ],
        scratch_shapes=[
            pltpu.VMEM((head_count, key_size, value_size), F32),
            pltpu.VMEM((CHUNK + PAD, width), F32),
            pltpu.VMEM((CHUNK + PAD, width), F32),
        ],
        compiler_params=pltpu.CompilerParams(vmem_limit_bytes=48 * 1024 * 1024),
        name="delta_backward",
    )(proj, proj, info, seg_rows, par, taps, gain, states, inverses, pseudos, outputs, dnormed)


def middle_kernel(place, own, after, before, x_ref, gain, hidden_out, normed_out):
    mixer = own[...].astype(F32) + after[...].astype(F32) + before[...].astype(F32)
    hidden = mixer + x_ref[...].astype(F32)
    rate = lax.rsqrt(jnp.mean(hidden * hidden, axis=1, keepdims=True) + square_eps)
    hidden_out[...] = hidden
    normed_out[...] = (hidden * rate * gain[0:1, :]).astype(BF16)


def norm_back(grad, value, gain):
    rate = lax.rsqrt(jnp.mean(value * value, axis=1, keepdims=True) + square_eps)
    scaled = grad * gain
    inner = jnp.mean(value * scaled, axis=1, keepdims=True)
    return rate * scaled - rate * rate * rate * value * inner, grad * value * rate


def rows_summed(value):
    return jnp.sum(value.reshape(value.shape[0] // PAD, PAD, value.shape[1]), axis=0)


def middle_back_kernel(place, moved, hidden, dy_ref, gain, grad_out, low_out, gain_out):
    @pl.when(pl.program_id(0) == 0)
    def start():
        gain_out[...] = jnp.zeros_like(gain_out)

    back, part = norm_back(moved[...].astype(F32), hidden[...], gain[0:1, :])
    grad = dy_ref[...].astype(F32) + back
    grad_out[...] = grad
    low_out[...] = grad.astype(BF16)
    gain_out[...] += rows_summed(part)


def first_back_kernel(place, moved, after, x_ref, gain, grad_out, gain_out):
    @pl.when(pl.program_id(0) == 0)
    def start():
        gain_out[...] = jnp.zeros_like(gain_out)

    back, part = norm_back(moved[...].astype(F32), x_ref[...].astype(F32), gain[0:1, :])
    grad_out[...] = (after[...] + back).astype(BF16)
    gain_out[...] += rows_summed(part)


def row_parts(kernel, place, arrays, outs, rows):
    part = 48 if rows % 48 == 0 else rows
    steps = rows // part

    def spec(kind, shape):
        if kind == "own":
            return pl.BlockSpec((part, shape[1]), lambda i, p: (i, 0))
        if kind == "all":
            return pl.BlockSpec((part, shape[1]), lambda i, p: (p[0] * steps + i, 0))
        return pl.BlockSpec(shape, lambda i, p: (0, 0))

    return pl.pallas_call(
        kernel,
        grid_spec=pltpu.PrefetchScalarGridSpec(
            num_scalar_prefetch=1,
            grid=(steps,),
            in_specs=[spec(kind, value.shape) for kind, value in arrays],
            out_specs=[spec(kind, value.shape) for kind, value in outs],
        ),
        out_shape=[value for kind, value in outs],
        compiler_params=pltpu.CompilerParams(vmem_limit_bytes=40 * 1024 * 1024),
        name=kernel.__name__,
    )(place, *[value for kind, value in arrays])


def place_arrays(length_row, total):
    places = jnp.arange(total, dtype=jnp.int32)
    ids = jnp.arange(length_row.shape[0])
    ends = jnp.sum(jnp.where(ids[None, :] <= ids[:, None], length_row[None, :], 0), axis=1)
    starts = ends - length_row

    def seg_at(at):
        return jnp.sum((at[:, None] >= starts[None, :]).astype(jnp.int32), axis=1) - 1

    segment = seg_at(places)
    valid = (places < ends[-1]).astype(F32)
    lanes = [segment.astype(F32), valid]
    for d in (1, 2, 3):
        lanes.append((seg_at(places - d) == segment).astype(F32))
    for d in (1, 2, 3):
        lanes.append(((seg_at(places + d) == segment) & (places + d < total)).astype(F32))
    head_place = places - places % CHUNK
    lanes.append(((seg_at(head_place - 1) == segment) & (head_place > 0)).astype(F32))
    lanes.append((seg_at(head_place + CHUNK - 1) == segment).astype(F32))
    info = jnp.stack(lanes, axis=1)
    info = jnp.pad(info, ((0, 0), (0, LANES - len(lanes))))
    rows = jnp.broadcast_to(segment.astype(F32)[None, :], (PAD, total))
    return info, rows


GROUP = ("fsdp", "ctx")


def pair_rows(values):
    high, low = halves(values)
    return jnp.stack([high, low], axis=-2)


SC_SUM = "bn"
SC_COPY = ""


def deal(part, name=""):
    if name and name in SC_SUM:
        return lax.psum_scatter(part, "tp", scatter_dimension=0, tiled=True)
    return lax.all_to_all(part, "tp", split_axis=0, concat_axis=0, tiled=True)


def add_dealt(moved, name=""):
    if name and name in SC_SUM:
        return moved.astype(F32)
    count = lax.axis_size("tp")
    return jnp.sum(moved.reshape(count, -1, moved.shape[1]).astype(F32), axis=0)


def copy_rows(own, name=""):
    if name and name in SC_COPY:
        return lax.all_gather(own, "tp", axis=0, tiled=True)
    return deal(jnp.concatenate([own] * lax.axis_size("tp"), axis=0))


def relay_send(value, route):
    return lax.ppermute(value, "tp", route)


def relay_first(own):
    return relay_send(own, [(0, 1), (1, 2), (2, 3)]), relay_send(own, [(1, 0), (2, 1), (3, 2)])


def relay_second(before, after):
    place = lax.axis_index("tp")
    before_2 = relay_send(before, [(1, 2), (2, 3)])
    after_2 = relay_send(after, [(2, 1), (1, 0)])
    far = relay_send(jnp.where(place == 1, before, after), [(1, 3), (2, 0)])
    return before_2, after_2, far


def relayed_blocks(own):
    before, after = relay_first(own)
    return (own, before, after, *relay_second(before, after))


def sum_rows_relayed(part, rows, along):
    place = lax.axis_index("tp")

    def block(index):
        return lax.dynamic_slice(part, (jnp.clip(index, 0, 3) * rows, 0), (rows, part.shape[1]))

    from_after = relay_send(block(place - 2), [(2, 1), (3, 2)])
    from_before = relay_send(block(place + 2), [(1, 2), (0, 1)])
    far = relay_send(block(jnp.where(place == 3, 0, 3)), [(3, 1), (0, 2)])
    from_after, from_before, far, along = together((from_after, from_before, far, along))
    far = far.astype(F32)
    to_before = (
        block(place - 1).astype(F32) + from_after.astype(F32) + jnp.where(place == 1, far, 0.0)
    )
    to_after = (
        block(place + 1).astype(F32) + from_before.astype(F32) + jnp.where(place == 2, far, 0.0)
    )
    return (
        relay_send(to_before.astype(BF16), [(1, 0), (2, 1), (3, 2)]),
        relay_send(to_after.astype(BF16), [(0, 1), (1, 2), (2, 3)]),
        along,
    )


def copy_rows_ordered(own):
    place = lax.axis_index("tp")
    own, before, after, before_2, after_2, far = relayed_blocks(own)
    parts = []
    for source in range(4):
        part = own
        for apart, block in ((-1, before), (1, after), (-2, before_2), (2, after_2)):
            if 0 <= source - apart < 4:
                part = jnp.where(source - place == apart, block, part)
        if source in (0, 3):
            part = jnp.where(jnp.abs(source - place) == 3, far, part)
        parts.append(part)
    return jnp.concatenate(parts, axis=0)


def relayed_block(place, source):
    apart = source - place
    near = jnp.where(apart == 0, 0, jnp.where(apart == -1, 1, 2))
    return jnp.where(jnp.abs(apart) == 3, 5, jnp.where(apart == -2, 3, jnp.where(apart == 2, 4, near)))


RELAYED = 6


def copy_rows_turned(own):
    count = lax.axis_size("tp")
    blocks = [own]
    for turn in range(1, count):
        blocks.append(lax.ppermute(own, "tp", [(i, (i + turn) % count) for i in range(count)]))
    return jnp.concatenate(blocks, axis=0)


together = lax.optimization_barrier


def per_device(
    tokens, cotangent, lengths, order, gain_in, query_proj, key_proj, value_proj, gate_proj,
    alpha_proj, beta_proj, query_conv, key_conv, value_conv, decay_log, step_bias, gain_head,
    out_proj, gain_mid, ffn_gate, ffn_up, ffn_down,
):
    groups = lax.axis_size(GROUP)
    tp_count = lax.axis_size("tp")
    tp_place = lax.axis_index("tp")
    group = lax.axis_index(GROUP)
    micros, rows, width = tokens.shape
    packs = lengths.shape[1]
    all_rows = order.shape[1]
    pack_rows = all_rows // packs
    assert micros * packs == groups and pack_rows == tp_count * rows and tp_count == 4
    share = rows // groups
    heads = decay_log.shape[0]
    spans = query_conv.shape[0]
    key_size = query_conv.shape[2] * groups
    value_size = value_conv.shape[2] * groups
    sizes = (heads, key_size, value_size)
    key_cols = heads * key_size
    value_cols = heads * value_size
    own = width // groups
    my_micro = group // packs
    my_pack = group % packs

    strict_up = jnp.triu(jnp.ones((rows, rows), BF16), 1)
    mine = (order // rows == group).reshape(micros * packs * tp_count, rows)
    rank = jnp.dot(mine.astype(BF16), strict_up, preferred_element_type=F32).astype(jnp.int32)
    rank = rank.reshape(micros, packs, tp_count, rows)
    ids = jnp.arange(packs * tp_count, dtype=jnp.int32).reshape(packs, tp_count, 1)
    send_slot = (ids * share + rank).reshape(micros, 1, all_rows)
    held = rows + PAD
    pack_id = jnp.arange(groups, dtype=jnp.int32).reshape(micros, packs, 1, 1)
    tp_id = jnp.arange(tp_count, dtype=jnp.int32).reshape(tp_count, 1)
    back_slot = (relayed_block(tp_place, tp_id) * held + pack_id * share + rank).reshape(micros, 1, all_rows)
    local = group * rows + jnp.arange(rows, dtype=jnp.int32)
    hit = order[:, None, :] == local[None, :, None]
    send_at = jnp.sum(jnp.where(hit, send_slot, 0), axis=2)
    back_at = jnp.sum(jnp.where(hit, back_slot, 0), axis=2).reshape(micros * rows)
    row_ids = jnp.arange(rows, dtype=jnp.int32)
    send_row = send_at // (share * tp_count) * share + send_at % share
    send_ids = jnp.arange(packs * share, dtype=jnp.int32)[None, :, None]
    sent_here = send_at // share % tp_count == tp_place
    part_pick = ((send_ids == send_row[:, None, :]) & sent_here[:, None, :]).astype(BF16)
    send_pick = (row_ids[None, :, None] == send_at[:, None, :]).astype(BF16)
    back_ids = jnp.arange(RELAYED * held, dtype=jnp.int32)
    back_pick = (back_at[:, None] == back_ids[None, :]).astype(BF16)

    pack_order = lax.dynamic_slice(order, (my_micro, my_pack * pack_rows), (1, pack_rows))
    source = (pack_order // rows).reshape(tp_count, rows)
    from_each = (source[:, :, None] == jnp.arange(groups, dtype=jnp.int32)).astype(BF16)
    before = jnp.einsum(
        "qp,tqg->tpg", strict_up, from_each, preferred_element_type=F32
    )
    source_rank = jnp.sum(before * from_each.astype(F32), axis=2).astype(jnp.int32)
    arrive_at = source * (tp_count * share) + tp_id * share + source_rank
    pack_ids = jnp.arange(pack_rows, dtype=jnp.int32)
    arrive_pick = (arrive_at.reshape(pack_rows, 1) == pack_ids[None, :]).astype(BF16)
    part_at = (tp_place - tp_id) % tp_count * rows + source * share + source_rank
    place_pick = (part_at.reshape(pack_rows, 1) == pack_ids[None, :]).astype(BF16)
    return_at = lax.dynamic_slice(source * share + source_rank, (tp_place, 0), (1, rows))
    return_pick = (row_ids[:, None] == return_at).astype(BF16)

    def picked(pick, values):
        return jnp.einsum("msi,mid->msd", pick, values, preferred_element_type=F32).astype(BF16)

    def exchange(sent):
        return lax.all_to_all(sent, GROUP, split_axis=0, concat_axis=0, tiled=True)

    def to_sources(values):
        sent = jnp.dot(return_pick, values, preferred_element_type=F32).astype(BF16)
        return sent.reshape(groups, share, width)

    def to_given(blocks):
        full = jnp.concatenate(blocks, axis=0)
        values = jnp.dot(back_pick, full, preferred_element_type=F32).astype(BF16)
        return values.reshape(micros, rows, width), full

    small = jnp.concatenate(
        [
            gain_in,
            gain_mid,
            query_conv.reshape(-1),
            key_conv.reshape(-1),
            value_conv.reshape(-1),
            gain_head,
        ],
        axis=0,
    )
    small_size = small.shape[0]
    small = jnp.pad(small, (0, width - small_size))
    gates_pad = jnp.zeros((own, LANES - 2 * heads), BF16)
    mixer_weight = lax.all_gather(
        jnp.concatenate(
            [query_proj, key_proj, value_proj, gate_proj, alpha_proj, beta_proj, gates_pad], axis=1
        ),
        GROUP, axis=0, tiled=True,
    )
    dy_sent = jnp.concatenate(
        [
            picked(part_pick, cotangent).reshape(groups, share, width),
            jnp.broadcast_to(small[None, None, :], (groups, PAD, width)),
        ],
        axis=1,
    )
    x_sent = picked(send_pick, tokens).reshape(pack_rows, width)
    x_moved, dy_sent = together((exchange(x_sent), dy_sent))
    x_low = jnp.dot(arrive_pick, x_moved, preferred_element_type=F32).astype(BF16)
    dy_moved = exchange(dy_sent)
    extras = dy_moved[:, share, :small_size].astype(F32)
    dy_own = dy_moved[:, :share].reshape(rows, width)
    out_weight = lax.all_gather(out_proj.T, GROUP, axis=0, tiled=True)
    down_weight = lax.all_gather(ffn_down.T, GROUP, axis=0, tiled=True)
    pair_shard = jnp.concatenate([ffn_gate, ffn_up], axis=1)

    tail_at = 2 * key_cols + 2 * value_cols
    gain_in_full = extras[:, :own].reshape(1, width)
    gain_mid_full = extras[:, own : 2 * own].reshape(1, width)

    def taps_of(start, weight):
        flat = extras[:, start : start + weight.size]
        flat = flat.reshape(groups, spans, heads, weight.shape[2])
        return jnp.transpose(flat, (1, 2, 0, 3)).reshape(spans, -1), start + weight.size

    query_taps, at = taps_of(2 * own, query_conv)
    key_taps, at = taps_of(at, key_conv)
    value_taps, at = taps_of(at, value_conv)
    taps = jnp.pad(
        jnp.concatenate([query_taps, key_taps, value_taps], axis=1), ((0, PAD - spans), (0, 0))
    )
    head_gain = jnp.broadcast_to(extras[:, at:].reshape(1, value_size), (PAD, value_size))
    par = jnp.zeros((PAD, LANES), F32)
    par = par.at[0, :heads].set(-jnp.exp(decay_log)).at[1, :heads].set(step_bias)
    length_row = lax.dynamic_slice(
        lengths, (my_micro, my_pack, 0), (1, 1, lengths.shape[2])
    ).reshape(-1)
    info, seg_rows = place_arrays(length_row, pack_rows)

    x_float = x_low.astype(F32)
    rate_in = lax.rsqrt(jnp.mean(x_float * x_float, axis=1, keepdims=True) + square_eps)
    normed_in = (x_float * rate_in * gain_in_full).astype(BF16)
    proj = dot_nn(normed_in, mixer_weight)
    dy_all = copy_rows_turned(together((dy_own, mixer_weight))[0])
    normed_low, *saved = delta_forward(proj, info, seg_rows, par, taps, head_gain, sizes)

    mixed_part = dot_nt(normed_low, out_weight).astype(BF16)
    from_after, from_before, dy_all = sum_rows_relayed(mixed_part, rows, dy_all)
    pair_weight = lax.all_gather(pair_shard, GROUP, axis=0, tiled=True)
    dy_low = jnp.dot(place_pick, dy_all, preferred_element_type=F32).astype(BF16)
    own_f32 = jax.ShapeDtypeStruct((rows, width), F32)
    own_low = jax.ShapeDtypeStruct((rows, width), BF16)
    gain_part = jax.ShapeDtypeStruct((PAD, width), F32)
    place = tp_place.reshape(1)
    gain_in_8 = jnp.broadcast_to(gain_in_full, (PAD, width))
    gain_mid_8 = jnp.broadcast_to(gain_mid_full, (PAD, width))
    hidden_in, mid_own = row_parts(
        middle_kernel,
        place,
        [
            ("all", mixed_part),
            ("own", from_after),
            ("own", from_before),
            ("all", x_low),
            ("one", gain_mid_8),
        ],
        [("own", own_f32), ("own", own_low)],
        rows,
    )
    mid_low = copy_rows_ordered(mid_own)
    grad_hidden = dot_nn(dy_low, down_weight)
    mid_low, grad_hidden = together((mid_low, grad_hidden))
    units = ffn_gate.shape[1]
    both = dot_nn(mid_low, pair_weight)
    gate_value, up_value = both[:, :units], both[:, units:]
    gate_sig = sigmoid(gate_value)
    gate_act = gate_value * gate_sig
    hidden_low = (gate_act * up_value).astype(BF16)
    pair_grad = jnp.concatenate(
        [
            (grad_hidden * up_value * (gate_sig * (1.0 + gate_value * (1.0 - gate_sig)))).astype(BF16),
            (grad_hidden * gate_act).astype(BF16),
        ],
        axis=1,
    )
    back_part = dot_nt(pair_grad, pair_weight).astype(BF16)
    back_part, pair_late, hidden_late, mid_late = together(
        (back_part, pair_grad, hidden_low, mid_low)
    )
    back_moved = deal(back_part, "b")
    ffn_part = dot_nt(hidden_late, down_weight).astype(BF16)
    grad_ffn_part = jnp.concatenate(
        [
            dot_tn(mid_late, pair_late).astype(BF16),
            dot_tn(dy_low, hidden_late).astype(BF16),
        ],
        axis=1,
    )
    back_moved, ffn_part, grad_ffn_part = together((back_moved, ffn_part, grad_ffn_part))

    def owners(value):
        return lax.psum_scatter(value, GROUP, scatter_dimension=0, tiled=True)

    hidden_grad, mix_own, grad_mid_gain = row_parts(
        middle_back_kernel,
        place,
        [("own", back_moved), ("own", hidden_in), ("all", dy_low), ("one", gain_mid_8)],
        [("own", own_f32), ("own", own_low), ("one", gain_part)],
        rows,
    )
    grad_mid_gain = jnp.sum(grad_mid_gain, axis=0)
    mix_low = copy_rows_ordered(mix_own)
    mix_low, ffn_part = together((mix_low, ffn_part))
    grad_ffn = owners(grad_ffn_part)
    dnormed = dot_nn(mix_low, out_weight)
    grad_proj, conv_grad, head_gain_grad, decay_grads = delta_backward(
        proj, info, seg_rows, par, taps, head_gain, saved, dnormed, sizes
    )
    first_part = dot_nt(grad_proj, mixer_weight).astype(BF16)
    result_moved = deal(ffn_part, "y")
    first_part, proj_late, mix_late, normed_late, grad_ffn, result_moved = together(
        (first_part, grad_proj, mix_low, normed_low, grad_ffn, result_moved)
    )
    first_moved = deal(first_part, "n")
    grad_mixer_part = jnp.concatenate(
        [
            dot_tn(normed_in, proj_late).astype(BF16),
            dot_tn(mix_late, normed_late).astype(BF16),
        ],
        axis=1,
    )
    result = (hidden_in + add_dealt(result_moved, "y")).astype(BF16)
    result_back = exchange(to_sources(result)).reshape(rows, width)
    result_back = jnp.pad(result_back, ((0, PAD), (0, 0)))
    result_near = relay_first(result_back)
    first_moved, grad_mixer_part, *result_near = together(
        (first_moved, grad_mixer_part, *result_near)
    )

    grad_mixer_all = owners(grad_mixer_part)
    grad_mixer = grad_mixer_all[:, : mixer_weight.shape[1]].astype(F32)
    grad_out = grad_mixer_all[:, mixer_weight.shape[1] :].astype(F32).T
    grad_pair = grad_ffn[:, : 2 * units].astype(F32)
    grad_down = grad_ffn[:, 2 * units :].astype(F32).T

    token_grad, grad_in_gain = row_parts(
        first_back_kernel,
        place,
        [("own", first_moved), ("own", hidden_grad), ("all", x_low), ("one", gain_in_8)],
        [("own", own_low), ("one", gain_part)],
        rows,
    )
    grad_in_gain = jnp.sum(grad_in_gain, axis=0)

    conv_sum = jnp.sum(conv_grad.reshape(spans, PAD, -1), axis=1)

    def taps_to(value, size):
        parted = value.reshape(spans, heads, groups, size // groups)
        return jnp.transpose(parted, (2, 0, 1, 3)).reshape(groups, -1)

    gain_sum = jnp.sum(head_gain_grad.reshape(PAD * heads, value_size), axis=0)
    decay_sums = jnp.sum(decay_grads.reshape(2, PAD, LANES), axis=1)[:, :heads].reshape(1, -1)
    parts = [
        grad_in_gain.reshape(groups, own),
        grad_mid_gain.reshape(groups, own),
        gain_sum.reshape(groups, -1),
        taps_to(conv_sum[:, :key_cols], key_size),
        taps_to(conv_sum[:, key_cols : 2 * key_cols], key_size),
        taps_to(conv_sum[:, 2 * key_cols :], value_size),
        jnp.broadcast_to(decay_sums, (groups, decay_sums.shape[1])),
    ]
    lens = [part.shape[1] for part in parts]
    packed = jnp.concatenate(parts, axis=1)
    packed = jnp.pad(packed, ((0, 0), (0, width - packed.shape[1])))
    extra = jnp.pad(pair_rows(packed), ((0, 0), (0, PAD - 2), (0, 0)))
    grad_sent = to_sources(token_grad)
    came = exchange(jnp.concatenate([grad_sent, extra], axis=1))
    before, after = result_near
    result_far = relay_second(before, after)
    mixed, unused = to_given((result_back, before, after, *result_far))
    summed = jnp.sum(came[:, share : share + 2].astype(F32), axis=(0, 1))
    block = jnp.concatenate(
        [
            came[:, :share].reshape(rows, width),
            jnp.pad(pair_rows(summed), ((0, PAD - 2), (0, 0))),
        ],
        axis=0,
    )
    grad_tokens, full = to_given(relayed_blocks(block))
    tp_summed = jnp.sum(
        full.reshape(RELAYED, held, width)[:, rows : rows + 2].astype(F32), axis=(0, 1)
    )
    pieces = []
    offset = 0
    for index, length in enumerate(lens):
        origin = tp_summed if index < 3 else summed
        pieces.append(origin[offset : offset + length])
        offset += length
    decay_pair = pieces[6].reshape(2, heads)
    edges = [0, key_cols, 2 * key_cols, 2 * key_cols + value_cols, tail_at]
    return (
        mixed,
        grad_tokens,
        pieces[0],
        grad_mixer[:, edges[0] : edges[1]],
        grad_mixer[:, edges[1] : edges[2]],
        grad_mixer[:, edges[2] : edges[3]],
        grad_mixer[:, edges[3] : edges[4]],
        grad_mixer[:, tail_at : tail_at + heads],
        grad_mixer[:, tail_at + heads : tail_at + 2 * heads],
        pieces[3].reshape(query_conv.shape),
        pieces[4].reshape(key_conv.shape),
        pieces[5].reshape(value_conv.shape),
        decay_pair[0],
        decay_pair[1],
        pieces[2],
        grad_out,
        pieces[1],
        grad_pair[:, :units],
        grad_pair[:, units:],
        grad_down,
    )


def solution(mesh):
    in_specs = (
        P(None, ("fsdp", "ctx"), None),
        P(None, ("fsdp", "ctx"), None),
        P(),
        P(),
        P(("fsdp", "ctx")),
        P(("fsdp", "ctx"), "tp"),
        P(("fsdp", "ctx"), "tp"),
        P(("fsdp", "ctx"), "tp"),
        P(("fsdp", "ctx"), "tp"),
        P(("fsdp", "ctx"), "tp"),
        P(("fsdp", "ctx"), "tp"),
        P(None, "tp", ("fsdp", "ctx")),
        P(None, "tp", ("fsdp", "ctx")),
        P(None, "tp", ("fsdp", "ctx")),
        P("tp"),
        P("tp"),
        P(("fsdp", "ctx")),
        P("tp", ("fsdp", "ctx")),
        P(("fsdp", "ctx")),
        P(("fsdp", "ctx"), "tp"),
        P(("fsdp", "ctx"), "tp"),
        P("tp", ("fsdp", "ctx")),
    )
    out_specs = (
        P(None, ("fsdp", "ctx"), None),
        P(None, ("fsdp", "ctx"), None),
        P(("fsdp", "ctx")),
        P(("fsdp", "ctx"), "tp"),
        P(("fsdp", "ctx"), "tp"),
        P(("fsdp", "ctx"), "tp"),
        P(("fsdp", "ctx"), "tp"),
        P(("fsdp", "ctx"), "tp"),
        P(("fsdp", "ctx"), "tp"),
        P(None, "tp", ("fsdp", "ctx")),
        P(None, "tp", ("fsdp", "ctx")),
        P(None, "tp", ("fsdp", "ctx")),
        P("tp"),
        P("tp"),
        P(("fsdp", "ctx")),
        P("tp", ("fsdp", "ctx")),
        P(("fsdp", "ctx")),
        P(("fsdp", "ctx"), "tp"),
        P(("fsdp", "ctx"), "tp"),
        P("tp", ("fsdp", "ctx")),
    )
    return jax.shard_map(
        per_device, mesh=mesh, in_specs=in_specs, out_specs=out_specs, check_vma=False
    )
```

```python
import functools
import jax
import jax.numpy as jnp
from jax import lax
from jax.sharding import PartitionSpec as P
from jax.experimental import pallas as pl
from jax.experimental.pallas import tpu as pltpu

CHUNK = 128
LANES = 128
PAD = 8
square_eps = 1e-05
unit_eps = 1e-06
F32 = jnp.float32
BF16 = jnp.bfloat16


def dot_nn(left, right):
    return lax.dot_general(left, right, (((1,), (0,)), ((), ())), preferred_element_type=F32)


def dot_nt(left, right):
    return lax.dot_general(left, right, (((1,), (1,)), ((), ())), preferred_element_type=F32)


def dot_tn(left, right):
    return lax.dot_general(left, right, (((0,), (0,)), ((), ())), preferred_element_type=F32)


def halves(value):
    high = value.astype(BF16)
    return high, (value - high.astype(F32)).astype(BF16)


def dot_fine(left, right):
    left_high, left_low = halves(left)
    right_high, right_low = halves(right)
    return (
        dot_nn(left_high, right_high)
        + dot_nn(left_high, right_low)
        + dot_nn(left_low, right_high)
    )


def sum_by(mask, value):
    high, rest = halves(value)
    middle, low = halves(value - high.astype(F32))
    return dot_nn(mask, high) + dot_nn(mask, middle) + dot_nn(mask, low)


def sigmoid(value):
    return 1.0 / (1.0 + jnp.exp(-value))


def softplus(value):
    return jnp.maximum(value, 0.0) + jnp.log1p(jnp.exp(-jnp.abs(value)))


def low_dot(left, right):
    return dot_nn(left.astype(BF16), right.astype(BF16))


def inverses_lower(lower_mats, row_id, col_id):
    size = row_id.shape[0]

    def level(width):
        same = row_id // (2 * width) == col_id // (2 * width)
        return same & ((row_id // width) % 2 == 1) & ((col_id // width) % 2 == 0)

    unit = jnp.where(row_id == col_id, 1.0, 0.0)
    mask = level(1)
    results = [unit - jnp.where(mask, mat, 0.0) for mat in lower_mats]
    width = 2
    while width < size:
        mask = level(width)
        parts = [low_dot(r, jnp.where(mask, mat, 0.0)) for r, mat in zip(results, lower_mats)]
        results = [r - low_dot(p, r) for p, r in zip(parts, results)]
        width *= 2
    rests = [unit - r - dot_fine(mat, r) for r, mat in zip(results, lower_mats)]
    return [r + low_dot(r, rest) for r, rest in zip(results, rests)]


def in_turn(bodies):
    asked = [next(body) for body in bodies]
    while asked:
        made = asked[0][0]([item[1] for item in asked]) if asked[0] else [None] * len(asked)
        following = []
        for body, value in zip(bodies, made):
            try:
                following.append(body.send(value))
            except StopIteration:
                pass
        asked = following


def chunk_basics(gates, par, info, seg_row, row_id, col_id, lane_id, head_count):
    step = gates + par[1:2, :]
    log_decay = jnp.where(lane_id < head_count, par[0:1, :] * softplus(step), 0.0)
    beta_raw = sigmoid(gates)
    valid = info[:, 1:2]
    lower = row_id >= col_id
    cumulative = sum_by(jnp.where(lower, 1.0, 0.0).astype(BF16), log_decay)
    both = jnp.where(lane_id < head_count, cumulative, beta_raw * valid)
    turned = jnp.transpose(both)
    inner = lower & (info[:, 0:1] == seg_row)
    return step, log_decay, beta_raw, both, turned, inner


def activations(ext, taps, masks, start, stop, rows):
    value = taps[3:4, start:stop] * ext[PAD : PAD + rows, start:stop]
    for distance in (1, 2, 3):
        shifted = ext[PAD - distance : PAD - distance + rows, start:stop]
        value = value + masks[distance - 1] * (taps[3 - distance : 4 - distance, start:stop] * shifted)
    return value


def forward_kernel(
    head_count, key_size, value_size,
    proj, info_ref, segr, par_ref, taps, gain_ref,
    normed_out, state_out, inverse_out, pseudo_out, output_out,
    state, ext,
):
    rows = proj.shape[0]
    width = head_count * (2 * key_size + value_size)
    gate_at = width
    tail_at = width + head_count * value_size

    @pl.when(pl.program_id(0) == 0)
    def start():
        state[...] = jnp.zeros_like(state)
        ext[0:PAD, :] = jnp.zeros((PAD, width), F32)

    ext[PAD : PAD + rows, :] = proj[:, 0:width]
    info = info_ref[...]
    row_id = lax.broadcasted_iota(jnp.int32, (rows, rows), 0)
    col_id = lax.broadcasted_iota(jnp.int32, (rows, rows), 1)
    lane_id = lax.broadcasted_iota(jnp.int32, (rows, LANES), 1)
    masks = tuple(info[:, 1 + d : 2 + d] for d in (1, 2, 3))
    valid = info[:, 1:2]
    unused, log_decay, beta_raw, both, turned, inner = chunk_basics(
        proj[:, tail_at : tail_at + LANES], par_ref[...], info, segr[0:1, :],
        row_id, col_id, lane_id, head_count,
    )
    carried_mask = info[:, 8:9]
    tail_mask = info[:, 9:10]
    strict = row_id > col_id
    key_at = head_count * key_size
    value_at = 2 * key_at
    def one_head(head):
        ks = key_size
        vs = value_size
        act_q = activations(ext, taps, masks, head * ks, (head + 1) * ks, rows)
        act_k = activations(ext, taps, masks, key_at + head * ks, key_at + (head + 1) * ks, rows)
        act_v = activations(ext, taps, masks, value_at + head * vs, value_at + (head + 1) * vs, rows)
        cq = act_q * sigmoid(act_q)
        ck = act_k * sigmoid(act_k)
        values = act_v * sigmoid(act_v)
        query = cq * (lax.rsqrt(jnp.sum(cq * cq, axis=1, keepdims=True) + unit_eps) * ks ** -0.5)
        key = ck * lax.rsqrt(jnp.sum(ck * ck, axis=1, keepdims=True) + unit_eps)
        yield
        qb = query.astype(BF16)
        kb = key.astype(BF16)
        cum = both[:, head : head + 1]
        beta = both[:, head_count + head : head_count + head + 1]
        cum_row = turned[head : head + 1, :]
        beta_row = turned[head_count + head : head_count + head + 1, :]
        decays = jnp.where(inner, jnp.exp(jnp.minimum(cum - cum_row, 0.0)), 0.0)
        lower_mat = jnp.where(strict, decays * dot_nt(kb, kb) * beta_row, 0.0)
        inverse = yield (lambda mats: inverses_lower(mats, row_id, col_id)), lower_mat
        yield
        carried = jnp.exp(cum) * carried_mask
        last = cum[rows - 1 : rows, :]
        tail = jnp.exp(last - cum) * tail_mask
        keep = carried[rows - 1 : rows, :]
        before = state[head]
        state_out[0, head] = before
        sb = before.astype(BF16)
        target = values - carried * dot_nn(kb, sb)
        ib = inverse.astype(BF16)
        pseudo = dot_nn(ib, target.astype(BF16))
        inverse_out[0, head] = ib
        pseudo_out[:, head * vs : (head + 1) * vs] = pseudo
        yield
        weighted = beta * pseudo
        mix = decays * dot_nt(qb, kb)
        output = carried * dot_nn(qb, sb) + dot_nn(mix.astype(BF16), weighted.astype(BF16))
        output_out[:, head * vs : (head + 1) * vs] = output
        state[head] = keep * before + dot_tn(kb, (tail * weighted).astype(BF16))
        yield
        gate = proj[:, gate_at + head * vs : gate_at + (head + 1) * vs]
        scale = lax.rsqrt(jnp.mean(output * output, axis=1, keepdims=True) + square_eps)
        normed = output * scale * gain_ref[0:1, :] * (gate * sigmoid(gate)) * valid
        normed_out[:, head * vs : (head + 1) * vs] = normed.astype(BF16)

    in_turn([one_head(head) for head in range(head_count)])
    ext[0:PAD, :] = ext[rows : rows + PAD, :]


def backward_kernel(
    head_count, key_size, value_size,
    proj, prior, info_ref, segr, par_ref, taps, gain_ref,
    state_in, inverse_in, pseudo_in, output_in, dnormed,
    grad_out, conv_out, gain_out, small_out,
    dstate, ext, dext,
):
    rows = proj.shape[0]
    width = head_count * (2 * key_size + value_size)
    gate_at = width
    tail_at = width + head_count * value_size
    place = pl.program_id(0)
    count = pl.num_programs(0)

    @pl.when(place == 0)
    def start():
        dstate[...] = jnp.zeros_like(dstate)
        dext[rows : rows + PAD, :] = jnp.zeros((PAD, width), F32)
        conv_out[...] = jnp.zeros_like(conv_out)
        gain_out[...] = jnp.zeros_like(gain_out)
        small_out[...] = jnp.zeros_like(small_out)

    first = place == count - 1
    ext[0:PAD, :] = jnp.where(first, 0.0, prior[:, 0:width])
    ext[PAD : PAD + rows, :] = proj[:, 0:width]
    info = info_ref[...]
    row_id = lax.broadcasted_iota(jnp.int32, (rows, rows), 0)
    col_id = lax.broadcasted_iota(jnp.int32, (rows, rows), 1)
    lane_id = lax.broadcasted_iota(jnp.int32, (rows, LANES), 1)
    masks = tuple(info[:, 1 + d : 2 + d] for d in (1, 2, 3))
    later = tuple(info[:, 4 + d : 5 + d] for d in (1, 2, 3))
    valid = info[:, 1:2]
    step, log_decay, beta_raw, both, turned, inner = chunk_basics(
        proj[:, tail_at : tail_at + LANES], par_ref[...], info, segr[0:1, :],
        row_id, col_id, lane_id, head_count,
    )
    carried_mask = info[:, 8:9]
    tail_mask = info[:, 9:10]
    strict = row_id > col_id
    last_row = lax.broadcasted_iota(jnp.int32, (rows, 1), 0) == rows - 1
    row_of = lax.broadcasted_iota(jnp.int32, (LANES, rows), 0)
    ks = key_size
    vs = value_size
    key_at = head_count * ks
    value_at = 2 * key_at
    sums = {}

    def fold(value):
        return jnp.sum(value.reshape(rows // PAD, PAD, value.shape[1]), axis=0)

    def conv_back(da, start, stop):
        dext[0:rows, start:stop] = da
        back = taps[3:4, start:stop] * da
        conv_out[3 * PAD : 4 * PAD, start:stop] += fold(da * ext[PAD : PAD + rows, start:stop])
        for d in (1, 2, 3):
            back = back + later[d - 1] * (taps[3 - d : 4 - d, start:stop] * dext[d : d + rows, start:stop])
            shifted = ext[PAD - d : PAD - d + rows, start:stop]
            conv_out[(3 - d) * PAD : (4 - d) * PAD, start:stop] += fold(masks[d - 1] * da * shifted)
        grad_out[:, start:stop] = back.astype(BF16)

    def one_head(head):
        act_q = activations(ext, taps, masks, head * ks, (head + 1) * ks, rows)
        act_k = activations(ext, taps, masks, key_at + head * ks, key_at + (head + 1) * ks, rows)
        act_v = activations(ext, taps, masks, value_at + head * vs, value_at + (head + 1) * vs, rows)
        sig_q, sig_k, sig_v = sigmoid(act_q), sigmoid(act_k), sigmoid(act_v)
        cq, ck, values = act_q * sig_q, act_k * sig_k, act_v * sig_v
        rate_q = lax.rsqrt(jnp.sum(cq * cq, axis=1, keepdims=True) + unit_eps)
        rate_k = lax.rsqrt(jnp.sum(ck * ck, axis=1, keepdims=True) + unit_eps)
        unit_q = cq * rate_q
        query = unit_q * ks ** -0.5
        key = ck * rate_k
        yield
        qb = query.astype(BF16)
        kb = key.astype(BF16)
        cum = both[:, head : head + 1]
        beta = both[:, head_count + head : head_count + head + 1]
        cum_row = turned[head : head + 1, :]
        beta_row = turned[head_count + head : head_count + head + 1, :]
        decays = jnp.where(inner, jnp.exp(jnp.minimum(cum - cum_row, 0.0)), 0.0)
        carried = jnp.exp(cum) * carried_mask
        tail = jnp.exp(cum[rows - 1 : rows, :] - cum) * tail_mask
        keep = carried[rows - 1 : rows, :]
        yield
        before = state_in[0, head]
        sb = before.astype(BF16)
        ib = inverse_in[0, head]
        pseudo = pseudo_in[:, head * vs : (head + 1) * vs]
        output = output_in[:, head * vs : (head + 1) * vs]
        gate = proj[:, gate_at + head * vs : gate_at + (head + 1) * vs]
        given = dnormed[:, head * vs : (head + 1) * vs] * valid
        gain = gain_ref[0:1, :]
        scale = lax.rsqrt(jnp.mean(output * output, axis=1, keepdims=True) + square_eps)
        unit_o = output * scale
        sig_g = sigmoid(gate)
        silu_g = gate * sig_g
        dunit = given * gain * silu_g
        doutput = scale * (dunit - unit_o * jnp.mean(unit_o * dunit, axis=1, keepdims=True))
        dgate = given * unit_o * gain * (sig_g * (1.0 + gate * (1.0 - sig_g)))
        gain_out[:, head * vs : (head + 1) * vs] += fold(given * unit_o * silu_g)
        grad_out[:, gate_at + head * vs : gate_at + (head + 1) * vs] = dgate.astype(BF16)
        yield
        dob = doutput.astype(BF16)
        weighted = beta * pseudo
        wb = weighted.astype(BF16)
        gram = dot_nt(kb, kb)
        cross = dot_nt(qb, kb)
        mix = decays * cross
        yield
        after = dstate[head]
        ab = after.astype(BF16)
        from_state = dot_nn(kb, ab)
        dweighted = dot_tn(mix.astype(BF16), dob) + tail * from_state
        dbeta = jnp.sum(dweighted * pseudo, axis=1, keepdims=True)
        yield
        dtarget = dot_tn(ib, (beta * dweighted).astype(BF16))
        dtb = dtarget.astype(BF16)
        read = dot_nn(kb, sb)
        yield
        dcarried = jnp.sum(doutput * dot_nn(qb, sb), axis=1, keepdims=True) - jnp.sum(
            dtarget * read, axis=1, keepdims=True
        )
        dtail = jnp.sum(weighted * from_state, axis=1, keepdims=True)
        dkeep = jnp.sum(jnp.sum(after * before, axis=1, keepdims=True), axis=0, keepdims=True)
        cdo = (carried * doutput).astype(BF16)
        cdt = (carried * dtarget).astype(BF16)
        dstate[head] = keep * after + dot_tn(qb, cdo) - dot_tn(kb, cdt)
        yield
        dmix = dot_nt(dob, wb)
        dcross = (dmix * decays).astype(BF16)
        dlower = jnp.where(strict, -dot_nt(dtb, pseudo.astype(BF16)), 0.0) * decays
        dgram = (dlower * beta_row).astype(BF16)
        plain = dlower * gram
        inner_grad = dmix * mix + plain * beta_row
        yield
        dquery = dot_nt(cdo, sb) + dot_nn(dcross, kb)
        dkey = (
            dot_tn(dcross, qb)
            + dot_nn(dgram, kb)
            + dot_tn(dgram, kb)
            + dot_nt((tail * weighted).astype(BF16), ab)
            - dot_nt(cdt, sb)
        )
        yield
        dlast = jnp.sum(dtail * tail, axis=0, keepdims=True) + dkeep * keep
        dcum_col = (
            jnp.sum(inner_grad, axis=1, keepdims=True)
            + dcarried * carried
            - dtail * tail
            + jnp.where(last_row, dlast, 0.0)
        )
        sums[head] = (
            dcum_col,
            dbeta,
            -jnp.sum(inner_grad, axis=0, keepdims=True),
            jnp.sum(plain, axis=0, keepdims=True),
        )
        yield
        dq_scaled = dquery * ks ** -0.5
        dcq = (dq_scaled - unit_q * jnp.sum(unit_q * dq_scaled, axis=1, keepdims=True)) * rate_q
        dck = (dkey - key * jnp.sum(key * dkey, axis=1, keepdims=True)) * rate_k
        conv_back(dcq * (sig_q * (1.0 + act_q * (1.0 - sig_q))), head * ks, (head + 1) * ks)
        yield
        conv_back(
            dck * (sig_k * (1.0 + act_k * (1.0 - sig_k))), key_at + head * ks, key_at + (head + 1) * ks
        )
        conv_back(
            dtarget * (sig_v * (1.0 + act_v * (1.0 - sig_v))),
            value_at + head * vs,
            value_at + (head + 1) * vs,
        )

    for head in range(head_count):
        in_turn([one_head(head)])
    dcum = jnp.zeros((rows, LANES), F32)
    dturned = jnp.zeros((LANES, rows), F32)
    for head, (dcum_col, dbeta, dcum_row, dbeta_row) in sums.items():
        dcum = jnp.where(lane_id == head, dcum_col, dcum)
        dcum = jnp.where(lane_id == head_count + head, dbeta, dcum)
        dturned = jnp.where(row_of == head, dcum_row, dturned)
        dturned = jnp.where(row_of == head_count + head, dbeta_row, dturned)
    dboth = dcum + jnp.transpose(dturned)
    upper = jnp.where(row_id <= col_id, 1.0, 0.0).astype(BF16)
    dlog = sum_by(upper, jnp.where(lane_id < head_count, dboth, 0.0))
    dalpha = dlog * par_ref[0:1, :] * sigmoid(step)
    dbeta_raw = dboth * valid * beta_raw * (1.0 - beta_raw)
    tail_grad = jnp.where(
        lane_id < head_count, dalpha, jnp.where(lane_id < 2 * head_count, dbeta_raw, 0.0)
    )
    grad_out[:, tail_at : tail_at + LANES] = tail_grad.astype(BF16)
    small_out[0:PAD, :] += fold(dlog * log_decay)
    small_out[PAD : 2 * PAD, :] += fold(jnp.where(lane_id < head_count, dalpha, 0.0))
    dext[rows : rows + PAD, :] = dext[0:PAD, :]


def delta_forward(proj, info, seg_rows, par, taps, gain, sizes):
    head_count, key_size, value_size = sizes
    total, columns = proj.shape
    steps = total // CHUNK
    width = head_count * (2 * key_size + value_size)
    span = head_count * value_size
    whole = lambda a: pl.BlockSpec(a.shape, lambda i: (0, 0))
    by_rows = lambda n: pl.BlockSpec((CHUNK, n), lambda i: (i, 0))
    return pl.pallas_call(
        functools.partial(forward_kernel, head_count, key_size, value_size),
        grid=(steps,),
        in_specs=[
            by_rows(columns),
            by_rows(LANES),
            pl.BlockSpec((PAD, CHUNK), lambda i: (0, i)),
            whole(par),
            whole(taps),
            whole(gain),
        ],
        out_specs=[
            by_rows(span),
            pl.BlockSpec((1, head_count, key_size, value_size), lambda i: (i, 0, 0, 0)),
            pl.BlockSpec((1, head_count, CHUNK, CHUNK), lambda i: (i, 0, 0, 0)),
            by_rows(span),
            by_rows(span),
        ],
        out_shape=[
            jax.ShapeDtypeStruct((total, span), BF16),
            jax.ShapeDtypeStruct((steps, head_count, key_size, value_size), F32),
            jax.ShapeDtypeStruct((steps, head_count, CHUNK, CHUNK), BF16),
            jax.ShapeDtypeStruct((total, span), F32),
            jax.ShapeDtypeStruct((total, span), F32),
        ],
        scratch_shapes=[
            pltpu.VMEM((head_count, key_size, value_size), F32),
            pltpu.VMEM((CHUNK + PAD, width), F32),
        ],
        compiler_params=pltpu.CompilerParams(vmem_limit_bytes=48 * 1024 * 1024),
        name="delta_forward",
    )(proj, info, seg_rows, par, taps, gain)


def delta_backward(proj, info, seg_rows, par, taps, gain, saved, dnormed, sizes):
    head_count, key_size, value_size = sizes
    total, columns = proj.shape
    steps = total // CHUNK
    width = head_count * (2 * key_size + value_size)
    span = head_count * value_size
    states, inverses, pseudos, outputs = saved
    blocks = CHUNK // PAD
    turn = lambda i: steps - 1 - i
    whole = lambda a: pl.BlockSpec(a.shape, lambda i: (0, 0))
    by_rows = lambda n: pl.BlockSpec((CHUNK, n), lambda i: (turn(i), 0))
    return pl.pallas_call(
        functools.partial(backward_kernel, head_count, key_size, value_size),
        grid=(steps,),
        in_specs=[
            by_rows(columns),
            pl.BlockSpec((PAD, columns), lambda i: (jnp.maximum(turn(i) * blocks - 1, 0), 0)),
            by_rows(LANES),
            pl.BlockSpec((PAD, CHUNK), lambda i: (0, turn(i))),
            whole(par),
            whole(taps),
            whole(gain),
            pl.BlockSpec((1, head_count, key_size, value_size), lambda i: (turn(i), 0, 0, 0)),
            pl.BlockSpec((1, head_count, CHUNK, CHUNK), lambda i: (turn(i), 0, 0, 0)),
            by_rows(span),
            by_rows(span),
            by_rows(span),
        ],
        out_specs=[
            by_rows(columns),
            pl.BlockSpec((4 * PAD, width), lambda i: (0, 0)),
            pl.BlockSpec((PAD, span), lambda i: (0, 0)),
            pl.BlockSpec((2 * PAD, LANES), lambda i: (0, 0)),
        ],
        out_shape=[
            jax.ShapeDtypeStruct((total, columns), BF16),
            jax.ShapeDtypeStruct((4 * PAD, width), F32),
            jax.ShapeDtypeStruct((PAD, span), F32),
            jax.ShapeDtypeStruct((2 * PAD, LANES), F32),
        ],
        scratch_shapes=[
            pltpu.VMEM((head_count, key_size, value_size), F32),
            pltpu.VMEM((CHUNK + PAD, width), F32),
            pltpu.VMEM((CHUNK + PAD, width), F32),
        ],
        compiler_params=pltpu.CompilerParams(vmem_limit_bytes=48 * 1024 * 1024),
        name="delta_backward",
    )(proj, proj, info, seg_rows, par, taps, gain, states, inverses, pseudos, outputs, dnormed)


def middle_kernel(place, own, after, before, x_ref, gain, hidden_out, normed_out):
    mixer = own[...].astype(F32) + after[...].astype(F32) + before[...].astype(F32)
    hidden = mixer + x_ref[...].astype(F32)
    rate = lax.rsqrt(jnp.mean(hidden * hidden, axis=1, keepdims=True) + square_eps)
    hidden_out[...] = hidden
    normed_out[...] = (hidden * rate * gain[0:1, :]).astype(BF16)


def norm_back(grad, value, gain):
    rate = lax.rsqrt(jnp.mean(value * value, axis=1, keepdims=True) + square_eps)
    scaled = grad * gain
    inner = jnp.mean(value * scaled, axis=1, keepdims=True)
    return rate * scaled - rate * rate * rate * value * inner, grad * value * rate


def rows_summed(value):
    return jnp.sum(value.reshape(value.shape[0] // PAD, PAD, value.shape[1]), axis=0)


def middle_back_kernel(place, moved, hidden, dy_ref, gain, grad_out, low_out, gain_out):
    @pl.when(pl.program_id(0) == 0)
    def start():
        gain_out[...] = jnp.zeros_like(gain_out)

    back, part = norm_back(moved[...].astype(F32), hidden[...], gain[0:1, :])
    grad = dy_ref[...].astype(F32) + back
    grad_out[...] = grad
    low_out[...] = grad.astype(BF16)
    gain_out[...] += rows_summed(part)


def first_back_kernel(place, own, after, before, late, x_ref, gain, grad_out, gain_out):
    @pl.when(pl.program_id(0) == 0)
    def start():
        gain_out[...] = jnp.zeros_like(gain_out)

    moved = own[...].astype(F32) + after[...].astype(F32) + before[...].astype(F32)
    back, part = norm_back(moved, x_ref[...].astype(F32), gain[0:1, :])
    grad_out[...] = (late[...] + back).astype(BF16)
    gain_out[...] += rows_summed(part)


def row_parts(kernel, place, arrays, outs, rows):
    part = 48 if rows % 48 == 0 else rows
    steps = rows // part

    def spec(kind, shape):
        if kind == "own":
            return pl.BlockSpec((part, shape[1]), lambda i, p: (i, 0))
        if kind == "all":
            return pl.BlockSpec((part, shape[1]), lambda i, p: (p[0] * steps + i, 0))
        return pl.BlockSpec(shape, lambda i, p: (0, 0))

    return pl.pallas_call(
        kernel,
        grid_spec=pltpu.PrefetchScalarGridSpec(
            num_scalar_prefetch=1,
            grid=(steps,),
            in_specs=[spec(kind, value.shape) for kind, value in arrays],
            out_specs=[spec(kind, value.shape) for kind, value in outs],
        ),
        out_shape=[value for kind, value in outs],
        compiler_params=pltpu.CompilerParams(vmem_limit_bytes=40 * 1024 * 1024),
        name=kernel.__name__,
    )(place, *[value for kind, value in arrays])


def widen_kernel(grads, *outs):
    *direct, turned, out_turned = outs
    start = 0
    for out in direct:
        stop = start + out.shape[1]
        out[...] = grads[:, start:stop].astype(F32)
        start = stop
    turned[...] = jnp.transpose(grads[:, start : start + LANES].astype(F32))
    out_turned[...] = jnp.transpose(grads[:, start + LANES :].astype(F32))


def widened(grads, columns):
    own, total = grads.shape
    shapes = [(own, count) for count in columns]
    shapes += [(LANES, own), (total - sum(columns) - LANES, own)]
    return pl.pallas_call(
        widen_kernel,
        out_shape=[jax.ShapeDtypeStruct(shape, F32) for shape in shapes],
        compiler_params=pltpu.CompilerParams(vmem_limit_bytes=40 * 1024 * 1024),
        name="widen",
    )(grads)


def place_arrays(length_row, total):
    places = jnp.arange(total, dtype=jnp.int32)
    ids = jnp.arange(length_row.shape[0])
    ends = jnp.sum(jnp.where(ids[None, :] <= ids[:, None], length_row[None, :], 0), axis=1)
    starts = ends - length_row

    def seg_at(at):
        return jnp.sum((at[:, None] >= starts[None, :]).astype(jnp.int32), axis=1) - 1

    segment = seg_at(places)
    valid = (places < ends[-1]).astype(F32)
    lanes = [segment.astype(F32), valid]
    for d in (1, 2, 3):
        lanes.append((seg_at(places - d) == segment).astype(F32))
    for d in (1, 2, 3):
        lanes.append(((seg_at(places + d) == segment) & (places + d < total)).astype(F32))
    head_place = places - places % CHUNK
    lanes.append(((seg_at(head_place - 1) == segment) & (head_place > 0)).astype(F32))
    lanes.append((seg_at(head_place + CHUNK - 1) == segment).astype(F32))
    info = jnp.stack(lanes, axis=1)
    info = jnp.pad(info, ((0, 0), (0, LANES - len(lanes))))
    rows = jnp.broadcast_to(segment.astype(F32)[None, :], (PAD, total))
    return info, rows


GROUP = ("fsdp", "ctx")


def pair_rows(values):
    high, low = halves(values)
    return jnp.stack([high, low], axis=-2)


SC_SUM = "by"
SC_COPY = ""


def deal(part, name=""):
    if name and name in SC_SUM:
        return lax.psum_scatter(part, "tp", scatter_dimension=0, tiled=True)
    return lax.all_to_all(part, "tp", split_axis=0, concat_axis=0, tiled=True)


def add_dealt(moved, name=""):
    if name and name in SC_SUM:
        return moved.astype(F32)
    count = lax.axis_size("tp")
    return jnp.sum(moved.reshape(count, -1, moved.shape[1]).astype(F32), axis=0)


def copy_rows(own, name=""):
    if name and name in SC_COPY:
        return lax.all_gather(own, "tp", axis=0, tiled=True)
    return deal(jnp.concatenate([own] * lax.axis_size("tp"), axis=0))


def relay_send(value, route):
    return lax.ppermute(value, "tp", route)


def relay_first(own):
    return relay_send(own, [(0, 1), (1, 2), (2, 3)]), relay_send(own, [(1, 0), (2, 1), (3, 2)])


def relay_second(before, after):
    place = lax.axis_index("tp")
    before_2 = relay_send(before, [(1, 2), (2, 3)])
    after_2 = relay_send(after, [(2, 1), (1, 0)])
    far = relay_send(jnp.where(place == 1, before, after), [(1, 3), (2, 0)])
    return before_2, after_2, far


def relayed_blocks(own):
    before, after = relay_first(own)
    return (own, before, after, *relay_second(before, after))


def sum_first(part, rows):
    place = lax.axis_index("tp")
    block = rows_of(part, rows)
    return (
        relay_send(block(place - 2), [(2, 1), (3, 2)]),
        relay_send(block(place + 2), [(1, 2), (0, 1)]),
        relay_send(block(jnp.where(place == 3, 0, 3)), [(3, 1), (0, 2)]),
    )


def rows_of(part, rows):
    def block(index):
        return lax.dynamic_slice(part, (jnp.clip(index, 0, 3) * rows, 0), (rows, part.shape[1]))

    return block


def sum_middle(part, rows, came):
    place = lax.axis_index("tp")
    block = rows_of(part, rows)
    from_after, from_before, far = (value.astype(F32) for value in came)
    to_before = block(place - 1).astype(F32) + from_after + jnp.where(place == 1, far, 0.0)
    to_after = block(place + 1).astype(F32) + from_before + jnp.where(place == 2, far, 0.0)
    return to_before.astype(BF16), to_after.astype(BF16)


def sum_second(to_before, to_after):
    return (
        relay_send(to_before, [(1, 0), (2, 1), (3, 2)]),
        relay_send(to_after, [(0, 1), (1, 2), (2, 3)]),
    )


def copy_rows_ordered(own):
    place = lax.axis_index("tp")
    own, before, after, before_2, after_2, far = relayed_blocks(own)
    parts = []
    for source in range(4):
        part = own
        for apart, block in ((-1, before), (1, after), (-2, before_2), (2, after_2)):
            if 0 <= source - apart < 4:
                part = jnp.where(source - place == apart, block, part)
        if source in (0, 3):
            part = jnp.where(jnp.abs(source - place) == 3, far, part)
        parts.append(part)
    return jnp.concatenate(parts, axis=0)


def relayed_block(place, source):
    apart = source - place
    near = jnp.where(apart == 0, 0, jnp.where(apart == -1, 1, 2))
    return jnp.where(jnp.abs(apart) == 3, 5, jnp.where(apart == -2, 3, jnp.where(apart == 2, 4, near)))


RELAYED = 6


together = lax.optimization_barrier


def per_device(
    tokens, cotangent, lengths, order, gain_in, query_proj, key_proj, value_proj, gate_proj,
    alpha_proj, beta_proj, query_conv, key_conv, value_conv, decay_log, step_bias, gain_head,
    out_proj, gain_mid, ffn_gate, ffn_up, ffn_down,
):
    groups = lax.axis_size(GROUP)
    tp_count = lax.axis_size("tp")
    tp_place = lax.axis_index("tp")
    group = lax.axis_index(GROUP)
    micros, rows, width = tokens.shape
    packs = lengths.shape[1]
    all_rows = order.shape[1]
    pack_rows = all_rows // packs
    assert micros * packs == groups and pack_rows == tp_count * rows and tp_count == 4
    assert rows // groups % 2 == 0
    share = rows // groups
    heads = decay_log.shape[0]
    spans = query_conv.shape[0]
    key_size = query_conv.shape[2] * groups
    value_size = value_conv.shape[2] * groups
    sizes = (heads, key_size, value_size)
    key_cols = heads * key_size
    value_cols = heads * value_size
    own = width // groups
    my_micro = group // packs
    my_pack = group % packs

    strict_up = jnp.triu(jnp.ones((rows, rows), BF16), 1)
    mine = (order // rows == group).reshape(micros * packs * tp_count, rows)
    rank = jnp.dot(mine.astype(BF16), strict_up, preferred_element_type=F32).astype(jnp.int32)
    rank = rank.reshape(micros, packs, tp_count, rows)
    ids = jnp.arange(packs * tp_count, dtype=jnp.int32).reshape(packs, tp_count, 1)
    send_slot = (ids * share + rank).reshape(micros, 1, all_rows)
    held = rows + PAD
    pack_id = jnp.arange(groups, dtype=jnp.int32).reshape(micros, packs, 1, 1)
    tp_id = jnp.arange(tp_count, dtype=jnp.int32).reshape(tp_count, 1)
    back_slot = (relayed_block(tp_place, tp_id) * held + pack_id * share + rank).reshape(micros, 1, all_rows)
    local = group * rows + jnp.arange(rows, dtype=jnp.int32)
    hit = order[:, None, :] == local[None, :, None]
    send_at = jnp.sum(jnp.where(hit, send_slot, 0), axis=2)
    back_at = jnp.sum(jnp.where(hit, back_slot, 0), axis=2).reshape(micros * rows)
    row_ids = jnp.arange(rows, dtype=jnp.int32)
    half = share // 2
    near_ranges = tp_count // 2
    near_rows = groups * near_ranges * share
    far_rows = groups * half
    send_rank = send_at % share
    send_range = send_at // share % tp_count
    send_pack = send_at // (share * tp_count)

    def pick_rows(slot, wanted, count):
        ids = jnp.arange(count, dtype=jnp.int32)[None, :, None]
        return ((ids == slot[:, None, :]) & wanted[:, None, :]).astype(BF16)

    send_pick = pick_rows(send_at, send_at >= 0, rows)
    near_pick = pick_rows(
        send_pack * (near_ranges * share) + send_range * share + send_rank,
        send_range < near_ranges,
        packs * near_ranges * share,
    )
    far_pick = pick_rows(
        send_pack * half + send_rank % half,
        (send_range == near_ranges + tp_place // 2) & (send_rank // half == tp_place % 2),
        packs * half,
    )
    back_ids = jnp.arange(RELAYED * held, dtype=jnp.int32)
    back_pick = (back_at[:, None] == back_ids[None, :]).astype(BF16)

    def picked(pick, values):
        return jnp.einsum("msi,mid->msd", pick, values, preferred_element_type=F32).astype(BF16)

    def exchange(sent):
        return lax.all_to_all(sent, GROUP, split_axis=0, concat_axis=0, tiled=True)

    def to_sources(values):
        sent = jnp.dot(return_pick, values, preferred_element_type=F32).astype(BF16)
        return sent.reshape(groups, share, width)

    def to_given(blocks):
        full = jnp.concatenate(blocks, axis=0)
        values = jnp.dot(back_pick, full, preferred_element_type=F32).astype(BF16)
        return values.reshape(micros, rows, width), full

    small = jnp.concatenate(
        [
            gain_in,
            gain_mid,
            query_conv.reshape(-1),
            key_conv.reshape(-1),
            value_conv.reshape(-1),
            gain_head,
        ],
        axis=0,
    )
    small_size = small.shape[0]
    small = jnp.pad(small, (0, width - small_size))
    gates_pad = jnp.zeros((own, LANES - 2 * heads), BF16)
    x_sent = picked(far_pick, tokens).reshape(far_rows, width)
    query_proj, key_proj, value_proj, gate_proj = together(
        (query_proj, key_proj, value_proj, gate_proj, x_sent)
    )[:4]
    mixer_weight = lax.all_gather(
        jnp.concatenate(
            [query_proj, key_proj, value_proj, gate_proj, alpha_proj, beta_proj, gates_pad], axis=1
        ),
        GROUP, axis=0, tiled=True,
    )
    small_count = PAD - half % PAD
    x_moved, near_sent = together(
        (
            exchange(
                jnp.concatenate(
                    [
                        x_sent.reshape(groups, half, width),
                        jnp.broadcast_to(small[None, None, :], (groups, small_count, width)),
                    ],
                    axis=1,
                )
            ),
            picked(near_pick, tokens).reshape(near_rows, width),
        )
    )
    near_moved = exchange(near_sent)
    far_own = x_moved[:, :half].reshape(far_rows, width)
    x_near = relay_first(far_own)
    x_moved, order, lengths = together((x_moved, order, lengths, *x_near))[:3]
    extras = x_moved[:, half, :small_size].astype(F32)

    pack_order = lax.dynamic_slice(order, (my_micro, my_pack * pack_rows), (1, pack_rows))
    source = (pack_order // rows).reshape(tp_count, rows)
    from_each = (source[:, :, None] == jnp.arange(groups, dtype=jnp.int32)).astype(BF16)
    before = jnp.einsum(
        "qp,tqg->tpg", strict_up, from_each, preferred_element_type=F32
    )
    source_rank = jnp.sum(before * from_each.astype(F32), axis=2).astype(jnp.int32)
    relayer = 2 * (tp_id - near_ranges) + source_rank // half
    arrive_at = jnp.where(
        tp_id < near_ranges,
        source * (near_ranges * share) + tp_id * share + source_rank,
        near_rows
        + relayed_block(tp_place, relayer) * far_rows
        + source * half
        + source_rank % half,
    )
    arrive_ids = jnp.arange(near_rows + RELAYED * far_rows, dtype=jnp.int32)
    arrive_pick = (arrive_at.reshape(pack_rows, 1) == arrive_ids[None, :]).astype(BF16)
    pack_ids = jnp.arange(pack_rows, dtype=jnp.int32)
    full_at = source * (tp_count * share) + tp_id * share + source_rank
    place_pick = (full_at.reshape(pack_rows, 1) == pack_ids[None, :]).astype(BF16)
    return_at = lax.dynamic_slice(source * share + source_rank, (tp_place, 0), (1, rows))
    return_pick = (row_ids[:, None] == return_at).astype(BF16)

    x_all = jnp.concatenate((near_moved, far_own, *x_near, *relay_second(*x_near)), axis=0)
    x_low = jnp.dot(arrive_pick, x_all, preferred_element_type=F32).astype(BF16)
    dy_sent = picked(send_pick, cotangent).reshape(pack_rows, width)
    out_proj, ffn_down = together((out_proj, ffn_down, x_low))[:2]
    out_weight = lax.all_gather(out_proj.T, GROUP, axis=0, tiled=True)
    down_weight = lax.all_gather(ffn_down.T, GROUP, axis=0, tiled=True)
    pair_shard = jnp.concatenate(together((ffn_gate, ffn_up, x_moved))[:2], axis=1)

    tail_at = 2 * key_cols + 2 * value_cols
    gain_in_full = extras[:, :own].reshape(1, width)
    gain_mid_full = extras[:, own : 2 * own].reshape(1, width)

    def taps_of(start, weight):
        flat = extras[:, start : start + weight.size]
        flat = flat.reshape(groups, spans, heads, weight.shape[2])
        return jnp.transpose(flat, (1, 2, 0, 3)).reshape(spans, -1), start + weight.size

    query_taps, at = taps_of(2 * own, query_conv)
    key_taps, at = taps_of(at, key_conv)
    value_taps, at = taps_of(at, value_conv)
    taps = jnp.pad(
        jnp.concatenate([query_taps, key_taps, value_taps], axis=1), ((0, PAD - spans), (0, 0))
    )
    head_gain = jnp.broadcast_to(extras[:, at:].reshape(1, value_size), (PAD, value_size))
    par = jnp.zeros((PAD, LANES), F32)
    par = par.at[0, :heads].set(-jnp.exp(decay_log)).at[1, :heads].set(step_bias)
    length_row = lax.dynamic_slice(
        lengths, (my_micro, my_pack, 0), (1, 1, lengths.shape[2])
    ).reshape(-1)
    info, seg_rows = place_arrays(length_row, pack_rows)

    x_float = x_low.astype(F32)
    rate_in = lax.rsqrt(jnp.mean(x_float * x_float, axis=1, keepdims=True) + square_eps)
    normed_in = (x_float * rate_in * gain_in_full).astype(BF16)
    proj = dot_nn(normed_in, mixer_weight)
    dy_all = exchange(together((dy_sent, proj))[0])
    normed_low, *saved = delta_forward(proj, info, seg_rows, par, taps, head_gain, sizes)

    mixed_part = dot_nt(normed_low, out_weight).astype(BF16)
    *mixer_came, dy_all = together((*sum_first(mixed_part, rows), dy_all))
    from_after, from_before = sum_second(*sum_middle(mixed_part, rows, mixer_came))
    pair_weight = lax.all_gather(pair_shard, GROUP, axis=0, tiled=True)
    dy_low = jnp.dot(place_pick, dy_all, preferred_element_type=F32).astype(BF16)
    own_f32 = jax.ShapeDtypeStruct((rows, width), F32)
    own_low = jax.ShapeDtypeStruct((rows, width), BF16)
    gain_part = jax.ShapeDtypeStruct((PAD, width), F32)
    place = tp_place.reshape(1)
    gain_in_8 = jnp.broadcast_to(gain_in_full, (PAD, width))
    gain_mid_8 = jnp.broadcast_to(gain_mid_full, (PAD, width))
    hidden_in, mid_own = row_parts(
        middle_kernel,
        place,
        [
            ("all", mixed_part),
            ("own", from_after),
            ("own", from_before),
            ("all", x_low),
            ("one", gain_mid_8),
        ],
        [("own", own_f32), ("own", own_low)],
        rows,
    )
    mid_low = copy_rows_ordered(mid_own)
    grad_hidden = dot_nn(dy_low, down_weight)
    mid_low, grad_hidden = together((mid_low, grad_hidden))
    units = ffn_gate.shape[1]
    both = dot_nn(mid_low, pair_weight)
    gate_value, up_value = both[:, :units], both[:, units:]
    gate_sig = sigmoid(gate_value)
    gate_act = gate_value * gate_sig
    hidden_low = (gate_act * up_value).astype(BF16)
    pair_grad = jnp.concatenate(
        [
            (grad_hidden * up_value * (gate_sig * (1.0 + gate_value * (1.0 - gate_sig)))).astype(BF16),
            (grad_hidden * gate_act).astype(BF16),
        ],
        axis=1,
    )
    back_part = dot_nt(pair_grad, pair_weight).astype(BF16)
    back_part, pair_late, hidden_late, mid_late = together(
        (back_part, pair_grad, hidden_low, mid_low)
    )
    back_moved = deal(back_part, "b")
    ffn_part = dot_nt(hidden_late, down_weight).astype(BF16)
    grad_down_part = dot_tn(dy_low, hidden_late).astype(BF16)
    grad_pair_part = dot_tn(mid_late, pair_late).astype(BF16)
    back_moved, ffn_part, grad_down_part, grad_pair_part = together(
        (back_moved, ffn_part, grad_down_part, grad_pair_part)
    )

    def owners(value):
        return lax.psum_scatter(value, GROUP, scatter_dimension=0, tiled=True)

    hidden_grad, mix_own, grad_mid_gain = row_parts(
        middle_back_kernel,
        place,
        [("own", back_moved), ("own", hidden_in), ("all", dy_low), ("one", gain_mid_8)],
        [("own", own_f32), ("own", own_low), ("one", gain_part)],
        rows,
    )
    grad_mid_gain = jnp.sum(grad_mid_gain, axis=0)
    mix_low = copy_rows_ordered(mix_own)
    mix_low, ffn_part, grad_down = together((mix_low, ffn_part, owners(grad_down_part)))
    dnormed = dot_nn(mix_low, out_weight)
    grad_proj, conv_grad, head_gain_grad, decay_grads = delta_backward(
        proj, info, seg_rows, par, taps, head_gain, saved, dnormed, sizes
    )
    first_part = dot_nt(grad_proj, mixer_weight).astype(BF16)
    result_moved = deal(ffn_part, "y")
    first_part, proj_late, mix_late, normed_late, result_moved, grad_pair_part = together(
        (first_part, grad_proj, mix_low, normed_low, result_moved, grad_pair_part)
    )
    grad_pair = owners(grad_pair_part)
    grad_out_part = dot_tn(mix_late, normed_late).astype(BF16)
    grad_mixer_part = dot_tn(normed_in, proj_late).astype(BF16)
    grad_mixer_part = jnp.concatenate([grad_mixer_part, grad_out_part], axis=1)
    *first_came, grad_mixer_part = together((*sum_first(first_part, rows), grad_mixer_part))
    first_middle = sum_middle(first_part, rows, first_came)
    late_after, late_before = sum_second(*first_middle)
    result_moved = together((result_moved, *first_middle))[0]
    result = (hidden_in + add_dealt(result_moved, "y")).astype(BF16)
    result_back = exchange(to_sources(result)).reshape(rows, width)
    result_back = jnp.pad(result_back, ((0, PAD), (0, 0)))
    result_near = relay_first(result_back)

    token_grad, grad_in_gain = row_parts(
        first_back_kernel,
        place,
        [
            ("all", first_part),
            ("own", late_after),
            ("own", late_before),
            ("own", hidden_grad),
            ("all", x_low),
            ("one", gain_in_8),
        ],
        [("own", own_low), ("one", gain_part)],
        rows,
    )
    grad_in_gain = jnp.sum(grad_in_gain, axis=0)

    conv_sum = jnp.sum(conv_grad.reshape(spans, PAD, -1), axis=1)

    def taps_to(value, size):
        parted = value.reshape(spans, heads, groups, size // groups)
        return jnp.transpose(parted, (2, 0, 1, 3)).reshape(groups, -1)

    gain_sum = jnp.sum(head_gain_grad.reshape(PAD * heads, value_size), axis=0)
    decay_sums = jnp.sum(decay_grads.reshape(2, PAD, LANES), axis=1)[:, :heads].reshape(1, -1)
    parts = [
        grad_in_gain.reshape(groups, own),
        grad_mid_gain.reshape(groups, own),
        gain_sum.reshape(groups, -1),
        taps_to(conv_sum[:, :key_cols], key_size),
        taps_to(conv_sum[:, key_cols : 2 * key_cols], key_size),
        taps_to(conv_sum[:, 2 * key_cols :], value_size),
        jnp.broadcast_to(decay_sums, (groups, decay_sums.shape[1])),
    ]
    lens = [part.shape[1] for part in parts]
    packed = jnp.concatenate(parts, axis=1)
    packed = jnp.pad(packed, ((0, 0), (0, width - packed.shape[1])))
    extra = jnp.pad(pair_rows(packed), ((0, 0), (0, PAD - 2), (0, 0)))
    grad_sent = to_sources(token_grad)
    came = exchange(jnp.concatenate([grad_sent, extra], axis=1))
    before, after, grad_down = together((*result_near, grad_down, grad_sent))[:3]
    result_far = relay_second(before, after)
    summed = jnp.sum(came[:, share : share + 2].astype(F32), axis=(0, 1))
    block = jnp.concatenate(
        [
            came[:, :share].reshape(rows, width),
            jnp.pad(pair_rows(summed), ((0, PAD - 2), (0, 0))),
        ],
        axis=0,
    )
    result_far = together((*result_far, block))[:3]
    mixed, unused = to_given((result_back, before, after, *result_far))
    grad_tokens, full = to_given(relayed_blocks(block))
    *mixer_grads, gates_turned, grad_out = widened(
        owners(grad_mixer_part), [key_cols, key_cols, value_cols, value_cols]
    )
    mixer_grads += [gates_turned[:heads].T, gates_turned[heads : 2 * heads].T]
    grad_pair = grad_pair.astype(F32)
    grad_down = grad_down.astype(F32).T

    tp_summed = jnp.sum(
        full.reshape(RELAYED, held, width)[:, rows : rows + 2].astype(F32), axis=(0, 1)
    )
    pieces = []
    offset = 0
    for index, length in enumerate(lens):
        origin = tp_summed if index < 3 else summed
        pieces.append(origin[offset : offset + length])
        offset += length
    decay_pair = pieces[6].reshape(2, heads)
    return (
        mixed,
        grad_tokens,
        pieces[0],
        *mixer_grads,
        pieces[3].reshape(query_conv.shape),
        pieces[4].reshape(key_conv.shape),
        pieces[5].reshape(value_conv.shape),
        decay_pair[0],
        decay_pair[1],
        pieces[2],
        grad_out,
        pieces[1],
        grad_pair[:, :units],
        grad_pair[:, units:],
        grad_down,
    )


def solution(mesh):
    in_specs = (
        P(None, ("fsdp", "ctx"), None),
        P(None, ("fsdp", "ctx"), None),
        P(),
        P(),
        P(("fsdp", "ctx")),
        P(("fsdp", "ctx"), "tp"),
        P(("fsdp", "ctx"), "tp"),
        P(("fsdp", "ctx"), "tp"),
        P(("fsdp", "ctx"), "tp"),
        P(("fsdp", "ctx"), "tp"),
        P(("fsdp", "ctx"), "tp"),
        P(None, "tp", ("fsdp", "ctx")),
        P(None, "tp", ("fsdp", "ctx")),
        P(None, "tp", ("fsdp", "ctx")),
        P("tp"),
        P("tp"),
        P(("fsdp", "ctx")),
        P("tp", ("fsdp", "ctx")),
        P(("fsdp", "ctx")),
        P(("fsdp", "ctx"), "tp"),
        P(("fsdp", "ctx"), "tp"),
        P("tp", ("fsdp", "ctx")),
    )
    out_specs = (
        P(None, ("fsdp", "ctx"), None),
        P(None, ("fsdp", "ctx"), None),
        P(("fsdp", "ctx")),
        P(("fsdp", "ctx"), "tp"),
        P(("fsdp", "ctx"), "tp"),
        P(("fsdp", "ctx"), "tp"),
        P(("fsdp", "ctx"), "tp"),
        P(("fsdp", "ctx"), "tp"),
        P(("fsdp", "ctx"), "tp"),
        P(None, "tp", ("fsdp", "ctx")),
        P(None, "tp", ("fsdp", "ctx")),
        P(None, "tp", ("fsdp", "ctx")),
        P("tp"),
        P("tp"),
        P(("fsdp", "ctx")),
        P("tp", ("fsdp", "ctx")),
        P(("fsdp", "ctx")),
        P(("fsdp", "ctx"), "tp"),
        P(("fsdp", "ctx"), "tp"),
        P("tp", ("fsdp", "ctx")),
    )
    return jax.shard_map(
        per_device, mesh=mesh, in_specs=in_specs, out_specs=out_specs, check_vma=False
    )
```

```python
import functools
import jax
import jax.numpy as jnp
from jax import lax
from jax.sharding import PartitionSpec as P
from jax.experimental import pallas as pl
from jax.experimental.pallas import tpu as pltpu

CHUNK = 128
LANES = 128
PAD = 8
square_eps = 1e-05
unit_eps = 1e-06
F32 = jnp.float32
BF16 = jnp.bfloat16


def dot_nn(left, right):
    return lax.dot_general(left, right, (((1,), (0,)), ((), ())), preferred_element_type=F32)


def dot_nt(left, right):
    return lax.dot_general(left, right, (((1,), (1,)), ((), ())), preferred_element_type=F32)


def dot_tn(left, right):
    return lax.dot_general(left, right, (((0,), (0,)), ((), ())), preferred_element_type=F32)


def halves(value):
    high = value.astype(BF16)
    return high, (value - high.astype(F32)).astype(BF16)


def dot_fine(left, right):
    left_high, left_low = halves(left)
    right_high, right_low = halves(right)
    return (
        dot_nn(left_high, right_high)
        + dot_nn(left_high, right_low)
        + dot_nn(left_low, right_high)
    )


def sum_by(mask, value):
    high, rest = halves(value)
    middle, low = halves(value - high.astype(F32))
    return dot_nn(mask, high) + dot_nn(mask, middle) + dot_nn(mask, low)


def sigmoid(value):
    return 1.0 / (1.0 + jnp.exp(-value))


def softplus(value):
    return jnp.maximum(value, 0.0) + jnp.log1p(jnp.exp(-jnp.abs(value)))


def low_dot(left, right):
    return dot_nn(left.astype(BF16), right.astype(BF16))


def inverses_lower(lower_mats, row_id, col_id):
    size = row_id.shape[0]

    def level(width):
        same = row_id // (2 * width) == col_id // (2 * width)
        return same & ((row_id // width) % 2 == 1) & ((col_id // width) % 2 == 0)

    unit = jnp.where(row_id == col_id, 1.0, 0.0)
    mask = level(1)
    results = [unit - jnp.where(mask, mat, 0.0) for mat in lower_mats]
    width = 2
    while width < size:
        mask = level(width)
        parts = [low_dot(r, jnp.where(mask, mat, 0.0)) for r, mat in zip(results, lower_mats)]
        results = [r - low_dot(p, r) for p, r in zip(parts, results)]
        width *= 2
    rests = [unit - r - dot_fine(mat, r) for r, mat in zip(results, lower_mats)]
    return [r + low_dot(r, rest) for r, rest in zip(results, rests)]


def in_turn(bodies):
    asked = [next(body) for body in bodies]
    while asked:
        made = asked[0][0]([item[1] for item in asked]) if asked[0] else [None] * len(asked)
        following = []
        for body, value in zip(bodies, made):
            try:
                following.append(body.send(value))
            except StopIteration:
                pass
        asked = following


def chunk_basics(gates, par, info, seg_row, row_id, col_id, lane_id, head_count):
    step = gates + par[1:2, :]
    log_decay = jnp.where(lane_id < head_count, par[0:1, :] * softplus(step), 0.0)
    beta_raw = sigmoid(gates)
    valid = info[:, 1:2]
    lower = row_id >= col_id
    cumulative = sum_by(jnp.where(lower, 1.0, 0.0).astype(BF16), log_decay)
    both = jnp.where(lane_id < head_count, cumulative, beta_raw * valid)
    turned = jnp.transpose(both)
    inner = lower & (info[:, 0:1] == seg_row)
    return step, log_decay, beta_raw, both, turned, inner


def activations(ext, taps, masks, start, stop, rows):
    value = taps[3:4, start:stop] * ext[PAD : PAD + rows, start:stop]
    for distance in (1, 2, 3):
        shifted = ext[PAD - distance : PAD - distance + rows, start:stop]
        value = value + masks[distance - 1] * (taps[3 - distance : 4 - distance, start:stop] * shifted)
    return value


def forward_kernel(
    head_count, key_size, value_size,
    proj, info_ref, segr, par_ref, taps, gain_ref,
    normed_out, state_out, inverse_out, pseudo_out, output_out,
    state, ext,
):
    rows = proj.shape[0]
    width = head_count * (2 * key_size + value_size)
    gate_at = width
    tail_at = width + head_count * value_size

    @pl.when(pl.program_id(0) == 0)
    def start():
        state[...] = jnp.zeros_like(state)
        ext[0:PAD, :] = jnp.zeros((PAD, width), F32)

    ext[PAD : PAD + rows, :] = proj[:, 0:width]
    info = info_ref[...]
    row_id = lax.broadcasted_iota(jnp.int32, (rows, rows), 0)
    col_id = lax.broadcasted_iota(jnp.int32, (rows, rows), 1)
    lane_id = lax.broadcasted_iota(jnp.int32, (rows, LANES), 1)
    masks = tuple(info[:, 1 + d : 2 + d] for d in (1, 2, 3))
    valid = info[:, 1:2]
    unused, log_decay, beta_raw, both, turned, inner = chunk_basics(
        proj[:, tail_at : tail_at + LANES], par_ref[...], info, segr[0:1, :],
        row_id, col_id, lane_id, head_count,
    )
    carried_mask = info[:, 8:9]
    tail_mask = info[:, 9:10]
    strict = row_id > col_id
    key_at = head_count * key_size
    value_at = 2 * key_at
    def one_head(head):
        ks = key_size
        vs = value_size
        act_q = activations(ext, taps, masks, head * ks, (head + 1) * ks, rows)
        act_k = activations(ext, taps, masks, key_at + head * ks, key_at + (head + 1) * ks, rows)
        act_v = activations(ext, taps, masks, value_at + head * vs, value_at + (head + 1) * vs, rows)
        cq = act_q * sigmoid(act_q)
        ck = act_k * sigmoid(act_k)
        values = act_v * sigmoid(act_v)
        query = cq * (lax.rsqrt(jnp.sum(cq * cq, axis=1, keepdims=True) + unit_eps) * ks ** -0.5)
        key = ck * lax.rsqrt(jnp.sum(ck * ck, axis=1, keepdims=True) + unit_eps)
        yield
        qb = query.astype(BF16)
        kb = key.astype(BF16)
        cum = both[:, head : head + 1]
        beta = both[:, head_count + head : head_count + head + 1]
        cum_row = turned[head : head + 1, :]
        beta_row = turned[head_count + head : head_count + head + 1, :]
        decays = jnp.where(inner, jnp.exp(jnp.minimum(cum - cum_row, 0.0)), 0.0)
        lower_mat = jnp.where(strict, decays * dot_nt(kb, kb) * beta_row, 0.0)
        inverse = yield (lambda mats: inverses_lower(mats, row_id, col_id)), lower_mat
        yield
        carried = jnp.exp(cum) * carried_mask
        last = cum[rows - 1 : rows, :]
        tail = jnp.exp(last - cum) * tail_mask
        keep = carried[rows - 1 : rows, :]
        before = state[head]
        sb = before.astype(BF16)
        state_out[0, head] = sb
        target = values - carried * dot_nn(kb, sb)
        ib = inverse.astype(BF16)
        pseudo = dot_nn(ib, target.astype(BF16))
        inverse_out[0, head] = ib
        pseudo_out[:, head * vs : (head + 1) * vs] = pseudo
        yield
        weighted = beta * pseudo
        mix = decays * dot_nt(qb, kb)
        output = carried * dot_nn(qb, sb) + dot_nn(mix.astype(BF16), weighted.astype(BF16))
        output_out[:, head * vs : (head + 1) * vs] = output
        state[head] = keep * before + dot_tn(kb, (tail * weighted).astype(BF16))
        yield
        gate = proj[:, gate_at + head * vs : gate_at + (head + 1) * vs]
        scale = lax.rsqrt(jnp.mean(output * output, axis=1, keepdims=True) + square_eps)
        normed = output * scale * gain_ref[0:1, :] * (gate * sigmoid(gate)) * valid
        normed_out[:, head * vs : (head + 1) * vs] = normed.astype(BF16)

    in_turn([one_head(head) for head in range(head_count)])
    ext[0:PAD, :] = ext[rows : rows + PAD, :]


def backward_kernel(
    head_count, key_size, value_size,
    proj, prior, info_ref, segr, par_ref, taps, gain_ref,
    state_in, inverse_in, pseudo_in, output_in, dnormed,
    grad_out, conv_out, gain_out, small_out,
    dstate, ext, dext,
):
    rows = proj.shape[0]
    width = head_count * (2 * key_size + value_size)
    gate_at = width
    tail_at = width + head_count * value_size
    place = pl.program_id(0)
    count = pl.num_programs(0)

    @pl.when(place == 0)
    def start():
        dstate[...] = jnp.zeros_like(dstate)
        dext[rows : rows + PAD, :] = jnp.zeros((PAD, width), F32)
        conv_out[...] = jnp.zeros_like(conv_out)
        gain_out[...] = jnp.zeros_like(gain_out)
        small_out[...] = jnp.zeros_like(small_out)

    first = place == count - 1
    ext[0:PAD, :] = jnp.where(first, 0.0, prior[:, 0:width])
    ext[PAD : PAD + rows, :] = proj[:, 0:width]
    info = info_ref[...]
    row_id = lax.broadcasted_iota(jnp.int32, (rows, rows), 0)
    col_id = lax.broadcasted_iota(jnp.int32, (rows, rows), 1)
    lane_id = lax.broadcasted_iota(jnp.int32, (rows, LANES), 1)
    masks = tuple(info[:, 1 + d : 2 + d] for d in (1, 2, 3))
    later = tuple(info[:, 4 + d : 5 + d] for d in (1, 2, 3))
    valid = info[:, 1:2]
    step, log_decay, beta_raw, both, turned, inner = chunk_basics(
        proj[:, tail_at : tail_at + LANES], par_ref[...], info, segr[0:1, :],
        row_id, col_id, lane_id, head_count,
    )
    carried_mask = info[:, 8:9]
    tail_mask = info[:, 9:10]
    strict = row_id > col_id
    last_row = lax.broadcasted_iota(jnp.int32, (rows, 1), 0) == rows - 1
    row_of = lax.broadcasted_iota(jnp.int32, (LANES, rows), 0)
    ks = key_size
    vs = value_size
    key_at = head_count * ks
    value_at = 2 * key_at
    sums = {}

    def fold(value):
        return jnp.sum(value.reshape(rows // PAD, PAD, value.shape[1]), axis=0)

    def conv_back(da, start, stop):
        dext[0:rows, start:stop] = da
        back = taps[3:4, start:stop] * da
        conv_out[3 * PAD : 4 * PAD, start:stop] += fold(da * ext[PAD : PAD + rows, start:stop])
        for d in (1, 2, 3):
            back = back + later[d - 1] * (taps[3 - d : 4 - d, start:stop] * dext[d : d + rows, start:stop])
            shifted = ext[PAD - d : PAD - d + rows, start:stop]
            conv_out[(3 - d) * PAD : (4 - d) * PAD, start:stop] += fold(masks[d - 1] * da * shifted)
        grad_out[:, start:stop] = back.astype(BF16)

    def one_head(head):
        act_q = activations(ext, taps, masks, head * ks, (head + 1) * ks, rows)
        act_k = activations(ext, taps, masks, key_at + head * ks, key_at + (head + 1) * ks, rows)
        act_v = activations(ext, taps, masks, value_at + head * vs, value_at + (head + 1) * vs, rows)
        sig_q, sig_k, sig_v = sigmoid(act_q), sigmoid(act_k), sigmoid(act_v)
        cq, ck, values = act_q * sig_q, act_k * sig_k, act_v * sig_v
        rate_q = lax.rsqrt(jnp.sum(cq * cq, axis=1, keepdims=True) + unit_eps)
        rate_k = lax.rsqrt(jnp.sum(ck * ck, axis=1, keepdims=True) + unit_eps)
        unit_q = cq * rate_q
        query = unit_q * ks ** -0.5
        key = ck * rate_k
        yield
        qb = query.astype(BF16)
        kb = key.astype(BF16)
        cum = both[:, head : head + 1]
        beta = both[:, head_count + head : head_count + head + 1]
        cum_row = turned[head : head + 1, :]
        beta_row = turned[head_count + head : head_count + head + 1, :]
        decays = jnp.where(inner, jnp.exp(jnp.minimum(cum - cum_row, 0.0)), 0.0)
        carried = jnp.exp(cum) * carried_mask
        tail = jnp.exp(cum[rows - 1 : rows, :] - cum) * tail_mask
        keep = carried[rows - 1 : rows, :]
        yield
        sb = state_in[0, head]
        before = sb.astype(F32)
        ib = inverse_in[0, head]
        pseudo = pseudo_in[:, head * vs : (head + 1) * vs]
        output = output_in[:, head * vs : (head + 1) * vs]
        gate = proj[:, gate_at + head * vs : gate_at + (head + 1) * vs]
        given = dnormed[:, head * vs : (head + 1) * vs] * valid
        gain = gain_ref[0:1, :]
        scale = lax.rsqrt(jnp.mean(output * output, axis=1, keepdims=True) + square_eps)
        unit_o = output * scale
        sig_g = sigmoid(gate)
        silu_g = gate * sig_g
        dunit = given * gain * silu_g
        doutput = scale * (dunit - unit_o * jnp.mean(unit_o * dunit, axis=1, keepdims=True))
        dgate = given * unit_o * gain * (sig_g * (1.0 + gate * (1.0 - sig_g)))
        gain_out[:, head * vs : (head + 1) * vs] += fold(given * unit_o * silu_g)
        grad_out[:, gate_at + head * vs : gate_at + (head + 1) * vs] = dgate.astype(BF16)
        yield
        dob = doutput.astype(BF16)
        weighted = beta * pseudo
        wb = weighted.astype(BF16)
        gram = dot_nt(kb, kb)
        cross = dot_nt(qb, kb)
        mix = decays * cross
        yield
        after = dstate[head]
        ab = after.astype(BF16)
        from_state = dot_nn(kb, ab)
        dweighted = dot_tn(mix.astype(BF16), dob) + tail * from_state
        dbeta = jnp.sum(dweighted * pseudo, axis=1, keepdims=True)
        yield
        dtarget = dot_tn(ib, (beta * dweighted).astype(BF16))
        dtb = dtarget.astype(BF16)
        read = dot_nn(kb, sb)
        yield
        dcarried = jnp.sum(doutput * dot_nn(qb, sb), axis=1, keepdims=True) - jnp.sum(
            dtarget * read, axis=1, keepdims=True
        )
        dtail = jnp.sum(weighted * from_state, axis=1, keepdims=True)
        dkeep = jnp.sum(jnp.sum(after * before, axis=1, keepdims=True), axis=0, keepdims=True)
        cdo = (carried * doutput).astype(BF16)
        cdt = (carried * dtarget).astype(BF16)
        dstate[head] = keep * after + dot_tn(qb, cdo) - dot_tn(kb, cdt)
        yield
        dmix = dot_nt(dob, wb)
        dcross = (dmix * decays).astype(BF16)
        dlower = jnp.where(strict, -dot_nt(dtb, pseudo.astype(BF16)), 0.0) * decays
        dgram = (dlower * beta_row).astype(BF16)
        plain = dlower * gram
        inner_grad = dmix * mix + plain * beta_row
        yield
        dquery = dot_nt(cdo, sb) + dot_nn(dcross, kb)
        dkey = (
            dot_tn(dcross, qb)
            + dot_nn(dgram, kb)
            + dot_tn(dgram, kb)
            + dot_nt((tail * weighted).astype(BF16), ab)
            - dot_nt(cdt, sb)
        )
        yield
        dlast = jnp.sum(dtail * tail, axis=0, keepdims=True) + dkeep * keep
        dcum_col = (
            jnp.sum(inner_grad, axis=1, keepdims=True)
            + dcarried * carried
            - dtail * tail
            + jnp.where(last_row, dlast, 0.0)
        )
        sums[head] = (
            dcum_col,
            dbeta,
            -jnp.sum(inner_grad, axis=0, keepdims=True),
            jnp.sum(plain, axis=0, keepdims=True),
        )
        yield
        dq_scaled = dquery * ks ** -0.5
        dcq = (dq_scaled - unit_q * jnp.sum(unit_q * dq_scaled, axis=1, keepdims=True)) * rate_q
        dck = (dkey - key * jnp.sum(key * dkey, axis=1, keepdims=True)) * rate_k
        conv_back(dcq * (sig_q * (1.0 + act_q * (1.0 - sig_q))), head * ks, (head + 1) * ks)
        yield
        conv_back(
            dck * (sig_k * (1.0 + act_k * (1.0 - sig_k))), key_at + head * ks, key_at + (head + 1) * ks
        )
        conv_back(
            dtarget * (sig_v * (1.0 + act_v * (1.0 - sig_v))),
            value_at + head * vs,
            value_at + (head + 1) * vs,
        )

    for head in range(head_count):
        in_turn([one_head(head)])
    dcum = jnp.zeros((rows, LANES), F32)
    dturned = jnp.zeros((LANES, rows), F32)
    for head, (dcum_col, dbeta, dcum_row, dbeta_row) in sums.items():
        dcum = jnp.where(lane_id == head, dcum_col, dcum)
        dcum = jnp.where(lane_id == head_count + head, dbeta, dcum)
        dturned = jnp.where(row_of == head, dcum_row, dturned)
        dturned = jnp.where(row_of == head_count + head, dbeta_row, dturned)
    dboth = dcum + jnp.transpose(dturned)
    upper = jnp.where(row_id <= col_id, 1.0, 0.0).astype(BF16)
    dlog = sum_by(upper, jnp.where(lane_id < head_count, dboth, 0.0))
    dalpha = dlog * par_ref[0:1, :] * sigmoid(step)
    dbeta_raw = dboth * valid * beta_raw * (1.0 - beta_raw)
    tail_grad = jnp.where(
        lane_id < head_count, dalpha, jnp.where(lane_id < 2 * head_count, dbeta_raw, 0.0)
    )
    grad_out[:, tail_at : tail_at + LANES] = tail_grad.astype(BF16)
    small_out[0:PAD, :] += fold(dlog * log_decay)
    small_out[PAD : 2 * PAD, :] += fold(jnp.where(lane_id < head_count, dalpha, 0.0))
    dext[rows : rows + PAD, :] = dext[0:PAD, :]


def delta_forward(proj, info, seg_rows, par, taps, gain, sizes):
    head_count, key_size, value_size = sizes
    total, columns = proj.shape
    steps = total // CHUNK
    width = head_count * (2 * key_size + value_size)
    span = head_count * value_size
    whole = lambda a: pl.BlockSpec(a.shape, lambda i: (0, 0))
    by_rows = lambda n: pl.BlockSpec((CHUNK, n), lambda i: (i, 0))
    return pl.pallas_call(
        functools.partial(forward_kernel, head_count, key_size, value_size),
        grid=(steps,),
        in_specs=[
            by_rows(columns),
            by_rows(LANES),
            pl.BlockSpec((PAD, CHUNK), lambda i: (0, i)),
            whole(par),
            whole(taps),
            whole(gain),
        ],
        out_specs=[
            by_rows(span),
            pl.BlockSpec((1, head_count, key_size, value_size), lambda i: (i, 0, 0, 0)),
            pl.BlockSpec((1, head_count, CHUNK, CHUNK), lambda i: (i, 0, 0, 0)),
            by_rows(span),
            by_rows(span),
        ],
        out_shape=[
            jax.ShapeDtypeStruct((total, span), BF16),
            jax.ShapeDtypeStruct((steps, head_count, key_size, value_size), BF16),
            jax.ShapeDtypeStruct((steps, head_count, CHUNK, CHUNK), BF16),
            jax.ShapeDtypeStruct((total, span), F32),
            jax.ShapeDtypeStruct((total, span), F32),
        ],
        scratch_shapes=[
            pltpu.VMEM((head_count, key_size, value_size), F32),
            pltpu.VMEM((CHUNK + PAD, width), F32),
        ],
        compiler_params=pltpu.CompilerParams(vmem_limit_bytes=48 * 1024 * 1024),
        name="delta_forward",
    )(proj, info, seg_rows, par, taps, gain)


def delta_backward(proj, info, seg_rows, par, taps, gain, saved, dnormed, sizes):
    head_count, key_size, value_size = sizes
    total, columns = proj.shape
    steps = total // CHUNK
    width = head_count * (2 * key_size + value_size)
    span = head_count * value_size
    states, inverses, pseudos, outputs = saved
    blocks = CHUNK // PAD
    turn = lambda i: steps - 1 - i
    whole = lambda a: pl.BlockSpec(a.shape, lambda i: (0, 0))
    by_rows = lambda n: pl.BlockSpec((CHUNK, n), lambda i: (turn(i), 0))
    return pl.pallas_call(
        functools.partial(backward_kernel, head_count, key_size, value_size),
        grid=(steps,),
        in_specs=[
            by_rows(columns),
            pl.BlockSpec((PAD, columns), lambda i: (jnp.maximum(turn(i) * blocks - 1, 0), 0)),
            by_rows(LANES),
            pl.BlockSpec((PAD, CHUNK), lambda i: (0, turn(i))),
            whole(par),
            whole(taps),
            whole(gain),
            pl.BlockSpec((1, head_count, key_size, value_size), lambda i: (turn(i), 0, 0, 0)),
            pl.BlockSpec((1, head_count, CHUNK, CHUNK), lambda i: (turn(i), 0, 0, 0)),
            by_rows(span),
            by_rows(span),
            by_rows(span),
        ],
        out_specs=[
            by_rows(columns),
            pl.BlockSpec((4 * PAD, width), lambda i: (0, 0)),
            pl.BlockSpec((PAD, span), lambda i: (0, 0)),
            pl.BlockSpec((2 * PAD, LANES), lambda i: (0, 0)),
        ],
        out_shape=[
            jax.ShapeDtypeStruct((total, columns), BF16),
            jax.ShapeDtypeStruct((4 * PAD, width), F32),
            jax.ShapeDtypeStruct((PAD, span), F32),
            jax.ShapeDtypeStruct((2 * PAD, LANES), F32),
        ],
        scratch_shapes=[
            pltpu.VMEM((head_count, key_size, value_size), F32),
            pltpu.VMEM((CHUNK + PAD, width), F32),
            pltpu.VMEM((CHUNK + PAD, width), F32),
        ],
        compiler_params=pltpu.CompilerParams(vmem_limit_bytes=48 * 1024 * 1024),
        name="delta_backward",
    )(proj, proj, info, seg_rows, par, taps, gain, states, inverses, pseudos, outputs, dnormed)


def middle_kernel(place, own, after, before, x_ref, gain, hidden_out, normed_out):
    mixer = own[...].astype(F32) + after[...].astype(F32) + before[...].astype(F32)
    hidden = mixer + x_ref[...].astype(F32)
    rate = lax.rsqrt(jnp.mean(hidden * hidden, axis=1, keepdims=True) + square_eps)
    hidden_out[...] = hidden
    normed_out[...] = (hidden * rate * gain[0:1, :]).astype(BF16)


def norm_back(grad, value, gain):
    rate = lax.rsqrt(jnp.mean(value * value, axis=1, keepdims=True) + square_eps)
    scaled = grad * gain
    inner = jnp.mean(value * scaled, axis=1, keepdims=True)
    return rate * scaled - rate * rate * rate * value * inner, grad * value * rate


def rows_summed(value):
    return jnp.sum(value.reshape(value.shape[0] // PAD, PAD, value.shape[1]), axis=0)


def middle_back_kernel(place, moved, hidden, dy_ref, gain, grad_out, low_out, gain_out):
    @pl.when(pl.program_id(0) == 0)
    def start():
        gain_out[...] = jnp.zeros_like(gain_out)

    back, part = norm_back(moved[...].astype(F32), hidden[...], gain[0:1, :])
    grad = dy_ref[...].astype(F32) + back
    grad_out[...] = grad
    low_out[...] = grad.astype(BF16)
    gain_out[...] += rows_summed(part)


def first_back_kernel(place, own, after, before, late, x_ref, gain, grad_out, gain_out):
    @pl.when(pl.program_id(0) == 0)
    def start():
        gain_out[...] = jnp.zeros_like(gain_out)

    moved = own[...].astype(F32) + after[...].astype(F32) + before[...].astype(F32)
    back, part = norm_back(moved, x_ref[...].astype(F32), gain[0:1, :])
    grad_out[...] = (late[...] + back).astype(BF16)
    gain_out[...] += rows_summed(part)


def row_parts(kernel, place, arrays, outs, rows):
    part = 48 if rows % 48 == 0 else rows
    steps = rows // part

    def spec(kind, shape):
        if kind == "own":
            return pl.BlockSpec((part, shape[1]), lambda i, p: (i, 0))
        if kind == "all":
            return pl.BlockSpec((part, shape[1]), lambda i, p: (p[0] * steps + i, 0))
        return pl.BlockSpec(shape, lambda i, p: (0, 0))

    return pl.pallas_call(
        kernel,
        grid_spec=pltpu.PrefetchScalarGridSpec(
            num_scalar_prefetch=1,
            grid=(steps,),
            in_specs=[spec(kind, value.shape) for kind, value in arrays],
            out_specs=[spec(kind, value.shape) for kind, value in outs],
        ),
        out_shape=[value for kind, value in outs],
        compiler_params=pltpu.CompilerParams(vmem_limit_bytes=40 * 1024 * 1024),
        name=kernel.__name__,
    )(place, *[value for kind, value in arrays])


def widen_kernel(grads, *outs):
    *direct, turned = outs
    start = 0
    for out in direct:
        stop = start + out.shape[1]
        out[...] = grads[:, start:stop].astype(F32)
        start = stop
    turned[...] = jnp.transpose(grads[:, start : start + LANES].astype(F32))


def widened(grads, columns):
    own, total = grads.shape
    shapes = [(own, count) for count in columns] + [(LANES, own)]
    return pl.pallas_call(
        widen_kernel,
        out_shape=[jax.ShapeDtypeStruct(shape, F32) for shape in shapes],
        compiler_params=pltpu.CompilerParams(vmem_limit_bytes=40 * 1024 * 1024),
        name="widen",
    )(grads)


def sum_turn_kernel(parts, out):
    out[...] = jnp.transpose(jnp.sum(parts[...].astype(F32), axis=0))


def summed_turned(parts):
    count, own, columns = parts.shape
    tile = 2 * LANES
    return pl.pallas_call(
        sum_turn_kernel,
        grid=(columns // tile,),
        in_specs=[pl.BlockSpec((count, own, tile), lambda i: (0, 0, i))],
        out_specs=pl.BlockSpec((tile, own), lambda i: (i, 0)),
        out_shape=jax.ShapeDtypeStruct((columns, own), F32),
        compiler_params=pltpu.CompilerParams(vmem_limit_bytes=40 * 1024 * 1024),
        name="sum_turn",
    )(parts)


def place_arrays(length_row, total):
    places = jnp.arange(total, dtype=jnp.int32)
    ids = jnp.arange(length_row.shape[0])
    ends = jnp.sum(jnp.where(ids[None, :] <= ids[:, None], length_row[None, :], 0), axis=1)
    starts = ends - length_row

    def seg_at(at):
        return jnp.sum((at[:, None] >= starts[None, :]).astype(jnp.int32), axis=1) - 1

    segment = seg_at(places)
    valid = (places < ends[-1]).astype(F32)
    lanes = [segment.astype(F32), valid]
    for d in (1, 2, 3):
        lanes.append((seg_at(places - d) == segment).astype(F32))
    for d in (1, 2, 3):
        lanes.append(((seg_at(places + d) == segment) & (places + d < total)).astype(F32))
    head_place = places - places % CHUNK
    lanes.append(((seg_at(head_place - 1) == segment) & (head_place > 0)).astype(F32))
    lanes.append((seg_at(head_place + CHUNK - 1) == segment).astype(F32))
    info = jnp.stack(lanes, axis=1)
    info = jnp.pad(info, ((0, 0), (0, LANES - len(lanes))))
    rows = jnp.broadcast_to(segment.astype(F32)[None, :], (PAD, total))
    return info, rows


GROUP = ("fsdp", "ctx")


def pair_rows(values):
    high, low = halves(values)
    return jnp.stack([high, low], axis=-2)


SC_SUM = "by"
SC_COPY = ""


def deal(part, name=""):
    if name and name in SC_SUM:
        return lax.psum_scatter(part, "tp", scatter_dimension=0, tiled=True)
    return lax.all_to_all(part, "tp", split_axis=0, concat_axis=0, tiled=True)


def add_dealt(moved, name=""):
    if name and name in SC_SUM:
        return moved.astype(F32)
    count = lax.axis_size("tp")
    return jnp.sum(moved.reshape(count, -1, moved.shape[1]).astype(F32), axis=0)


def copy_rows(own, name=""):
    if name and name in SC_COPY:
        return lax.all_gather(own, "tp", axis=0, tiled=True)
    return deal(jnp.concatenate([own] * lax.axis_size("tp"), axis=0))


def relay_send(value, route):
    return lax.ppermute(value, "tp", route)


def relay_first(own):
    return relay_send(own, [(0, 1), (1, 2), (2, 3)]), relay_send(own, [(1, 0), (2, 1), (3, 2)])


def relay_second(before, after):
    place = lax.axis_index("tp")
    before_2 = relay_send(before, [(1, 2), (2, 3)])
    after_2 = relay_send(after, [(2, 1), (1, 0)])
    far = relay_send(jnp.where(place == 1, before, after), [(1, 3), (2, 0)])
    return before_2, after_2, far


def relayed_blocks(own):
    before, after = relay_first(own)
    return (own, before, after, *relay_second(before, after))


def sum_first(part, rows):
    place = lax.axis_index("tp")
    block = rows_of(part, rows)
    return (
        relay_send(block(place - 2), [(2, 1), (3, 2)]),
        relay_send(block(place + 2), [(1, 2), (0, 1)]),
        relay_send(block(jnp.where(place == 3, 0, 3)), [(3, 1), (0, 2)]),
    )


def rows_of(part, rows):
    def block(index):
        return lax.dynamic_slice(part, (jnp.clip(index, 0, 3) * rows, 0), (rows, part.shape[1]))

    return block


def sum_middle(part, rows, came):
    place = lax.axis_index("tp")
    block = rows_of(part, rows)
    from_after, from_before, far = (value.astype(F32) for value in came)
    to_before = block(place - 1).astype(F32) + from_after + jnp.where(place == 1, far, 0.0)
    to_after = block(place + 1).astype(F32) + from_before + jnp.where(place == 2, far, 0.0)
    return to_before.astype(BF16), to_after.astype(BF16)


def sum_second(to_before, to_after):
    return (
        relay_send(to_before, [(1, 0), (2, 1), (3, 2)]),
        relay_send(to_after, [(0, 1), (1, 2), (2, 3)]),
    )


def copy_rows_ordered(own):
    place = lax.axis_index("tp")
    own, before, after, before_2, after_2, far = relayed_blocks(own)
    parts = []
    for source in range(4):
        part = own
        for apart, block in ((-1, before), (1, after), (-2, before_2), (2, after_2)):
            if 0 <= source - apart < 4:
                part = jnp.where(source - place == apart, block, part)
        if source in (0, 3):
            part = jnp.where(jnp.abs(source - place) == 3, far, part)
        parts.append(part)
    return jnp.concatenate(parts, axis=0)


def relayed_block(place, source):
    apart = source - place
    near = jnp.where(apart == 0, 0, jnp.where(apart == -1, 1, 2))
    return jnp.where(jnp.abs(apart) == 3, 5, jnp.where(apart == -2, 3, jnp.where(apart == 2, 4, near)))


RELAYED = 6


together = lax.optimization_barrier


def per_device(
    tokens, cotangent, lengths, order, gain_in, query_proj, key_proj, value_proj, gate_proj,
    alpha_proj, beta_proj, query_conv, key_conv, value_conv, decay_log, step_bias, gain_head,
    out_proj, gain_mid, ffn_gate, ffn_up, ffn_down,
):
    groups = lax.axis_size(GROUP)
    tp_count = lax.axis_size("tp")
    tp_place = lax.axis_index("tp")
    group = lax.axis_index(GROUP)
    micros, rows, width = tokens.shape
    packs = lengths.shape[1]
    all_rows = order.shape[1]
    pack_rows = all_rows // packs
    assert micros * packs == groups and pack_rows == tp_count * rows and tp_count == 4
    assert rows // groups % 2 == 0
    share = rows // groups
    heads = decay_log.shape[0]
    spans = query_conv.shape[0]
    key_size = query_conv.shape[2] * groups
    value_size = value_conv.shape[2] * groups
    sizes = (heads, key_size, value_size)
    key_cols = heads * key_size
    value_cols = heads * value_size
    own = width // groups
    my_micro = group // packs
    my_pack = group % packs

    strict_up = jnp.triu(jnp.ones((rows, rows), BF16), 1)
    mine = (order // rows == group).reshape(micros * packs * tp_count, rows)
    rank = jnp.dot(mine.astype(BF16), strict_up, preferred_element_type=F32).astype(jnp.int32)
    rank = rank.reshape(micros, packs, tp_count, rows)
    ids = jnp.arange(packs * tp_count, dtype=jnp.int32).reshape(packs, tp_count, 1)
    send_slot = (ids * share + rank).reshape(micros, 1, all_rows)
    held = rows + PAD
    pack_id = jnp.arange(groups, dtype=jnp.int32).reshape(micros, packs, 1, 1)
    tp_id = jnp.arange(tp_count, dtype=jnp.int32).reshape(tp_count, 1)
    back_slot = (relayed_block(tp_place, tp_id) * held + pack_id * share + rank).reshape(micros, 1, all_rows)
    local = group * rows + jnp.arange(rows, dtype=jnp.int32)
    hit = order[:, None, :] == local[None, :, None]
    send_at = jnp.sum(jnp.where(hit, send_slot, 0), axis=2)
    back_at = jnp.sum(jnp.where(hit, back_slot, 0), axis=2).reshape(micros * rows)
    row_ids = jnp.arange(rows, dtype=jnp.int32)
    half = share // 2
    near_ranges = tp_count // 2
    near_rows = groups * near_ranges * share
    far_rows = groups * half
    send_rank = send_at % share
    send_range = send_at // share % tp_count
    send_pack = send_at // (share * tp_count)

    def pick_rows(slot, wanted, count):
        ids = jnp.arange(count, dtype=jnp.int32)[None, :, None]
        return ((ids == slot[:, None, :]) & wanted[:, None, :]).astype(BF16)

    send_pick = pick_rows(send_at, send_at >= 0, rows)
    near_pick = pick_rows(
        send_pack * (near_ranges * share) + send_range * share + send_rank,
        send_range < near_ranges,
        packs * near_ranges * share,
    )
    far_pick = pick_rows(
        send_pack * half + send_rank % half,
        (send_range == near_ranges + tp_place // 2) & (send_rank // half == tp_place % 2),
        packs * half,
    )
    back_ids = jnp.arange(RELAYED * held, dtype=jnp.int32)
    back_pick = (back_at[:, None] == back_ids[None, :]).astype(BF16)

    def picked(pick, values):
        return jnp.einsum("msi,mid->msd", pick, values, preferred_element_type=F32).astype(BF16)

    def exchange(sent):
        return lax.all_to_all(sent, GROUP, split_axis=0, concat_axis=0, tiled=True)

    def to_sources(values):
        sent = jnp.dot(return_pick, values, preferred_element_type=F32).astype(BF16)
        return sent.reshape(groups, share, width)

    def to_given(blocks):
        full = jnp.concatenate(blocks, axis=0)
        values = jnp.dot(back_pick, full, preferred_element_type=F32).astype(BF16)
        return values.reshape(micros, rows, width), full

    small = jnp.concatenate(
        [
            gain_in,
            gain_mid,
            query_conv.reshape(-1),
            key_conv.reshape(-1),
            value_conv.reshape(-1),
            gain_head,
        ],
        axis=0,
    )
    small_size = small.shape[0]
    small = jnp.pad(small, (0, width - small_size))
    gates_pad = jnp.zeros((own, LANES - 2 * heads), BF16)
    x_sent = picked(far_pick, tokens).reshape(far_rows, width)
    query_proj, key_proj, value_proj, gate_proj = together(
        (query_proj, key_proj, value_proj, gate_proj, x_sent)
    )[:4]
    mixer_weight = lax.all_gather(
        jnp.concatenate(
            [query_proj, key_proj, value_proj, gate_proj, alpha_proj, beta_proj, gates_pad], axis=1
        ),
        GROUP, axis=0, tiled=True,
    )
    small_count = PAD - half % PAD
    x_moved, near_sent = together(
        (
            exchange(
                jnp.concatenate(
                    [
                        x_sent.reshape(groups, half, width),
                        jnp.broadcast_to(small[None, None, :], (groups, small_count, width)),
                    ],
                    axis=1,
                )
            ),
            picked(near_pick, tokens).reshape(near_rows, width),
        )
    )
    near_moved = exchange(near_sent)
    far_own = x_moved[:, :half].reshape(far_rows, width)
    x_near = relay_first(far_own)
    x_moved, order, lengths = together((x_moved, order, lengths, *x_near))[:3]
    extras = x_moved[:, half, :small_size].astype(F32)

    pack_order = lax.dynamic_slice(order, (my_micro, my_pack * pack_rows), (1, pack_rows))
    source = (pack_order // rows).reshape(tp_count, rows)
    from_each = (source[:, :, None] == jnp.arange(groups, dtype=jnp.int32)).astype(BF16)
    before = jnp.einsum(
        "qp,tqg->tpg", strict_up, from_each, preferred_element_type=F32
    )
    source_rank = jnp.sum(before * from_each.astype(F32), axis=2).astype(jnp.int32)
    relayer = 2 * (tp_id - near_ranges) + source_rank // half
    arrive_at = jnp.where(
        tp_id < near_ranges,
        source * (near_ranges * share) + tp_id * share + source_rank,
        near_rows
        + relayed_block(tp_place, relayer) * far_rows
        + source * half
        + source_rank % half,
    )
    arrive_ids = jnp.arange(near_rows + RELAYED * far_rows, dtype=jnp.int32)
    arrive_pick = (arrive_at.reshape(pack_rows, 1) == arrive_ids[None, :]).astype(BF16)
    pack_ids = jnp.arange(pack_rows, dtype=jnp.int32)
    full_at = source * (tp_count * share) + tp_id * share + source_rank
    place_pick = (full_at.reshape(pack_rows, 1) == pack_ids[None, :]).astype(BF16)
    return_at = lax.dynamic_slice(source * share + source_rank, (tp_place, 0), (1, rows))
    return_pick = (row_ids[:, None] == return_at).astype(BF16)

    x_all = jnp.concatenate((near_moved, far_own, *x_near, *relay_second(*x_near)), axis=0)
    x_low = jnp.dot(arrive_pick, x_all, preferred_element_type=F32).astype(BF16)
    dy_sent = picked(send_pick, cotangent).reshape(pack_rows, width)
    out_proj, ffn_down = together((out_proj, ffn_down, x_low))[:2]
    out_weight = lax.all_gather(out_proj.T, GROUP, axis=0, tiled=True)
    down_weight = lax.all_gather(ffn_down.T, GROUP, axis=0, tiled=True)
    pair_shard = jnp.concatenate(together((ffn_gate, ffn_up, x_moved))[:2], axis=1)

    tail_at = 2 * key_cols + 2 * value_cols
    gain_in_full = extras[:, :own].reshape(1, width)
    gain_mid_full = extras[:, own : 2 * own].reshape(1, width)

    def taps_of(start, weight):
        flat = extras[:, start : start + weight.size]
        flat = flat.reshape(groups, spans, heads, weight.shape[2])
        return jnp.transpose(flat, (1, 2, 0, 3)).reshape(spans, -1), start + weight.size

    query_taps, at = taps_of(2 * own, query_conv)
    key_taps, at = taps_of(at, key_conv)
    value_taps, at = taps_of(at, value_conv)
    taps = jnp.pad(
        jnp.concatenate([query_taps, key_taps, value_taps], axis=1), ((0, PAD - spans), (0, 0))
    )
    head_gain = jnp.broadcast_to(extras[:, at:].reshape(1, value_size), (PAD, value_size))
    par = jnp.zeros((PAD, LANES), F32)
    par = par.at[0, :heads].set(-jnp.exp(decay_log)).at[1, :heads].set(step_bias)
    length_row = lax.dynamic_slice(
        lengths, (my_micro, my_pack, 0), (1, 1, lengths.shape[2])
    ).reshape(-1)
    info, seg_rows = place_arrays(length_row, pack_rows)

    x_float = x_low.astype(F32)
    rate_in = lax.rsqrt(jnp.mean(x_float * x_float, axis=1, keepdims=True) + square_eps)
    normed_in = (x_float * rate_in * gain_in_full).astype(BF16)
    proj = dot_nn(normed_in, mixer_weight)
    dy_all = exchange(together((dy_sent, proj))[0])
    normed_low, *saved = delta_forward(proj, info, seg_rows, par, taps, head_gain, sizes)

    mixed_part = dot_nt(normed_low, out_weight).astype(BF16)
    *mixer_came, dy_all = together((*sum_first(mixed_part, rows), dy_all))
    from_after, from_before = sum_second(*sum_middle(mixed_part, rows, mixer_came))
    pair_weight = lax.all_gather(pair_shard, GROUP, axis=0, tiled=True)
    dy_low = jnp.dot(place_pick, dy_all, preferred_element_type=F32).astype(BF16)
    own_f32 = jax.ShapeDtypeStruct((rows, width), F32)
    own_low = jax.ShapeDtypeStruct((rows, width), BF16)
    gain_part = jax.ShapeDtypeStruct((PAD, width), F32)
    place = tp_place.reshape(1)
    gain_in_8 = jnp.broadcast_to(gain_in_full, (PAD, width))
    gain_mid_8 = jnp.broadcast_to(gain_mid_full, (PAD, width))
    hidden_in, mid_own = row_parts(
        middle_kernel,
        place,
        [
            ("all", mixed_part),
            ("own", from_after),
            ("own", from_before),
            ("all", x_low),
            ("one", gain_mid_8),
        ],
        [("own", own_f32), ("own", own_low)],
        rows,
    )
    mid_low = copy_rows_ordered(mid_own)
    grad_hidden = dot_nn(dy_low, down_weight)
    mid_low, grad_hidden = together((mid_low, grad_hidden))
    units = ffn_gate.shape[1]
    both = dot_nn(mid_low, pair_weight)
    gate_value, up_value = both[:, :units], both[:, units:]
    gate_sig = sigmoid(gate_value)
    gate_act = gate_value * gate_sig
    hidden_low = (gate_act * up_value).astype(BF16)
    pair_grad = jnp.concatenate(
        [
            (grad_hidden * up_value * (gate_sig * (1.0 + gate_value * (1.0 - gate_sig)))).astype(BF16),
            (grad_hidden * gate_act).astype(BF16),
        ],
        axis=1,
    )
    back_part = dot_nt(pair_grad, pair_weight).astype(BF16)
    back_part, pair_late, hidden_late, mid_late = together(
        (back_part, pair_grad, hidden_low, mid_low)
    )
    back_moved = deal(back_part, "b")
    ffn_part = dot_nt(hidden_late, down_weight).astype(BF16)
    grad_down_part = dot_tn(dy_low, hidden_late).astype(BF16)
    grad_pair_part = dot_tn(mid_late, pair_late).astype(BF16)
    back_moved, ffn_part, grad_down_part, grad_pair_part = together(
        (back_moved, ffn_part, grad_down_part, grad_pair_part)
    )

    def owners(value):
        return lax.psum_scatter(value, GROUP, scatter_dimension=0, tiled=True)

    hidden_grad, mix_own, grad_mid_gain = row_parts(
        middle_back_kernel,
        place,
        [("own", back_moved), ("own", hidden_in), ("all", dy_low), ("one", gain_mid_8)],
        [("own", own_f32), ("own", own_low), ("one", gain_part)],
        rows,
    )
    grad_mid_gain = jnp.sum(grad_mid_gain, axis=0)
    mix_low = copy_rows_ordered(mix_own)
    mix_low, ffn_part, grad_down = together((mix_low, ffn_part, owners(grad_down_part)))
    dnormed = dot_nn(mix_low, out_weight)
    grad_proj, conv_grad, head_gain_grad, decay_grads = delta_backward(
        proj, info, seg_rows, par, taps, head_gain, saved, dnormed, sizes
    )
    first_part = dot_nt(grad_proj, mixer_weight).astype(BF16)
    result_moved = deal(ffn_part, "y")
    grad_out_moved = exchange(dot_tn(mix_low, normed_low).astype(BF16))
    first_part, proj_late, result_moved, grad_pair_part, grad_out_moved = together(
        (first_part, grad_proj, result_moved, grad_pair_part, grad_out_moved)
    )
    grad_pair = owners(grad_pair_part)
    grad_mixer_part = dot_tn(normed_in, proj_late).astype(BF16)
    result = (hidden_in + add_dealt(result_moved, "y")).astype(BF16)
    result_back = exchange(to_sources(result)).reshape(rows, width)
    *first_came, grad_mixer_part, result_back = together(
        (*sum_first(first_part, rows), grad_mixer_part, result_back)
    )
    first_middle = sum_middle(first_part, rows, first_came)
    late_after, late_before = sum_second(*first_middle)
    result_back = together((result_back, *first_middle))[0]
    result_back = jnp.pad(result_back, ((0, PAD), (0, 0)))
    result_near = relay_first(result_back)

    token_grad, grad_in_gain = row_parts(
        first_back_kernel,
        place,
        [
            ("all", first_part),
            ("own", late_after),
            ("own", late_before),
            ("own", hidden_grad),
            ("all", x_low),
            ("one", gain_in_8),
        ],
        [("own", own_low), ("one", gain_part)],
        rows,
    )
    grad_in_gain = jnp.sum(grad_in_gain, axis=0)

    conv_sum = jnp.sum(conv_grad.reshape(spans, PAD, -1), axis=1)

    def taps_to(value, size):
        parted = value.reshape(spans, heads, groups, size // groups)
        return jnp.transpose(parted, (2, 0, 1, 3)).reshape(groups, -1)

    gain_sum = jnp.sum(head_gain_grad.reshape(PAD * heads, value_size), axis=0)
    decay_sums = jnp.sum(decay_grads.reshape(2, PAD, LANES), axis=1)[:, :heads].reshape(1, -1)
    parts = [
        grad_in_gain.reshape(groups, own),
        grad_mid_gain.reshape(groups, own),
        gain_sum.reshape(groups, -1),
        taps_to(conv_sum[:, :key_cols], key_size),
        taps_to(conv_sum[:, key_cols : 2 * key_cols], key_size),
        taps_to(conv_sum[:, 2 * key_cols :], value_size),
        jnp.broadcast_to(decay_sums, (groups, decay_sums.shape[1])),
    ]
    lens = [part.shape[1] for part in parts]
    packed = jnp.concatenate(parts, axis=1)
    packed = jnp.pad(packed, ((0, 0), (0, width - packed.shape[1])))
    extra = jnp.pad(pair_rows(packed), ((0, 0), (0, PAD - 2), (0, 0)))
    grad_sent = to_sources(token_grad)
    came = exchange(jnp.concatenate([grad_sent, extra], axis=1))
    before, after, grad_down, grad_out_moved = together(
        (*result_near, grad_down, grad_out_moved, grad_sent)
    )[:4]
    grad_out = summed_turned(grad_out_moved.reshape(groups, own, -1))
    result_far = relay_second(before, after)
    summed = jnp.sum(came[:, share : share + 2].astype(F32), axis=(0, 1))
    block = jnp.concatenate(
        [
            came[:, :share].reshape(rows, width),
            jnp.pad(pair_rows(summed), ((0, PAD - 2), (0, 0))),
        ],
        axis=0,
    )
    token_near = relay_first(block)
    result_far = together((*result_far, *token_near))[:3]
    mixed, unused = to_given((result_back, before, after, *result_far))
    grad_gate = grad_pair[:, :units].astype(F32)
    grad_up = grad_pair[:, units:].astype(F32)
    *token_blocks, grad_gate, grad_up = together(
        (block, *token_near, *relay_second(*token_near), grad_gate, grad_up)
    )
    grad_tokens, full = to_given(token_blocks)
    *mixer_grads, gates_turned = widened(
        owners(grad_mixer_part), [key_cols, key_cols, value_cols, value_cols]
    )
    mixer_grads += [gates_turned[:heads].T, gates_turned[heads : 2 * heads].T]
    grad_down = grad_down.astype(F32).T

    tp_summed = jnp.sum(
        full.reshape(RELAYED, held, width)[:, rows : rows + 2].astype(F32), axis=(0, 1)
    )
    pieces = []
    offset = 0
    for index, length in enumerate(lens):
        origin = tp_summed if index < 3 else summed
        pieces.append(origin[offset : offset + length])
        offset += length
    decay_pair = pieces[6].reshape(2, heads)
    return (
        mixed,
        grad_tokens,
        pieces[0],
        *mixer_grads,
        pieces[3].reshape(query_conv.shape),
        pieces[4].reshape(key_conv.shape),
        pieces[5].reshape(value_conv.shape),
        decay_pair[0],
        decay_pair[1],
        pieces[2],
        grad_out,
        pieces[1],
        grad_gate,
        grad_up,
        grad_down,
    )


def solution(mesh):
    in_specs = (
        P(None, ("fsdp", "ctx"), None),
        P(None, ("fsdp", "ctx"), None),
        P(),
        P(),
        P(("fsdp", "ctx")),
        P(("fsdp", "ctx"), "tp"),
        P(("fsdp", "ctx"), "tp"),
        P(("fsdp", "ctx"), "tp"),
        P(("fsdp", "ctx"), "tp"),
        P(("fsdp", "ctx"), "tp"),
        P(("fsdp", "ctx"), "tp"),
        P(None, "tp", ("fsdp", "ctx")),
        P(None, "tp", ("fsdp", "ctx")),
        P(None, "tp", ("fsdp", "ctx")),
        P("tp"),
        P("tp"),
        P(("fsdp", "ctx")),
        P("tp", ("fsdp", "ctx")),
        P(("fsdp", "ctx")),
        P(("fsdp", "ctx"), "tp"),
        P(("fsdp", "ctx"), "tp"),
        P("tp", ("fsdp", "ctx")),
    )
    out_specs = (
        P(None, ("fsdp", "ctx"), None),
        P(None, ("fsdp", "ctx"), None),
        P(("fsdp", "ctx")),
        P(("fsdp", "ctx"), "tp"),
        P(("fsdp", "ctx"), "tp"),
        P(("fsdp", "ctx"), "tp"),
        P(("fsdp", "ctx"), "tp"),
        P(("fsdp", "ctx"), "tp"),
        P(("fsdp", "ctx"), "tp"),
        P(None, "tp", ("fsdp", "ctx")),
        P(None, "tp", ("fsdp", "ctx")),
        P(None, "tp", ("fsdp", "ctx")),
        P("tp"),
        P("tp"),
        P(("fsdp", "ctx")),
        P("tp", ("fsdp", "ctx")),
        P(("fsdp", "ctx")),
        P(("fsdp", "ctx"), "tp"),
        P(("fsdp", "ctx"), "tp"),
        P("tp", ("fsdp", "ctx")),
    )
    return jax.shard_map(
        per_device, mesh=mesh, in_specs=in_specs, out_specs=out_specs, check_vma=False
    )
```

```python
import functools
import jax
import jax.numpy as jnp
from jax import lax
from jax.sharding import PartitionSpec as P
from jax.experimental import pallas as pl
from jax.experimental.pallas import tpu as pltpu

CHUNK = 128
LANES = 128
PAD = 8
square_eps = 1e-05
unit_eps = 1e-06
F32 = jnp.float32
BF16 = jnp.bfloat16


def dot_nn(left, right):
    return lax.dot_general(left, right, (((1,), (0,)), ((), ())), preferred_element_type=F32)


def dot_nt(left, right):
    return lax.dot_general(left, right, (((1,), (1,)), ((), ())), preferred_element_type=F32)


def dot_tn(left, right):
    return lax.dot_general(left, right, (((0,), (0,)), ((), ())), preferred_element_type=F32)


def halves(value):
    high = value.astype(BF16)
    return high, (value - high.astype(F32)).astype(BF16)


def dot_fine(left, right):
    left_high, left_low = halves(left)
    right_high, right_low = halves(right)
    return (
        dot_nn(left_high, right_high)
        + dot_nn(left_high, right_low)
        + dot_nn(left_low, right_high)
    )


def sum_by(mask, value):
    high, rest = halves(value)
    middle, low = halves(value - high.astype(F32))
    return dot_nn(mask, high) + dot_nn(mask, middle) + dot_nn(mask, low)


def sigmoid(value):
    return 1.0 / (1.0 + jnp.exp(-value))


def softplus(value):
    return jnp.maximum(value, 0.0) + jnp.log1p(jnp.exp(-jnp.abs(value)))


def low_dot(left, right):
    return dot_nn(left.astype(BF16), right.astype(BF16))


def inverses_lower(lower_mats, row_id, col_id):
    size = row_id.shape[0]

    def level(width):
        same = row_id // (2 * width) == col_id // (2 * width)
        return same & ((row_id // width) % 2 == 1) & ((col_id // width) % 2 == 0)

    unit = jnp.where(row_id == col_id, 1.0, 0.0)
    mask = level(1)
    results = [unit - jnp.where(mask, mat, 0.0) for mat in lower_mats]
    width = 2
    while width < size:
        mask = level(width)
        parts = [low_dot(r, jnp.where(mask, mat, 0.0)) for r, mat in zip(results, lower_mats)]
        results = [r - low_dot(p, r) for p, r in zip(parts, results)]
        width *= 2
    rests = [unit - r - dot_fine(mat, r) for r, mat in zip(results, lower_mats)]
    return [r + low_dot(r, rest) for r, rest in zip(results, rests)]


def in_turn(bodies):
    asked = [next(body) for body in bodies]
    while asked:
        made = asked[0][0]([item[1] for item in asked]) if asked[0] else [None] * len(asked)
        following = []
        for body, value in zip(bodies, made):
            try:
                following.append(body.send(value))
            except StopIteration:
                pass
        asked = following


def chunk_basics(gates, par, info, seg_row, row_id, col_id, lane_id, head_count):
    step = gates + par[1:2, :]
    log_decay = jnp.where(lane_id < head_count, par[0:1, :] * softplus(step), 0.0)
    beta_raw = sigmoid(gates)
    valid = info[:, 1:2]
    lower = row_id >= col_id
    cumulative = sum_by(jnp.where(lower, 1.0, 0.0).astype(BF16), log_decay)
    both = jnp.where(lane_id < head_count, cumulative, beta_raw * valid)
    turned = jnp.transpose(both)
    inner = lower & (info[:, 0:1] == seg_row)
    return step, log_decay, beta_raw, both, turned, inner


def activations(ext, taps, masks, start, stop, rows):
    value = taps[3:4, start:stop] * ext[PAD : PAD + rows, start:stop]
    for distance in (1, 2, 3):
        shifted = ext[PAD - distance : PAD - distance + rows, start:stop]
        value = value + masks[distance - 1] * (taps[3 - distance : 4 - distance, start:stop] * shifted)
    return value


def forward_kernel(
    head_count, key_size, value_size,
    proj, info_ref, segr, par_ref, taps, gain_ref,
    normed_out, state_out, inverse_out, pseudo_out, output_out,
    state, ext,
):
    rows = proj.shape[0]
    width = head_count * (2 * key_size + value_size)
    gate_at = width
    tail_at = width + head_count * value_size

    @pl.when(pl.program_id(0) == 0)
    def start():
        state[...] = jnp.zeros_like(state)
        ext[0:PAD, :] = jnp.zeros((PAD, width), F32)

    ext[PAD : PAD + rows, :] = proj[:, 0:width]
    info = info_ref[...]
    row_id = lax.broadcasted_iota(jnp.int32, (rows, rows), 0)
    col_id = lax.broadcasted_iota(jnp.int32, (rows, rows), 1)
    lane_id = lax.broadcasted_iota(jnp.int32, (rows, LANES), 1)
    masks = tuple(info[:, 1 + d : 2 + d] for d in (1, 2, 3))
    valid = info[:, 1:2]
    unused, log_decay, beta_raw, both, turned, inner = chunk_basics(
        proj[:, tail_at : tail_at + LANES], par_ref[...], info, segr[0:1, :],
        row_id, col_id, lane_id, head_count,
    )
    carried_mask = info[:, 8:9]
    tail_mask = info[:, 9:10]
    strict = row_id > col_id
    key_at = head_count * key_size
    value_at = 2 * key_at
    def one_head(head):
        ks = key_size
        vs = value_size
        act_q = activations(ext, taps, masks, head * ks, (head + 1) * ks, rows)
        act_k = activations(ext, taps, masks, key_at + head * ks, key_at + (head + 1) * ks, rows)
        act_v = activations(ext, taps, masks, value_at + head * vs, value_at + (head + 1) * vs, rows)
        cq = act_q * sigmoid(act_q)
        ck = act_k * sigmoid(act_k)
        values = act_v * sigmoid(act_v)
        query = cq * (lax.rsqrt(jnp.sum(cq * cq, axis=1, keepdims=True) + unit_eps) * ks ** -0.5)
        key = ck * lax.rsqrt(jnp.sum(ck * ck, axis=1, keepdims=True) + unit_eps)
        yield
        qb = query.astype(BF16)
        kb = key.astype(BF16)
        cum = both[:, head : head + 1]
        beta = both[:, head_count + head : head_count + head + 1]
        cum_row = turned[head : head + 1, :]
        beta_row = turned[head_count + head : head_count + head + 1, :]
        decays = jnp.where(inner, jnp.exp(jnp.minimum(cum - cum_row, 0.0)), 0.0)
        lower_mat = jnp.where(strict, decays * dot_nt(kb, kb) * beta_row, 0.0)
        inverse = yield (lambda mats: inverses_lower(mats, row_id, col_id)), lower_mat
        yield
        carried = jnp.exp(cum) * carried_mask
        last = cum[rows - 1 : rows, :]
        tail = jnp.exp(last - cum) * tail_mask
        keep = carried[rows - 1 : rows, :]
        before = state[head]
        sb = before.astype(BF16)
        state_out[0, head] = sb
        target = values - carried * dot_nn(kb, sb)
        ib = inverse.astype(BF16)
        pseudo = dot_nn(ib, target.astype(BF16))
        inverse_out[0, head] = ib
        pseudo_out[:, head * vs : (head + 1) * vs] = pseudo.astype(BF16)
        yield
        weighted = beta * pseudo
        mix = decays * dot_nt(qb, kb)
        output = carried * dot_nn(qb, sb) + dot_nn(mix.astype(BF16), weighted.astype(BF16))
        output_out[:, head * vs : (head + 1) * vs] = output
        state[head] = keep * before + dot_tn(kb, (tail * weighted).astype(BF16))
        yield
        gate = proj[:, gate_at + head * vs : gate_at + (head + 1) * vs]
        scale = lax.rsqrt(jnp.mean(output * output, axis=1, keepdims=True) + square_eps)
        normed = output * scale * gain_ref[0:1, :] * (gate * sigmoid(gate)) * valid
        normed_out[:, head * vs : (head + 1) * vs] = normed.astype(BF16)

    in_turn([one_head(head) for head in range(head_count)])
    ext[0:PAD, :] = ext[rows : rows + PAD, :]


def backward_kernel(
    head_count, key_size, value_size,
    proj, prior, info_ref, segr, par_ref, taps, gain_ref,
    state_in, inverse_in, pseudo_in, output_in, dnormed,
    grad_out, conv_out, gain_out, small_out,
    dstate, ext, dext,
):
    rows = proj.shape[0]
    width = head_count * (2 * key_size + value_size)
    gate_at = width
    tail_at = width + head_count * value_size
    place = pl.program_id(0)
    count = pl.num_programs(0)

    @pl.when(place == 0)
    def start():
        dstate[...] = jnp.zeros_like(dstate)
        dext[rows : rows + PAD, :] = jnp.zeros((PAD, width), F32)
        conv_out[...] = jnp.zeros_like(conv_out)
        gain_out[...] = jnp.zeros_like(gain_out)
        small_out[...] = jnp.zeros_like(small_out)

    first = place == count - 1
    ext[0:PAD, :] = jnp.where(first, 0.0, prior[:, 0:width])
    ext[PAD : PAD + rows, :] = proj[:, 0:width]
    info = info_ref[...]
    row_id = lax.broadcasted_iota(jnp.int32, (rows, rows), 0)
    col_id = lax.broadcasted_iota(jnp.int32, (rows, rows), 1)
    lane_id = lax.broadcasted_iota(jnp.int32, (rows, LANES), 1)
    masks = tuple(info[:, 1 + d : 2 + d] for d in (1, 2, 3))
    later = tuple(info[:, 4 + d : 5 + d] for d in (1, 2, 3))
    valid = info[:, 1:2]
    step, log_decay, beta_raw, both, turned, inner = chunk_basics(
        proj[:, tail_at : tail_at + LANES], par_ref[...], info, segr[0:1, :],
        row_id, col_id, lane_id, head_count,
    )
    carried_mask = info[:, 8:9]
    tail_mask = info[:, 9:10]
    strict = row_id > col_id
    last_row = lax.broadcasted_iota(jnp.int32, (rows, 1), 0) == rows - 1
    row_of = lax.broadcasted_iota(jnp.int32, (LANES, rows), 0)
    ks = key_size
    vs = value_size
    key_at = head_count * ks
    value_at = 2 * key_at
    sums = {}

    def fold(value):
        return jnp.sum(value.reshape(rows // PAD, PAD, value.shape[1]), axis=0)

    def conv_back(da, start, stop):
        dext[0:rows, start:stop] = da
        back = taps[3:4, start:stop] * da
        conv_out[3 * PAD : 4 * PAD, start:stop] += fold(da * ext[PAD : PAD + rows, start:stop])
        for d in (1, 2, 3):
            back = back + later[d - 1] * (taps[3 - d : 4 - d, start:stop] * dext[d : d + rows, start:stop])
            shifted = ext[PAD - d : PAD - d + rows, start:stop]
            conv_out[(3 - d) * PAD : (4 - d) * PAD, start:stop] += fold(masks[d - 1] * da * shifted)
        grad_out[:, start:stop] = back.astype(BF16)

    def one_head(head):
        act_q = activations(ext, taps, masks, head * ks, (head + 1) * ks, rows)
        act_k = activations(ext, taps, masks, key_at + head * ks, key_at + (head + 1) * ks, rows)
        act_v = activations(ext, taps, masks, value_at + head * vs, value_at + (head + 1) * vs, rows)
        sig_q, sig_k, sig_v = sigmoid(act_q), sigmoid(act_k), sigmoid(act_v)
        cq, ck, values = act_q * sig_q, act_k * sig_k, act_v * sig_v
        rate_q = lax.rsqrt(jnp.sum(cq * cq, axis=1, keepdims=True) + unit_eps)
        rate_k = lax.rsqrt(jnp.sum(ck * ck, axis=1, keepdims=True) + unit_eps)
        unit_q = cq * rate_q
        query = unit_q * ks ** -0.5
        key = ck * rate_k
        yield
        qb = query.astype(BF16)
        kb = key.astype(BF16)
        cum = both[:, head : head + 1]
        beta = both[:, head_count + head : head_count + head + 1]
        cum_row = turned[head : head + 1, :]
        beta_row = turned[head_count + head : head_count + head + 1, :]
        decays = jnp.where(inner, jnp.exp(jnp.minimum(cum - cum_row, 0.0)), 0.0)
        carried = jnp.exp(cum) * carried_mask
        tail = jnp.exp(cum[rows - 1 : rows, :] - cum) * tail_mask
        keep = carried[rows - 1 : rows, :]
        yield
        sb = state_in[0, head]
        before = sb.astype(F32)
        ib = inverse_in[0, head]
        pb = pseudo_in[:, head * vs : (head + 1) * vs]
        pseudo = pb.astype(F32)
        output = output_in[:, head * vs : (head + 1) * vs]
        gate = proj[:, gate_at + head * vs : gate_at + (head + 1) * vs]
        given = dnormed[:, head * vs : (head + 1) * vs] * valid
        gain = gain_ref[0:1, :]
        scale = lax.rsqrt(jnp.mean(output * output, axis=1, keepdims=True) + square_eps)
        unit_o = output * scale
        sig_g = sigmoid(gate)
        silu_g = gate * sig_g
        dunit = given * gain * silu_g
        doutput = scale * (dunit - unit_o * jnp.mean(unit_o * dunit, axis=1, keepdims=True))
        dgate = given * unit_o * gain * (sig_g * (1.0 + gate * (1.0 - sig_g)))
        gain_out[:, head * vs : (head + 1) * vs] += fold(given * unit_o * silu_g)
        grad_out[:, gate_at + head * vs : gate_at + (head + 1) * vs] = dgate.astype(BF16)
        yield
        dob = doutput.astype(BF16)
        weighted = beta * pseudo
        wb = weighted.astype(BF16)
        gram = dot_nt(kb, kb)
        cross = dot_nt(qb, kb)
        mix = decays * cross
        yield
        after = dstate[head]
        ab = after.astype(BF16)
        from_state = dot_nn(kb, ab)
        dweighted = dot_tn(mix.astype(BF16), dob) + tail * from_state
        dbeta = jnp.sum(dweighted * pseudo, axis=1, keepdims=True)
        yield
        dtarget = dot_tn(ib, (beta * dweighted).astype(BF16))
        dtb = dtarget.astype(BF16)
        read = dot_nn(kb, sb)
        yield
        dcarried = jnp.sum(doutput * dot_nn(qb, sb), axis=1, keepdims=True) - jnp.sum(
            dtarget * read, axis=1, keepdims=True
        )
        dtail = jnp.sum(weighted * from_state, axis=1, keepdims=True)
        dkeep = jnp.sum(jnp.sum(after * before, axis=1, keepdims=True), axis=0, keepdims=True)
        cdo = (carried * doutput).astype(BF16)
        cdt = (carried * dtarget).astype(BF16)
        dstate[head] = keep * after + dot_tn(qb, cdo) - dot_tn(kb, cdt)
        yield
        dmix = dot_nt(dob, wb)
        dcross = (dmix * decays).astype(BF16)
        dlower = jnp.where(strict, -dot_nt(dtb, pb), 0.0) * decays
        dgram = (dlower * beta_row).astype(BF16)
        plain = dlower * gram
        inner_grad = dmix * mix + plain * beta_row
        yield
        dquery = dot_nt(cdo, sb) + dot_nn(dcross, kb)
        dkey = (
            dot_tn(dcross, qb)
            + dot_nn(dgram, kb)
            + dot_tn(dgram, kb)
            + dot_nt((tail * weighted).astype(BF16), ab)
            - dot_nt(cdt, sb)
        )
        yield
        dlast = jnp.sum(dtail * tail, axis=0, keepdims=True) + dkeep * keep
        dcum_col = (
            jnp.sum(inner_grad, axis=1, keepdims=True)
            + dcarried * carried
            - dtail * tail
            + jnp.where(last_row, dlast, 0.0)
        )
        sums[head] = (
            dcum_col,
            dbeta,
            -jnp.sum(inner_grad, axis=0, keepdims=True),
            jnp.sum(plain, axis=0, keepdims=True),
        )
        yield
        dq_scaled = dquery * ks ** -0.5
        dcq = (dq_scaled - unit_q * jnp.sum(unit_q * dq_scaled, axis=1, keepdims=True)) * rate_q
        dck = (dkey - key * jnp.sum(key * dkey, axis=1, keepdims=True)) * rate_k
        conv_back(dcq * (sig_q * (1.0 + act_q * (1.0 - sig_q))), head * ks, (head + 1) * ks)
        yield
        conv_back(
            dck * (sig_k * (1.0 + act_k * (1.0 - sig_k))), key_at + head * ks, key_at + (head + 1) * ks
        )
        conv_back(
            dtarget * (sig_v * (1.0 + act_v * (1.0 - sig_v))),
            value_at + head * vs,
            value_at + (head + 1) * vs,
        )

    for head in range(head_count):
        in_turn([one_head(head)])
    dcum = jnp.zeros((rows, LANES), F32)
    dturned = jnp.zeros((LANES, rows), F32)
    for head, (dcum_col, dbeta, dcum_row, dbeta_row) in sums.items():
        dcum = jnp.where(lane_id == head, dcum_col, dcum)
        dcum = jnp.where(lane_id == head_count + head, dbeta, dcum)
        dturned = jnp.where(row_of == head, dcum_row, dturned)
        dturned = jnp.where(row_of == head_count + head, dbeta_row, dturned)
    dboth = dcum + jnp.transpose(dturned)
    upper = jnp.where(row_id <= col_id, 1.0, 0.0).astype(BF16)
    dlog = sum_by(upper, jnp.where(lane_id < head_count, dboth, 0.0))
    dalpha = dlog * par_ref[0:1, :] * sigmoid(step)
    dbeta_raw = dboth * valid * beta_raw * (1.0 - beta_raw)
    tail_grad = jnp.where(
        lane_id < head_count, dalpha, jnp.where(lane_id < 2 * head_count, dbeta_raw, 0.0)
    )
    grad_out[:, tail_at : tail_at + LANES] = tail_grad.astype(BF16)
    small_out[0:PAD, :] += fold(dlog * log_decay)
    small_out[PAD : 2 * PAD, :] += fold(jnp.where(lane_id < head_count, dalpha, 0.0))
    dext[rows : rows + PAD, :] = dext[0:PAD, :]


def delta_forward(proj, info, seg_rows, par, taps, gain, sizes):
    head_count, key_size, value_size = sizes
    total, columns = proj.shape
    steps = total // CHUNK
    width = head_count * (2 * key_size + value_size)
    span = head_count * value_size
    whole = lambda a: pl.BlockSpec(a.shape, lambda i: (0, 0))
    by_rows = lambda n: pl.BlockSpec((CHUNK, n), lambda i: (i, 0))
    return pl.pallas_call(
        functools.partial(forward_kernel, head_count, key_size, value_size),
        grid=(steps,),
        in_specs=[
            by_rows(columns),
            by_rows(LANES),
            pl.BlockSpec((PAD, CHUNK), lambda i: (0, i)),
            whole(par),
            whole(taps),
            whole(gain),
        ],
        out_specs=[
            by_rows(span),
            pl.BlockSpec((1, head_count, key_size, value_size), lambda i: (i, 0, 0, 0)),
            pl.BlockSpec((1, head_count, CHUNK, CHUNK), lambda i: (i, 0, 0, 0)),
            by_rows(span),
            by_rows(span),
        ],
        out_shape=[
            jax.ShapeDtypeStruct((total, span), BF16),
            jax.ShapeDtypeStruct((steps, head_count, key_size, value_size), BF16),
            jax.ShapeDtypeStruct((steps, head_count, CHUNK, CHUNK), BF16),
            jax.ShapeDtypeStruct((total, span), BF16),
            jax.ShapeDtypeStruct((total, span), F32),
        ],
        scratch_shapes=[
            pltpu.VMEM((head_count, key_size, value_size), F32),
            pltpu.VMEM((CHUNK + PAD, width), F32),
        ],
        compiler_params=pltpu.CompilerParams(vmem_limit_bytes=48 * 1024 * 1024),
        name="delta_forward",
    )(proj, info, seg_rows, par, taps, gain)


def delta_backward(proj, info, seg_rows, par, taps, gain, saved, dnormed, sizes):
    head_count, key_size, value_size = sizes
    total, columns = proj.shape
    steps = total // CHUNK
    width = head_count * (2 * key_size + value_size)
    span = head_count * value_size
    states, inverses, pseudos, outputs = saved
    blocks = CHUNK // PAD
    turn = lambda i: steps - 1 - i
    whole = lambda a: pl.BlockSpec(a.shape, lambda i: (0, 0))
    by_rows = lambda n: pl.BlockSpec((CHUNK, n), lambda i: (turn(i), 0))
    return pl.pallas_call(
        functools.partial(backward_kernel, head_count, key_size, value_size),
        grid=(steps,),
        in_specs=[
            by_rows(columns),
            pl.BlockSpec((PAD, columns), lambda i: (jnp.maximum(turn(i) * blocks - 1, 0), 0)),
            by_rows(LANES),
            pl.BlockSpec((PAD, CHUNK), lambda i: (0, turn(i))),
            whole(par),
            whole(taps),
            whole(gain),
            pl.BlockSpec((1, head_count, key_size, value_size), lambda i: (turn(i), 0, 0, 0)),
            pl.BlockSpec((1, head_count, CHUNK, CHUNK), lambda i: (turn(i), 0, 0, 0)),
            by_rows(span),
            by_rows(span),
            by_rows(span),
        ],
        out_specs=[
            by_rows(columns),
            pl.BlockSpec((4 * PAD, width), lambda i: (0, 0)),
            pl.BlockSpec((PAD, span), lambda i: (0, 0)),
            pl.BlockSpec((2 * PAD, LANES), lambda i: (0, 0)),
        ],
        out_shape=[
            jax.ShapeDtypeStruct((total, columns), BF16),
            jax.ShapeDtypeStruct((4 * PAD, width), F32),
            jax.ShapeDtypeStruct((PAD, span), F32),
            jax.ShapeDtypeStruct((2 * PAD, LANES), F32),
        ],
        scratch_shapes=[
            pltpu.VMEM((head_count, key_size, value_size), F32),
            pltpu.VMEM((CHUNK + PAD, width), F32),
            pltpu.VMEM((CHUNK + PAD, width), F32),
        ],
        compiler_params=pltpu.CompilerParams(vmem_limit_bytes=48 * 1024 * 1024),
        name="delta_backward",
    )(proj, proj, info, seg_rows, par, taps, gain, states, inverses, pseudos, outputs, dnormed)


def middle_kernel(place, own, after, before, x_ref, gain, hidden_out, normed_out):
    mixer = own[...].astype(F32) + after[...].astype(F32) + before[...].astype(F32)
    hidden = mixer + x_ref[...].astype(F32)
    rate = lax.rsqrt(jnp.mean(hidden * hidden, axis=1, keepdims=True) + square_eps)
    hidden_out[...] = hidden
    normed_out[...] = (hidden * rate * gain[0:1, :]).astype(BF16)


def norm_back(grad, value, gain):
    rate = lax.rsqrt(jnp.mean(value * value, axis=1, keepdims=True) + square_eps)
    scaled = grad * gain
    inner = jnp.mean(value * scaled, axis=1, keepdims=True)
    return rate * scaled - rate * rate * rate * value * inner, grad * value * rate


def rows_summed(value):
    return jnp.sum(value.reshape(value.shape[0] // PAD, PAD, value.shape[1]), axis=0)


def middle_back_kernel(place, moved, hidden, dy_ref, gain, grad_out, low_out, gain_out):
    @pl.when(pl.program_id(0) == 0)
    def start():
        gain_out[...] = jnp.zeros_like(gain_out)

    back, part = norm_back(moved[...].astype(F32), hidden[...], gain[0:1, :])
    grad = dy_ref[...].astype(F32) + back
    grad_out[...] = grad
    low_out[...] = grad.astype(BF16)
    gain_out[...] += rows_summed(part)


def first_back_kernel(place, own, after, before, late, x_ref, gain, grad_out, gain_out):
    @pl.when(pl.program_id(0) == 0)
    def start():
        gain_out[...] = jnp.zeros_like(gain_out)

    moved = own[...].astype(F32) + after[...].astype(F32) + before[...].astype(F32)
    back, part = norm_back(moved, x_ref[...].astype(F32), gain[0:1, :])
    grad_out[...] = (late[...] + back).astype(BF16)
    gain_out[...] += rows_summed(part)


def row_parts(kernel, place, arrays, outs, rows):
    part = 48 if rows % 48 == 0 else rows
    steps = rows // part

    def spec(kind, shape):
        if kind == "own":
            return pl.BlockSpec((part, shape[1]), lambda i, p: (i, 0))
        if kind == "all":
            return pl.BlockSpec((part, shape[1]), lambda i, p: (p[0] * steps + i, 0))
        return pl.BlockSpec(shape, lambda i, p: (0, 0))

    return pl.pallas_call(
        kernel,
        grid_spec=pltpu.PrefetchScalarGridSpec(
            num_scalar_prefetch=1,
            grid=(steps,),
            in_specs=[spec(kind, value.shape) for kind, value in arrays],
            out_specs=[spec(kind, value.shape) for kind, value in outs],
        ),
        out_shape=[value for kind, value in outs],
        compiler_params=pltpu.CompilerParams(vmem_limit_bytes=40 * 1024 * 1024),
        name=kernel.__name__,
    )(place, *[value for kind, value in arrays])


def widen_kernel(grads, *outs):
    *direct, turned = outs
    start = 0
    for out in direct:
        stop = start + out.shape[1]
        out[...] = grads[:, start:stop].astype(F32)
        start = stop
    turned[...] = jnp.transpose(grads[:, start : start + LANES].astype(F32))


def widened(grads, columns):
    own, total = grads.shape
    shapes = [(own, count) for count in columns] + [(LANES, own)]
    return pl.pallas_call(
        widen_kernel,
        out_shape=[jax.ShapeDtypeStruct(shape, F32) for shape in shapes],
        compiler_params=pltpu.CompilerParams(vmem_limit_bytes=40 * 1024 * 1024),
        name="widen",
    )(grads)


def sum_turn_kernel(parts, out):
    out[...] = jnp.transpose(jnp.sum(parts[...].astype(F32), axis=0))


def summed_turned(parts):
    count, own, columns = parts.shape
    tile = 2 * LANES
    return pl.pallas_call(
        sum_turn_kernel,
        grid=(columns // tile,),
        in_specs=[pl.BlockSpec((count, own, tile), lambda i: (0, 0, i))],
        out_specs=pl.BlockSpec((tile, own), lambda i: (i, 0)),
        out_shape=jax.ShapeDtypeStruct((columns, own), F32),
        compiler_params=pltpu.CompilerParams(vmem_limit_bytes=40 * 1024 * 1024),
        name="sum_turn",
    )(parts)


def place_arrays(length_row, total):
    places = jnp.arange(total, dtype=jnp.int32)
    ids = jnp.arange(length_row.shape[0])
    ends = jnp.sum(jnp.where(ids[None, :] <= ids[:, None], length_row[None, :], 0), axis=1)
    starts = ends - length_row

    def seg_at(at):
        return jnp.sum((at[:, None] >= starts[None, :]).astype(jnp.int32), axis=1) - 1

    segment = seg_at(places)
    valid = (places < ends[-1]).astype(F32)
    lanes = [segment.astype(F32), valid]
    for d in (1, 2, 3):
        lanes.append((seg_at(places - d) == segment).astype(F32))
    for d in (1, 2, 3):
        lanes.append(((seg_at(places + d) == segment) & (places + d < total)).astype(F32))
    head_place = places - places % CHUNK
    lanes.append(((seg_at(head_place - 1) == segment) & (head_place > 0)).astype(F32))
    lanes.append((seg_at(head_place + CHUNK - 1) == segment).astype(F32))
    info = jnp.stack(lanes, axis=1)
    info = jnp.pad(info, ((0, 0), (0, LANES - len(lanes))))
    rows = jnp.broadcast_to(segment.astype(F32)[None, :], (PAD, total))
    return info, rows


GROUP = ("fsdp", "ctx")


def pair_rows(values):
    high, low = halves(values)
    return jnp.stack([high, low], axis=-2)


SC_SUM = "by"
SC_COPY = ""


def deal(part, name=""):
    if name and name in SC_SUM:
        return lax.psum_scatter(part, "tp", scatter_dimension=0, tiled=True)
    return lax.all_to_all(part, "tp", split_axis=0, concat_axis=0, tiled=True)


def add_dealt(moved, name=""):
    if name and name in SC_SUM:
        return moved.astype(F32)
    count = lax.axis_size("tp")
    return jnp.sum(moved.reshape(count, -1, moved.shape[1]).astype(F32), axis=0)


def copy_rows(own, name=""):
    if name and name in SC_COPY:
        return lax.all_gather(own, "tp", axis=0, tiled=True)
    return deal(jnp.concatenate([own] * lax.axis_size("tp"), axis=0))


def relay_send(value, route):
    return lax.ppermute(value, "tp", route)


def relay_first(own):
    return relay_send(own, [(0, 1), (1, 2), (2, 3)]), relay_send(own, [(1, 0), (2, 1), (3, 2)])


def relay_second(before, after):
    place = lax.axis_index("tp")
    before_2 = relay_send(before, [(1, 2), (2, 3)])
    after_2 = relay_send(after, [(2, 1), (1, 0)])
    far = relay_send(jnp.where(place == 1, before, after), [(1, 3), (2, 0)])
    return before_2, after_2, far


def relayed_blocks(own):
    before, after = relay_first(own)
    return (own, before, after, *relay_second(before, after))


def sum_first(part, rows):
    place = lax.axis_index("tp")
    block = rows_of(part, rows)
    return (
        relay_send(block(place - 2), [(2, 1), (3, 2)]),
        relay_send(block(place + 2), [(1, 2), (0, 1)]),
        relay_send(block(jnp.where(place == 3, 0, 3)), [(3, 1), (0, 2)]),
    )


def rows_of(part, rows):
    def block(index):
        return lax.dynamic_slice(part, (jnp.clip(index, 0, 3) * rows, 0), (rows, part.shape[1]))

    return block


def sum_middle(part, rows, came):
    place = lax.axis_index("tp")
    block = rows_of(part, rows)
    from_after, from_before, far = (value.astype(F32) for value in came)
    to_before = block(place - 1).astype(F32) + from_after + jnp.where(place == 1, far, 0.0)
    to_after = block(place + 1).astype(F32) + from_before + jnp.where(place == 2, far, 0.0)
    return to_before.astype(BF16), to_after.astype(BF16)


def sum_second(to_before, to_after):
    return (
        relay_send(to_before, [(1, 0), (2, 1), (3, 2)]),
        relay_send(to_after, [(0, 1), (1, 2), (2, 3)]),
    )


def copy_rows_ordered(own):
    place = lax.axis_index("tp")
    own, before, after, before_2, after_2, far = relayed_blocks(own)
    parts = []
    for source in range(4):
        part = own
        for apart, block in ((-1, before), (1, after), (-2, before_2), (2, after_2)):
            if 0 <= source - apart < 4:
                part = jnp.where(source - place == apart, block, part)
        if source in (0, 3):
            part = jnp.where(jnp.abs(source - place) == 3, far, part)
        parts.append(part)
    return jnp.concatenate(parts, axis=0)


def relayed_block(place, source):
    apart = source - place
    near = jnp.where(apart == 0, 0, jnp.where(apart == -1, 1, 2))
    return jnp.where(jnp.abs(apart) == 3, 5, jnp.where(apart == -2, 3, jnp.where(apart == 2, 4, near)))


RELAYED = 6


together = lax.optimization_barrier


def per_device(
    tokens, cotangent, lengths, order, gain_in, query_proj, key_proj, value_proj, gate_proj,
    alpha_proj, beta_proj, query_conv, key_conv, value_conv, decay_log, step_bias, gain_head,
    out_proj, gain_mid, ffn_gate, ffn_up, ffn_down,
):
    groups = lax.axis_size(GROUP)
    tp_count = lax.axis_size("tp")
    tp_place = lax.axis_index("tp")
    group = lax.axis_index(GROUP)
    micros, rows, width = tokens.shape
    packs = lengths.shape[1]
    all_rows = order.shape[1]
    pack_rows = all_rows // packs
    assert micros * packs == groups and pack_rows == tp_count * rows and tp_count == 4
    assert rows // groups % 2 == 0
    share = rows // groups
    heads = decay_log.shape[0]
    spans = query_conv.shape[0]
    key_size = query_conv.shape[2] * groups
    value_size = value_conv.shape[2] * groups
    sizes = (heads, key_size, value_size)
    key_cols = heads * key_size
    value_cols = heads * value_size
    own = width // groups
    my_micro = group // packs
    my_pack = group % packs

    strict_up = jnp.triu(jnp.ones((rows, rows), BF16), 1)
    mine = (order // rows == group).reshape(micros * packs * tp_count, rows)
    rank = jnp.dot(mine.astype(BF16), strict_up, preferred_element_type=F32).astype(jnp.int32)
    rank = rank.reshape(micros, packs, tp_count, rows)
    ids = jnp.arange(packs * tp_count, dtype=jnp.int32).reshape(packs, tp_count, 1)
    send_slot = (ids * share + rank).reshape(micros, 1, all_rows)
    held = rows + PAD
    pack_id = jnp.arange(groups, dtype=jnp.int32).reshape(micros, packs, 1, 1)
    tp_id = jnp.arange(tp_count, dtype=jnp.int32).reshape(tp_count, 1)
    back_slot = (relayed_block(tp_place, tp_id) * held + pack_id * share + rank).reshape(micros, 1, all_rows)
    local = group * rows + jnp.arange(rows, dtype=jnp.int32)
    hit = order[:, None, :] == local[None, :, None]
    send_at = jnp.sum(jnp.where(hit, send_slot, 0), axis=2)
    back_at = jnp.sum(jnp.where(hit, back_slot, 0), axis=2).reshape(micros * rows)
    row_ids = jnp.arange(rows, dtype=jnp.int32)
    half = share // 2
    near_ranges = tp_count // 2
    near_rows = groups * near_ranges * share
    far_rows = groups * half
    send_rank = send_at % share
    send_range = send_at // share % tp_count
    send_pack = send_at // (share * tp_count)

    def pick_rows(slot, wanted, count):
        ids = jnp.arange(count, dtype=jnp.int32)[None, :, None]
        return ((ids == slot[:, None, :]) & wanted[:, None, :]).astype(BF16)

    send_pick = pick_rows(send_at, send_at >= 0, rows)
    near_pick = pick_rows(
        send_pack * (near_ranges * share) + send_range * share + send_rank,
        send_range < near_ranges,
        packs * near_ranges * share,
    )
    far_pick = pick_rows(
        send_pack * half + send_rank % half,
        (send_range == near_ranges + tp_place // 2) & (send_rank // half == tp_place % 2),
        packs * half,
    )
    back_ids = jnp.arange(RELAYED * held, dtype=jnp.int32)
    back_pick = (back_at[:, None] == back_ids[None, :]).astype(BF16)

    def picked(pick, values):
        return jnp.einsum("msi,mid->msd", pick, values, preferred_element_type=F32).astype(BF16)

    def exchange(sent):
        return lax.all_to_all(sent, GROUP, split_axis=0, concat_axis=0, tiled=True)

    def to_sources(values):
        sent = jnp.dot(return_pick, values, preferred_element_type=F32).astype(BF16)
        return sent.reshape(groups, share, width)

    def to_given(blocks):
        full = jnp.concatenate(blocks, axis=0)
        values = jnp.dot(back_pick, full, preferred_element_type=F32).astype(BF16)
        return values.reshape(micros, rows, width), full

    small = jnp.concatenate(
        [
            gain_in,
            gain_mid,
            query_conv.reshape(-1),
            key_conv.reshape(-1),
            value_conv.reshape(-1),
            gain_head,
        ],
        axis=0,
    )
    small_size = small.shape[0]
    small = jnp.pad(small, (0, width - small_size))
    gates_pad = jnp.zeros((own, LANES - 2 * heads), BF16)
    x_sent = picked(far_pick, tokens).reshape(far_rows, width)
    query_proj, key_proj, value_proj, gate_proj = together(
        (query_proj, key_proj, value_proj, gate_proj, x_sent)
    )[:4]
    mixer_weight = lax.all_gather(
        jnp.concatenate(
            [query_proj, key_proj, value_proj, gate_proj, alpha_proj, beta_proj, gates_pad], axis=1
        ),
        GROUP, axis=0, tiled=True,
    )
    small_count = PAD - half % PAD
    x_moved, near_sent = together(
        (
            exchange(
                jnp.concatenate(
                    [
                        x_sent.reshape(groups, half, width),
                        jnp.broadcast_to(small[None, None, :], (groups, small_count, width)),
                    ],
                    axis=1,
                )
            ),
            picked(near_pick, tokens).reshape(near_rows, width),
        )
    )
    near_moved = exchange(near_sent)
    far_own = x_moved[:, :half].reshape(far_rows, width)
    x_near = relay_first(far_own)
    x_moved, order, lengths = together((x_moved, order, lengths, *x_near))[:3]
    extras = x_moved[:, half, :small_size].astype(F32)

    pack_order = lax.dynamic_slice(order, (my_micro, my_pack * pack_rows), (1, pack_rows))
    source = (pack_order // rows).reshape(tp_count, rows)
    from_each = (source[:, :, None] == jnp.arange(groups, dtype=jnp.int32)).astype(BF16)
    before = jnp.einsum(
        "qp,tqg->tpg", strict_up, from_each, preferred_element_type=F32
    )
    source_rank = jnp.sum(before * from_each.astype(F32), axis=2).astype(jnp.int32)
    relayer = 2 * (tp_id - near_ranges) + source_rank // half
    arrive_at = jnp.where(
        tp_id < near_ranges,
        source * (near_ranges * share) + tp_id * share + source_rank,
        near_rows
        + relayed_block(tp_place, relayer) * far_rows
        + source * half
        + source_rank % half,
    )
    arrive_ids = jnp.arange(near_rows + RELAYED * far_rows, dtype=jnp.int32)
    arrive_pick = (arrive_at.reshape(pack_rows, 1) == arrive_ids[None, :]).astype(BF16)
    pack_ids = jnp.arange(pack_rows, dtype=jnp.int32)
    full_at = source * (tp_count * share) + tp_id * share + source_rank
    place_pick = (full_at.reshape(pack_rows, 1) == pack_ids[None, :]).astype(BF16)
    return_at = lax.dynamic_slice(source * share + source_rank, (tp_place, 0), (1, rows))
    return_pick = (row_ids[:, None] == return_at).astype(BF16)

    x_all = jnp.concatenate((near_moved, far_own, *x_near, *relay_second(*x_near)), axis=0)
    x_low = jnp.dot(arrive_pick, x_all, preferred_element_type=F32).astype(BF16)
    dy_sent = picked(send_pick, cotangent).reshape(pack_rows, width)
    out_proj, ffn_down = together((out_proj, ffn_down, x_low))[:2]
    out_weight = lax.all_gather(out_proj.T, GROUP, axis=0, tiled=True)
    down_weight = lax.all_gather(ffn_down.T, GROUP, axis=0, tiled=True)
    pair_shard = jnp.concatenate(together((ffn_gate, ffn_up, x_moved))[:2], axis=1)

    tail_at = 2 * key_cols + 2 * value_cols
    gain_in_full = extras[:, :own].reshape(1, width)
    gain_mid_full = extras[:, own : 2 * own].reshape(1, width)

    def taps_of(start, weight):
        flat = extras[:, start : start + weight.size]
        flat = flat.reshape(groups, spans, heads, weight.shape[2])
        return jnp.transpose(flat, (1, 2, 0, 3)).reshape(spans, -1), start + weight.size

    query_taps, at = taps_of(2 * own, query_conv)
    key_taps, at = taps_of(at, key_conv)
    value_taps, at = taps_of(at, value_conv)
    taps = jnp.pad(
        jnp.concatenate([query_taps, key_taps, value_taps], axis=1), ((0, PAD - spans), (0, 0))
    )
    head_gain = jnp.broadcast_to(extras[:, at:].reshape(1, value_size), (PAD, value_size))
    par = jnp.zeros((PAD, LANES), F32)
    par = par.at[0, :heads].set(-jnp.exp(decay_log)).at[1, :heads].set(step_bias)
    length_row = lax.dynamic_slice(
        lengths, (my_micro, my_pack, 0), (1, 1, lengths.shape[2])
    ).reshape(-1)
    info, seg_rows = place_arrays(length_row, pack_rows)

    x_float = x_low.astype(F32)
    rate_in = lax.rsqrt(jnp.mean(x_float * x_float, axis=1, keepdims=True) + square_eps)
    normed_in = (x_float * rate_in * gain_in_full).astype(BF16)
    proj = dot_nn(normed_in, mixer_weight)
    dy_all = exchange(together((dy_sent, proj))[0])
    normed_low, *saved = delta_forward(proj, info, seg_rows, par, taps, head_gain, sizes)

    mixed_part = dot_nt(normed_low, out_weight).astype(BF16)
    *mixer_came, dy_all = together((*sum_first(mixed_part, rows), dy_all))
    from_after, from_before = sum_second(*sum_middle(mixed_part, rows, mixer_came))
    pair_weight = lax.all_gather(pair_shard, GROUP, axis=0, tiled=True)
    dy_low = jnp.dot(place_pick, dy_all, preferred_element_type=F32).astype(BF16)
    own_f32 = jax.ShapeDtypeStruct((rows, width), F32)
    own_low = jax.ShapeDtypeStruct((rows, width), BF16)
    gain_part = jax.ShapeDtypeStruct((PAD, width), F32)
    place = tp_place.reshape(1)
    gain_in_8 = jnp.broadcast_to(gain_in_full, (PAD, width))
    gain_mid_8 = jnp.broadcast_to(gain_mid_full, (PAD, width))
    hidden_in, mid_own = row_parts(
        middle_kernel,
        place,
        [
            ("all", mixed_part),
            ("own", from_after),
            ("own", from_before),
            ("all", x_low),
            ("one", gain_mid_8),
        ],
        [("own", own_f32), ("own", own_low)],
        rows,
    )
    mid_low = copy_rows_ordered(mid_own)
    grad_hidden = dot_nn(dy_low, down_weight)
    mid_low, grad_hidden = together((mid_low, grad_hidden))
    units = ffn_gate.shape[1]
    both = dot_nn(mid_low, pair_weight)
    gate_value, up_value = both[:, :units], both[:, units:]
    gate_sig = sigmoid(gate_value)
    gate_act = gate_value * gate_sig
    hidden_low = (gate_act * up_value).astype(BF16)
    pair_grad = jnp.concatenate(
        [
            (grad_hidden * up_value * (gate_sig * (1.0 + gate_value * (1.0 - gate_sig)))).astype(BF16),
            (grad_hidden * gate_act).astype(BF16),
        ],
        axis=1,
    )
    back_part = dot_nt(pair_grad, pair_weight).astype(BF16)
    back_part, pair_late, hidden_late, mid_late = together(
        (back_part, pair_grad, hidden_low, mid_low)
    )
    back_moved = deal(back_part, "b")
    ffn_part = dot_nt(hidden_late, down_weight).astype(BF16)
    grad_down_part = dot_tn(dy_low, hidden_late).astype(BF16)
    grad_pair_part = dot_tn(mid_late, pair_late).astype(BF16)
    back_moved, ffn_part, grad_down_part, grad_pair_part = together(
        (back_moved, ffn_part, grad_down_part, grad_pair_part)
    )

    def owners(value):
        return lax.psum_scatter(value, GROUP, scatter_dimension=0, tiled=True)

    hidden_grad, mix_own, grad_mid_gain = row_parts(
        middle_back_kernel,
        place,
        [("own", back_moved), ("own", hidden_in), ("all", dy_low), ("one", gain_mid_8)],
        [("own", own_f32), ("own", own_low), ("one", gain_part)],
        rows,
    )
    grad_mid_gain = jnp.sum(grad_mid_gain, axis=0)
    mix_low = copy_rows_ordered(mix_own)
    mix_low, ffn_part, grad_down = together((mix_low, ffn_part, owners(grad_down_part)))
    dnormed = dot_nn(mix_low, out_weight)
    grad_proj, conv_grad, head_gain_grad, decay_grads = delta_backward(
        proj, info, seg_rows, par, taps, head_gain, saved, dnormed, sizes
    )
    first_part = dot_nt(grad_proj, mixer_weight).astype(BF16)
    result_moved = deal(ffn_part, "y")
    grad_out_moved = exchange(dot_tn(mix_low, normed_low).astype(BF16))
    first_part, proj_late, result_moved, grad_pair_part, grad_out_moved = together(
        (first_part, grad_proj, result_moved, grad_pair_part, grad_out_moved)
    )
    grad_pair = owners(grad_pair_part)
    grad_mixer_part = dot_tn(normed_in, proj_late).astype(BF16)
    result = (hidden_in + add_dealt(result_moved, "y")).astype(BF16)
    result_back = exchange(to_sources(result)).reshape(rows, width)
    *first_came, grad_mixer_part, result_back = together(
        (*sum_first(first_part, rows), grad_mixer_part, result_back)
    )
    first_middle = sum_middle(first_part, rows, first_came)
    late_after, late_before = sum_second(*first_middle)
    result_back = together((result_back, *first_middle))[0]
    result_back = jnp.pad(result_back, ((0, PAD), (0, 0)))
    result_near = relay_first(result_back)

    token_grad, grad_in_gain = row_parts(
        first_back_kernel,
        place,
        [
            ("all", first_part),
            ("own", late_after),
            ("own", late_before),
            ("own", hidden_grad),
            ("all", x_low),
            ("one", gain_in_8),
        ],
        [("own", own_low), ("one", gain_part)],
        rows,
    )
    grad_in_gain = jnp.sum(grad_in_gain, axis=0)

    conv_sum = jnp.sum(conv_grad.reshape(spans, PAD, -1), axis=1)

    def taps_to(value, size):
        parted = value.reshape(spans, heads, groups, size // groups)
        return jnp.transpose(parted, (2, 0, 1, 3)).reshape(groups, -1)

    gain_sum = jnp.sum(head_gain_grad.reshape(PAD * heads, value_size), axis=0)
    decay_sums = jnp.sum(decay_grads.reshape(2, PAD, LANES), axis=1)[:, :heads].reshape(1, -1)
    parts = [
        grad_in_gain.reshape(groups, own),
        grad_mid_gain.reshape(groups, own),
        gain_sum.reshape(groups, -1),
        taps_to(conv_sum[:, :key_cols], key_size),
        taps_to(conv_sum[:, key_cols : 2 * key_cols], key_size),
        taps_to(conv_sum[:, 2 * key_cols :], value_size),
        jnp.broadcast_to(decay_sums, (groups, decay_sums.shape[1])),
    ]
    lens = [part.shape[1] for part in parts]
    packed = jnp.concatenate(parts, axis=1)
    packed = jnp.pad(packed, ((0, 0), (0, width - packed.shape[1])))
    extra = jnp.pad(pair_rows(packed), ((0, 0), (0, PAD - 2), (0, 0)))
    grad_sent = to_sources(token_grad)
    came = exchange(jnp.concatenate([grad_sent, extra], axis=1))
    before, after, grad_down, grad_out_moved = together(
        (*result_near, grad_down, grad_out_moved, grad_sent)
    )[:4]
    grad_out = summed_turned(grad_out_moved.reshape(groups, own, -1))
    result_far = relay_second(before, after)
    summed = jnp.sum(came[:, share : share + 2].astype(F32), axis=(0, 1))
    block = jnp.concatenate(
        [
            came[:, :share].reshape(rows, width),
            jnp.pad(pair_rows(summed), ((0, PAD - 2), (0, 0))),
        ],
        axis=0,
    )
    token_near = relay_first(block)
    result_far = together((*result_far, *token_near))[:3]
    mixed, unused = to_given((result_back, before, after, *result_far))
    grad_gate = grad_pair[:, :units].astype(F32)
    grad_up = grad_pair[:, units:].astype(F32)
    *token_blocks, grad_gate, grad_up = together(
        (block, *token_near, *relay_second(*token_near), grad_gate, grad_up)
    )
    grad_tokens, full = to_given(token_blocks)
    *mixer_grads, gates_turned = widened(
        owners(grad_mixer_part), [key_cols, key_cols, value_cols, value_cols]
    )
    mixer_grads += [gates_turned[:heads].T, gates_turned[heads : 2 * heads].T]
    grad_down = grad_down.astype(F32).T

    tp_summed = jnp.sum(
        full.reshape(RELAYED, held, width)[:, rows : rows + 2].astype(F32), axis=(0, 1)
    )
    pieces = []
    offset = 0
    for index, length in enumerate(lens):
        origin = tp_summed if index < 3 else summed
        pieces.append(origin[offset : offset + length])
        offset += length
    decay_pair = pieces[6].reshape(2, heads)
    return (
        mixed,
        grad_tokens,
        pieces[0],
        *mixer_grads,
        pieces[3].reshape(query_conv.shape),
        pieces[4].reshape(key_conv.shape),
        pieces[5].reshape(value_conv.shape),
        decay_pair[0],
        decay_pair[1],
        pieces[2],
        grad_out,
        pieces[1],
        grad_gate,
        grad_up,
        grad_down,
    )


def solution(mesh):
    in_specs = (
        P(None, ("fsdp", "ctx"), None),
        P(None, ("fsdp", "ctx"), None),
        P(),
        P(),
        P(("fsdp", "ctx")),
        P(("fsdp", "ctx"), "tp"),
        P(("fsdp", "ctx"), "tp"),
        P(("fsdp", "ctx"), "tp"),
        P(("fsdp", "ctx"), "tp"),
        P(("fsdp", "ctx"), "tp"),
        P(("fsdp", "ctx"), "tp"),
        P(None, "tp", ("fsdp", "ctx")),
        P(None, "tp", ("fsdp", "ctx")),
        P(None, "tp", ("fsdp", "ctx")),
        P("tp"),
        P("tp"),
        P(("fsdp", "ctx")),
        P("tp", ("fsdp", "ctx")),
        P(("fsdp", "ctx")),
        P(("fsdp", "ctx"), "tp"),
        P(("fsdp", "ctx"), "tp"),
        P("tp", ("fsdp", "ctx")),
    )
    out_specs = (
        P(None, ("fsdp", "ctx"), None),
        P(None, ("fsdp", "ctx"), None),
        P(("fsdp", "ctx")),
        P(("fsdp", "ctx"), "tp"),
        P(("fsdp", "ctx"), "tp"),
        P(("fsdp", "ctx"), "tp"),
        P(("fsdp", "ctx"), "tp"),
        P(("fsdp", "ctx"), "tp"),
        P(("fsdp", "ctx"), "tp"),
        P(None, "tp", ("fsdp", "ctx")),
        P(None, "tp", ("fsdp", "ctx")),
        P(None, "tp", ("fsdp", "ctx")),
        P("tp"),
        P("tp"),
        P(("fsdp", "ctx")),
        P("tp", ("fsdp", "ctx")),
        P(("fsdp", "ctx")),
        P(("fsdp", "ctx"), "tp"),
        P(("fsdp", "ctx"), "tp"),
        P("tp", ("fsdp", "ctx")),
    )
    return jax.shard_map(
        per_device, mesh=mesh, in_specs=in_specs, out_specs=out_specs, check_vma=False
    )
```
